32 devices in a mesh: pitch: 2 (over y), span: 4 (over z), axial: 4 (over x, core).
Axes of the slice: x: 2, y: 2, z: 4, core: 2. Of those that a mesh axis runs over, the one named last changes fastest.
Arguments:
- guess: float32 [2, 6, 16, 64, 512], P(None, None, 'pitch', 'span', 'axial'), may hold values from -6 to 6
- right_side: float32 [2, 6, 16, 64, 512], P(None, None, 'pitch', 'span', 'axial'), may hold values from -60 to 60
- diag_block: bfloat16 [6, 6, 16, 64, 512], P(None, None, 'pitch', 'span', 'axial'), may hold values from -4 to 4
- neighbour_blocks: bfloat16 [6, 6, 6, 16, 64, 512], P(None, None, None, 'pitch', 'span', 'axial'), may hold values from -0.6484375 to 0.6484375
- dissipation: float32 [3, 16, 64, 512], P(None, 'pitch', 'span', 'axial'), may hold values from 0.03 to 0.25
- omega_volume: float32 [16, 64, 512], P('pitch', 'span', 'axial'), may hold values from 0.2 to 2
- pseudo_step: float32 [16, 64, 512], P('pitch', 'span', 'axial'), may hold values from 0.03 to 0.3
- phase: float32 [1], replicated, may hold values from -3.140625 to 3.140625
Outputs:
- solution_field: float32 [2, 6, 16, 64, 512], P(None, None, 'pitch', 'span', 'axial')
- norms: float32 [2], replicated
The draws below stay inside these ranges and needn't reach their ends.
All inputs are finite; a program needn't handle non-finite values.
Results may differ from the reference program's by a relative error of at most 0.0003.
Values sent between devices are 32-bit elements; how exact they have to be, the bound alone decides.
No kernel may reach another device: no remote copies, remote signals or barrier semaphores. Data moves between devices by JAX's collectives and lax.ppermute only.
A program may use at most 128 MiB of HBM per device.

```python
import math
import jax
import jax.numpy as jnp

NV = 6
ITERS = 2
NP = 16
NS = 64
NA = 512


def wall_profile():
    rows = jnp.arange(NS, dtype=jnp.float32)
    distance = jnp.minimum(rows, float(NS - 1) - rows)
    return jnp.exp(-distance / 1.5)


def draw_right_side(key, part):
    key_base = jax.random.fold_in(key, 11)
    key_scale = jax.random.fold_in(key, 12)
    shape_all = (2, NV, NP, NS, NA)
    span_pos = jnp.arange(NS, dtype=jnp.float32) / max(NS - 1, 1)
    wall_factor = 1.0 + 2.5 * wall_profile()
    base = jnp.clip(jax.random.normal(key_base, shape_all, jnp.float32), -3.0, 3.0)
    ramp = 1.0 + 2.0 * span_pos
    scale = jnp.exp(jax.random.uniform(key_scale, shape_all, jnp.float32, 0.0, math.log(10.0))) / 6.0
    profile = ramp * wall_factor
    return (base * scale * profile[None, None, None, :, None]).astype(jnp.float32)


def draw_diag_block(key, part):
    key_off = jax.random.fold_in(key, 21)
    key_mag = jax.random.fold_in(key, 22)
    off_part = jnp.clip(0.35 * jax.random.normal(key_off, (NV, NV, NP, NS, NA), jnp.float32), -0.45, 0.45)
    magnitude = jax.random.uniform(key_mag, (NV, NP, NS, NA), jnp.float32, 2.5, 4.0)
    identity = jnp.eye(NV, dtype=jnp.float32)[:, :, None, None, None]
    return (off_part * (1.0 - identity) + identity * magnitude[:, None]).astype(jnp.bfloat16)


def draw_pseudo_step(key, part):
    key_step = jax.random.fold_in(key, 31)
    base = jnp.exp(jax.random.uniform(key_step, (NP, NS, NA), jnp.float32, math.log(0.1), math.log(0.3)))
    shrink = 1.0 + 2.0 * wall_profile()
    return (base / shrink[None, :, None]).astype(jnp.float32)


def block_levels(key, dims, split, smallest, largest):
    loudness, own = 1.0, jax.random.fold_in(key, 6)
    for axis_at, shards_of in split:
        heights = jnp.exp(jax.random.uniform(jax.random.fold_in(own, axis_at), (shards_of,), jnp.float32, smallest / len(split), largest / len(split)))
        loudness = loudness * jnp.repeat(heights, dims[axis_at] // shards_of).reshape([-1 if axis == axis_at else 1 for axis in range(len(dims))])
    return loudness


def scatter_about(rng, extent, spread, limit, shards=(), kind=jnp.bfloat16):
    values = jax.random.normal(rng, extent, jnp.float32) * spread
    if len(shards) > 0:
        values = block_levels(rng, extent, shards, -0.22, 0.18) * values
    return jnp.clip(values, min=-limit, max=limit).astype(kind)


def setup_inputs(seed: int = 0) -> dict:
    key_of = jax.random.split(jax.random.key(seed), 9)
    return {
        "guess": scatter_about(key_of[0], (2, NV, NP, NS, NA), 1.0, 6.0, ((2, 2), (3, 4), (4, 4)), jnp.float32),
        "right_side": draw_right_side(jax.random.fold_in(key_of[8], 71), 0),
        "diag_block": draw_diag_block(jax.random.fold_in(key_of[8], 71), 0),
        "neighbour_blocks": scatter_about(key_of[3], (6, NV, NV, NP, NS, NA), 0.26, 0.6484375, ((3, 2), (4, 4), (5, 4))),
        "dissipation": jnp.clip(jnp.exp(math.log(0.25) - 2.1202636 * jax.random.uniform(key_of[4], (3, NP, NS, NA), jnp.float32) ** block_levels(key_of[4], (3, NP, NS, NA), ((1, 2), (2, 4), (3, 4)), -0.2, 0.2)), 0.03, 0.25),
        "omega_volume": jnp.clip(jnp.exp(math.log(2.0) - 2.3025851 * jax.random.uniform(key_of[5], (NP, NS, NA), jnp.float32) ** block_levels(key_of[5], (NP, NS, NA), ((0, 2), (1, 4), (2, 4)), -0.2, 0.2)), 0.2, 2.0),
        "pseudo_step": draw_pseudo_step(jax.random.fold_in(key_of[8], 71), 0),
        "phase": jnp.clip(jax.random.uniform(key_of[7], (1,), jnp.float32, -3.140625, 3.140625), -3.140625, 3.140625),
    }


def block_apply(blocks, vector_in):
    summed = None
    for column in range(blocks.shape[1]):
        product = blocks[:, column].astype(jnp.float32)[None] * vector_in[:, column][:, None]
        summed = product if summed is None else summed + product
    return summed

def rotate(values, cosine, sine_part):
    real_part = values[0]
    imag_part = values[1]
    return jnp.stack([cosine * real_part - sine_part * imag_part, sine_part * real_part + cosine * imag_part])

def operate(current, pitch_ext, span_ext, axial_ext, diag_block, neighbour_blocks, dissipation, omega_volume):
    summed = block_apply(diag_block, current)
    summed = summed + block_apply(neighbour_blocks[0], pitch_ext[:, :, 1:-3]) + block_apply(neighbour_blocks[1], pitch_ext[:, :, 3:-1])
    summed = summed + block_apply(neighbour_blocks[2], span_ext[:, :, :, 1:-3]) + block_apply(neighbour_blocks[3], span_ext[:, :, :, 3:-1])
    summed = summed + block_apply(neighbour_blocks[4], axial_ext[:, :, :, :, 1:-3]) + block_apply(neighbour_blocks[5], axial_ext[:, :, :, :, 3:-1])
    summed = summed + dissipation[0] * (pitch_ext[:, :, :-4] + pitch_ext[:, :, 4:])
    summed = summed + dissipation[1] * (span_ext[:, :, :, :-4] + span_ext[:, :, :, 4:])
    summed = summed + dissipation[2] * (axial_ext[:, :, :, :, :-4] + axial_ext[:, :, :, :, 4:])
    rotation_term = jnp.stack([-omega_volume * current[1], omega_volume * current[0]])
    return summed + rotation_term

def reference(guess, right_side, diag_block, neighbour_blocks, dissipation, omega_volume, pseudo_step, phase):
    cosine = jnp.cos(phase[0])
    sine_part = jnp.sin(phase[0])
    current = guess
    square_sums = []
    for iteration in range(ITERS):
        pitch_ext = jnp.concatenate([rotate(current[:, :, -2:], cosine, -sine_part), current, rotate(current[:, :, :2], cosine, sine_part)], axis=2)
        span_ext = jnp.pad(current, ((0, 0), (0, 0), (0, 0), (2, 2), (0, 0)))
        axial_ext = jnp.pad(current, ((0, 0), (0, 0), (0, 0), (0, 0), (2, 2)))
        residual = right_side - operate(current, pitch_ext, span_ext, axial_ext, diag_block, neighbour_blocks, dissipation, omega_volume)
        square_sums.append(jnp.sum(residual * residual))
        current = current + pseudo_step[None, None] * residual
    cell_count = float(guess.size)
    norms = jnp.sqrt(jnp.stack(square_sums) / cell_count)
    return (current, norms)
```

```python
import functools

import jax
import jax.numpy as jnp
from jax import lax
from jax.experimental import pallas as pl
from jax.experimental.pallas import tpu as pltpu
from jax.sharding import PartitionSpec as P

ITERS = 2
WIDTH = 2
VMEM = pl.BlockSpec(memory_space=pltpu.VMEM)
SMEM = pl.BlockSpec(memory_space=pltpu.SMEM)
ANY = pl.BlockSpec(memory_space=pl.ANY)
VMEM_LIMIT = 40 * 1024 * 1024
PAD = 8


def resident(values):
    return pltpu.with_memory_space_constraint(values, pltpu.VMEM)


def kept(shape):
    return pltpu.VMEM(shape, jnp.float32)


def params():
    return pltpu.CompilerParams(vmem_limit_bytes=VMEM_LIMIT)


def lane_place(k, planes, lanes):
    per_group = (lanes // (2 * WIDTH)) // planes
    return k // per_group, (k % per_group) * planes


def lane_groups(rows, planes, lanes):
    return lane_place(rows - 1, planes, lanes)[0] + 1


def pitch_faces_kernel(guess_ref, faces_ref, sems):
    planes = guess_ref.shape[1]
    tail = pltpu.make_async_copy(
        guess_ref.at[:, planes - WIDTH : planes], faces_ref.at[0], sems.at[0]
    )
    head = pltpu.make_async_copy(guess_ref.at[:, 0:WIDTH], faces_ref.at[1], sems.at[1])
    tail.start()
    head.start()
    tail.wait()
    head.wait()


def pack_faces(wide_ref, low_ref, high_ref, axial_ref):
    rows, wide, span, lanes = wide_ref.shape
    planes = wide - 2 * WIDTH
    lane = lax.broadcasted_iota(jnp.int32, (span, lanes), 1)
    groups = lane_groups(rows, planes, lanes)
    packed = [None] * groups
    for k in range(rows):
        group, base = lane_place(k, planes, lanes)
        for p in range(planes):
            cells = wide_ref[k, p + WIDTH]
            low_ref[k, p] = cells[:WIDTH]
            high_ref[k, p] = cells[span - WIDTH :]
            place = base + p
            moved = pltpu.roll(cells, (2 * WIDTH * place + WIDTH) % lanes, axis=1)
            if packed[group] is None:
                packed[group] = moved
            else:
                packed[group] = jnp.where(lane >= 2 * WIDTH * place, moved, packed[group])
        if k == rows - 1 or lane_place(k + 1, planes, lanes)[0] != group:
            axial_ref[group] = packed[group]


def first_pack_kernel(guess_ref, wide_ref, low_ref, high_ref, axial_ref, sem):
    rows, wide, span, lanes = wide_ref.shape
    planes = wide - 2 * WIDTH
    copy = pltpu.make_async_copy(guess_ref, wide_ref.at[:, WIDTH : WIDTH + planes], sem)
    copy.start()
    for k in range(rows):
        for p in (0, 1, wide - 2, wide - 1):
            wide_ref[k, p] = jnp.zeros((span, lanes), jnp.float32)
    copy.wait()
    pack_faces(wide_ref, low_ref, high_ref, axial_ref)


def pack_kernel(wide_ref, low_ref, high_ref, axial_ref):
    pack_faces(wide_ref, low_ref, high_ref, axial_ref)


def main_kernel(
    wide_ref,
    low_ref,
    high_ref,
    axial_low_ref,
    axial_high_ref,
    neighbour_ref,
    diag_ref,
    right_ref,
    dissipation_ref,
    omega_ref,
    step_ref,
    next_ref,
    error_ref,
    square_ref,
    span_buf,
    axial_buf,
):
    rows, wide, span, lanes = wide_ref.shape
    planes = wide - 2 * WIDTH
    nv = rows // 2
    lane = lax.broadcasted_iota(jnp.int32, (span, lanes), 1)
    for group in range(axial_buf.shape[0]):
        axial_buf[group] = jnp.where(
            lane % (2 * WIDTH) < WIDTH, axial_low_ref[group], axial_high_ref[group]
        )
    for k in range(rows):
        for p in (0, 1, wide - 2, wide - 1):
            next_ref[k, p] = jnp.zeros((span, lanes), jnp.float32)
    square_ref[...] = jnp.zeros_like(square_ref)

    def plane(p, carry):
        for k in range(rows):
            span_buf[k, PAD - WIDTH : PAD] = low_ref[k, p]
            span_buf[k, PAD : PAD + span] = wide_ref[k, p + WIDTH]
            span_buf[k, PAD + span : PAD + span + WIDTH] = high_ref[k, p]
        total = [None] * rows

        def add(k, value):
            total[k] = value if total[k] is None else total[k] + value

        def column(blocks, j, real, imag):
            for i in range(nv):
                block = blocks(i, j).astype(jnp.float32)
                add(i, block * real)
                add(nv + i, block * imag)

        spread_pitch = dissipation_ref[0, p]
        spread_span = dissipation_ref[1, p]
        spread_axial = dissipation_ref[2, p]
        for j in range(nv):
            pair = (j, nv + j)
            column(lambda i, j: diag_ref[i, j, p], j, *[wide_ref[k, p + 2] for k in pair])
            column(lambda i, j: neighbour_ref[0, i, j, p], j, *[wide_ref[k, p + 1] for k in pair])
            column(lambda i, j: neighbour_ref[1, i, j, p], j, *[wide_ref[k, p + 3] for k in pair])
            column(
                lambda i, j: neighbour_ref[2, i, j, p],
                j,
                *[span_buf[k, PAD - 1 : PAD - 1 + span] for k in pair],
            )
            column(
                lambda i, j: neighbour_ref[3, i, j, p],
                j,
                *[span_buf[k, PAD + 1 : PAD + 1 + span] for k in pair],
            )
            lower = []
            upper = []
            for k in pair:
                cells = wide_ref[k, p + WIDTH]
                group, base = lane_place(k, planes, lanes)
                shift = lanes - WIDTH - 2 * WIDTH * base - 2 * WIDTH * p
                shift = jnp.where(shift < 0, shift + lanes, shift)
                halo = pltpu.roll(axial_buf[group], shift, axis=1)
                low_near = jnp.where(lane >= lanes - 1, halo, cells)
                high_near = jnp.where(lane < 1, halo, cells)
                low_far = jnp.where(lane >= lanes - WIDTH, halo, cells)
                high_far = jnp.where(lane < WIDTH, halo, cells)
                lower.append(pltpu.roll(low_near, 1, axis=1))
                upper.append(pltpu.roll(high_near, lanes - 1, axis=1))
                far = pltpu.roll(low_far, 2, axis=1) + pltpu.roll(high_far, lanes - 2, axis=1)
                add(k, spread_axial * far)
                add(
                    k,
                    spread_span
                    * (
                        span_buf[k, PAD - 2 : PAD - 2 + span]
                        + span_buf[k, PAD + 2 : PAD + 2 + span]
                    ),
                )
                add(k, spread_pitch * (wide_ref[k, p] + wide_ref[k, p + 4]))
            column(lambda i, j: neighbour_ref[4, i, j, p], j, *lower)
            column(lambda i, j: neighbour_ref[5, i, j, p], j, *upper)
        omega = omega_ref[p]
        step = step_ref[p]
        square = None
        for i in range(nv):
            real = wide_ref[i, p + WIDTH]
            imag = wide_ref[nv + i, p + WIDTH]
            for k, cells, turned in ((i, real, -omega * imag), (nv + i, imag, omega * real)):
                error = (total[k] + turned) - right_ref[k, p]
                error_ref[k, p] = error
                next_ref[k, p + WIDTH] = cells - step * error
                square = error * error if square is None else square + error * error
        inner = jnp.logical_and(p >= WIDTH, p < planes - WIDTH)
        square_ref[...] += jnp.where(inner, square, 0.0)
        return carry

    lax.fori_loop(0, planes, plane, 0)


def pitch_terms(halo_ref, turn_ref, neighbour_ref, dissipation_ref, error_ref, store):
    rows, planes, span, lanes = error_ref.shape
    nv = rows // 2
    for side in range(2):
        cosine = turn_ref[2 * side]
        sine_part = turn_ref[2 * side + 1]
        near_at, far_at = (1, 0) if side == 0 else (0, 1)
        edge, inside = (0, 1) if side == 0 else (planes - 1, planes - 2)

        def turned(j, at):
            real = halo_ref[side, j, at]
            imag = halo_ref[side, nv + j, at]
            return (cosine * real - sine_part * imag, sine_part * real + cosine * imag)

        total = [error_ref[k, edge] for k in range(rows)]
        spread_edge = dissipation_ref[0, edge]
        spread_inside = dissipation_ref[0, inside]
        for j in range(nv):
            near = turned(j, near_at)
            far = turned(j, far_at)
            for c in range(2):
                k = c * nv + j
                total[k] = total[k] + spread_edge * far[c]
                store(k, inside, error_ref[k, inside] + spread_inside * near[c])
            for i in range(nv):
                block = neighbour_ref[side, i, j, edge].astype(jnp.float32)
                for c in range(2):
                    total[c * nv + i] = total[c * nv + i] + block * near[c]
        for k in range(rows):
            store(k, edge, total[k])


def turn_kernel(
    halo_ref,
    turn_ref,
    neighbour_ref,
    dissipation_ref,
    step_ref,
    wide_ref,
    error_ref,
    square_in_ref,
    next_in_ref,
    next_ref,
    faces_ref,
    square_ref,
):
    planes = error_ref.shape[1]
    square_ref[...] = square_in_ref[...]

    def store(k, p, error):
        value = wide_ref[k, p + WIDTH] - step_ref[p] * error
        next_ref[k, p + WIDTH] = value
        if p < WIDTH:
            faces_ref[1, k, p] = value
        else:
            faces_ref[0, k, p - (planes - WIDTH)] = value
        square_ref[...] += error * error

    pitch_terms(halo_ref, turn_ref, neighbour_ref, dissipation_ref, error_ref, store)


def last_kernel(
    halo_ref,
    turn_ref,
    neighbour_ref,
    dissipation_ref,
    step_ref,
    wide_ref,
    error_ref,
    next_ref,
    first_square_ref,
    square_in_ref,
    out_ref,
    share_ref,
    edge_buf,
    square_buf,
    sems,
):
    planes = error_ref.shape[1]
    span, lanes = square_buf.shape
    inner = pltpu.make_async_copy(
        next_ref.at[:, 2 * WIDTH : planes], out_ref.at[:, WIDTH : planes - WIDTH], sems.at[0]
    )
    inner.start()
    square_buf[...] = square_in_ref[...]

    def store(k, p, error):
        at = p if p < WIDTH else p - (planes - 2 * WIDTH)
        edge_buf[k, at] = wide_ref[k, p + WIDTH] - step_ref[p] * error
        square_buf[...] += error * error

    pitch_terms(halo_ref, turn_ref, neighbour_ref, dissipation_ref, error_ref, store)
    low = pltpu.make_async_copy(
        edge_buf.at[:, 0:WIDTH], out_ref.at[:, 0:WIDTH], sems.at[1]
    )
    high = pltpu.make_async_copy(
        edge_buf.at[:, WIDTH : 2 * WIDTH], out_ref.at[:, planes - WIDTH : planes], sems.at[2]
    )
    low.start()
    high.start()
    first = jnp.sum(first_square_ref[...], axis=(0, 1), keepdims=True)
    second = jnp.sum(square_buf[...], axis=(0, 1), keepdims=True)
    lane = lax.broadcasted_iota(jnp.int32, share_ref.shape, 2)
    share_ref[...] = jnp.where(
        lane == 0, first.reshape(1, 1, 1), jnp.where(lane == 1, second.reshape(1, 1, 1), 0.0)
    )
    inner.wait()
    low.wait()
    high.wait()


def body(
    guess, right_side, diag_block, neighbour_blocks, dissipation, omega_volume, pseudo_step, phase
):
    parts, nv, planes, span, lanes = guess.shape
    rows = parts * nv
    pitch_count = lax.axis_size("pitch")
    span_count = lax.axis_size("span")
    axial_count = lax.axis_size("axial")
    devices = pitch_count * span_count * axial_count
    wide = (rows, planes + 2 * WIDTH, span, lanes)
    block = (rows, planes, span, lanes)
    faces_shape = (2, rows, WIDTH, span, lanes)
    edge_shape = (rows, planes, WIDTH, lanes)
    axial_shape = (lane_groups(rows, planes, lanes), span, lanes)
    guess = guess.reshape(block)
    right_side = right_side.reshape(block)

    cosine = jnp.cos(phase[0])
    sine_part = jnp.sin(phase[0])
    first_pitch = lax.axis_index("pitch") == 0
    last_pitch = lax.axis_index("pitch") == pitch_count - 1
    one = jnp.float32(1.0)
    zero = jnp.float32(0.0)
    turn = jnp.stack(
        [
            jnp.where(first_pitch, cosine, one),
            jnp.where(first_pitch, -sine_part, zero),
            jnp.where(last_pitch, cosine, one),
            jnp.where(last_pitch, sine_part, zero),
        ]
    )

    def exchange_pitch(faces):
        up = [(i, (i + 1) % pitch_count) for i in range(pitch_count)]
        down = [(j, i) for i, j in up]
        if sorted(up) == sorted(down):
            return lax.ppermute(faces, "pitch", up)
        return jnp.stack(
            [lax.ppermute(faces[0], "pitch", up), lax.ppermute(faces[1], "pitch", down)]
        )

    def exchange_rest(low, high, axial):
        up_span = [(i, i + 1) for i in range(span_count - 1)]
        down_span = [(i + 1, i) for i in range(span_count - 1)]
        up_axial = [(i, i + 1) for i in range(axial_count - 1)]
        down_axial = [(i + 1, i) for i in range(axial_count - 1)]
        return (
            lax.ppermute(high, "span", up_span),
            lax.ppermute(low, "span", down_span),
            lax.ppermute(axial, "axial", up_axial),
            lax.ppermute(axial, "axial", down_axial),
        )

    faces = pl.pallas_call(
        pitch_faces_kernel,
        out_shape=kept(faces_shape),
        in_specs=[ANY],
        out_specs=VMEM,
        scratch_shapes=[pltpu.SemaphoreType.DMA((2,))],
        compiler_params=params(),
        name="pitch_faces",
    )(guess)
    state, low, high, axial = pl.pallas_call(
        first_pack_kernel,
        out_shape=(kept(wide), kept(edge_shape), kept(edge_shape), kept(axial_shape)),
        in_specs=[ANY],
        out_specs=(VMEM,) * 4,
        scratch_shapes=[pltpu.SemaphoreType.DMA],
        compiler_params=params(),
        name="first_pack",
    )(guess)

    neighbour_blocks = resident(neighbour_blocks)
    diag_block = resident(diag_block)
    right_side = resident(right_side)
    dissipation = resident(dissipation)
    omega_volume = resident(omega_volume)
    pseudo_step = resident(pseudo_step)
    squares = []
    for iteration in range(ITERS):
        halo = resident(exchange_pitch(faces))
        around = [resident(part) for part in exchange_rest(low, high, axial)]
        following, error, square = pl.pallas_call(
            main_kernel,
            out_shape=(kept(wide), kept(block), kept((span, lanes))),
            in_specs=[VMEM] * 11,
            out_specs=(VMEM,) * 3,
            scratch_shapes=[
                pltpu.VMEM((rows, span + 2 * PAD, lanes), jnp.float32),
                pltpu.VMEM(axial_shape, jnp.float32),
            ],
            compiler_params=params(),
            name="main",
        )(
            state,
            *around,
            neighbour_blocks,
            diag_block,
            right_side,
            dissipation,
            omega_volume,
            pseudo_step,
        )
        if iteration < ITERS - 1:
            state, faces, square = pl.pallas_call(
                turn_kernel,
                out_shape=(kept(wide), kept(faces_shape), kept((span, lanes))),
                in_specs=[VMEM, SMEM] + [VMEM] * 7,
                out_specs=(VMEM,) * 3,
                input_output_aliases={8: 0},
                compiler_params=params(),
                name="pitch_terms",
            )(
                halo,
                turn,
                neighbour_blocks,
                dissipation,
                pseudo_step,
                state,
                error,
                square,
                following,
            )
            squares.append(square)
            low, high, axial = pl.pallas_call(
                pack_kernel,
                out_shape=(kept(edge_shape), kept(edge_shape), kept(axial_shape)),
                in_specs=[VMEM],
                out_specs=(VMEM,) * 3,
                compiler_params=params(),
                name="pack",
            )(state)
        else:
            out, share = pl.pallas_call(
                last_kernel,
                out_shape=(
                    jax.ShapeDtypeStruct(block, jnp.float32),
                    kept((devices, 1, lanes)),
                ),
                in_specs=[VMEM, SMEM] + [VMEM] * 8,
                out_specs=(ANY, VMEM),
                scratch_shapes=[
                    pltpu.VMEM((rows, 2 * WIDTH, span, lanes), jnp.float32),
                    pltpu.VMEM((span, lanes), jnp.float32),
                    pltpu.SemaphoreType.DMA((3,)),
                ],
                compiler_params=params(),
                name="last_pitch_terms",
            )(
                halo,
                turn,
                neighbour_blocks,
                dissipation,
                pseudo_step,
                state,
                error,
                following,
                squares[0],
                square,
            )
    shares = lax.all_to_all(share, ("pitch", "span", "axial"), 0, 0, tiled=True)
    totals = jnp.sum(shares, axis=(0, 1))[:ITERS]
    cell_count = float(rows * planes * span * lanes * devices)
    norms = jnp.sqrt(totals / cell_count)
    return (out.reshape(parts, nv, planes, span, lanes), norms)


def solution(mesh):
    placed = (
        P(None, None, "pitch", "span", "axial"),
        P(None, None, "pitch", "span", "axial"),
        P(None, None, "pitch", "span", "axial"),
        P(None, None, None, "pitch", "span", "axial"),
        P(None, "pitch", "span", "axial"),
        P("pitch", "span", "axial"),
        P("pitch", "span", "axial"),
        P(),
    )
    return jax.shard_map(
        body,
        mesh=mesh,
        in_specs=placed,
        out_specs=(P(None, None, "pitch", "span", "axial"), P()),
        check_vma=False,
    )
```

```python
import functools

import jax
import jax.numpy as jnp
from jax import lax
from jax.experimental import pallas as pl
from jax.experimental.pallas import tpu as pltpu
from jax.sharding import PartitionSpec as P

ITERS = 2
WIDTH = 2
VMEM = pl.BlockSpec(memory_space=pltpu.VMEM)
SMEM = pl.BlockSpec(memory_space=pltpu.SMEM)
ANY = pl.BlockSpec(memory_space=pl.ANY)
VMEM_LIMIT = 4 * 1024 * 1024
PAD = 8
GROUPS = 4


def resident(values):
    return pltpu.with_memory_space_constraint(values, pltpu.VMEM)


def kept(shape):
    return pltpu.VMEM(shape, jnp.float32)


def params():
    return pltpu.CompilerParams(vmem_limit_bytes=VMEM_LIMIT)


def lane_place(k, planes, lanes):
    per_group = (lanes // (2 * WIDTH)) // planes
    return k // per_group, (k % per_group) * planes


def lane_groups(rows, planes, lanes):
    return lane_place(rows - 1, planes, lanes)[0] + 1


def pitch_faces_kernel(guess_ref, faces_ref, sems):
    planes = guess_ref.shape[1]
    tail = pltpu.make_async_copy(
        guess_ref.at[:, planes - WIDTH : planes], faces_ref.at[0], sems.at[0]
    )
    head = pltpu.make_async_copy(guess_ref.at[:, 0:WIDTH], faces_ref.at[1], sems.at[1])
    tail.start()
    head.start()
    tail.wait()
    head.wait()


def pack_faces(wide_ref, even_ref, odd_ref, axial_ref):
    rows, wide, span, lanes = wide_ref.shape
    span_even = lax.axis_index("span") % 2 == 0
    planes = wide - 2 * WIDTH
    lane = lax.broadcasted_iota(jnp.int32, (span, lanes), 1)
    groups = lane_groups(rows, planes, lanes)
    packed = [None] * groups
    for k in range(rows):
        group, base = lane_place(k, planes, lanes)
        for p in range(planes):
            cells = wide_ref[k, p + WIDTH]
            low = cells[:WIDTH]
            high = cells[span - WIDTH :]
            even_ref[k, p] = jnp.where(span_even, high, low)
            odd_ref[k, p] = jnp.where(span_even, low, high)
            place = base + p
            moved = pltpu.roll(cells, (2 * WIDTH * place + WIDTH) % lanes, axis=1)
            if packed[group] is None:
                packed[group] = moved
            else:
                packed[group] = jnp.where(lane >= 2 * WIDTH * place, moved, packed[group])
        if k == rows - 1 or lane_place(k + 1, planes, lanes)[0] != group:
            axial_ref[group] = packed[group]


def first_pack_kernel(guess_ref, wide_ref, even_ref, odd_ref, axial_ref, sem):
    rows, wide, span, lanes = wide_ref.shape
    planes = wide - 2 * WIDTH
    copy = pltpu.make_async_copy(guess_ref, wide_ref.at[:, WIDTH : WIDTH + planes], sem)
    copy.start()
    for k in range(rows):
        for p in (0, 1, wide - 2, wide - 1):
            wide_ref[k, p] = jnp.zeros((span, lanes), jnp.float32)
    copy.wait()
    pack_faces(wide_ref, even_ref, odd_ref, axial_ref)


def pack_kernel(wide_ref, even_ref, odd_ref, axial_ref):
    pack_faces(wide_ref, even_ref, odd_ref, axial_ref)


class Loads:
    def __init__(self, pairs, sems, planes):
        self.pairs = pairs
        self.sems = sems
        self.size = planes // sems.shape[1]

    def copies(self, group):
        return [
            pltpu.make_async_copy(
                source.at[(slice(None),) * dim + (pl.ds(group * self.size, self.size),)],
                target.at[(slice(None),) * dim + (pl.ds(group * self.size, self.size),)],
                self.sems.at[at, group],
            )
            for at, (source, target, dim) in enumerate(self.pairs)
        ]

    def start(self):
        for group in range(self.sems.shape[1]):
            for copy in self.copies(group):
                copy.start()

    def ready(self, p):
        @pl.when(p % self.size == 0)
        def _():
            for copy in self.copies(p // self.size):
                copy.wait()


def near_loading_kernel(
    wide_ref,
    neighbour_hbm,
    diag_hbm,
    right_hbm,
    dissipation_hbm,
    omega_hbm,
    error_ref,
    neighbour_ref,
    diag_ref,
    right_ref,
    dissipation_ref,
    omega_ref,
    sems,
):
    loads = Loads(
        [
            (right_hbm, right_ref, 1),
            (dissipation_hbm, dissipation_ref, 1),
            (omega_hbm, omega_ref, 0),
            (diag_hbm, diag_ref, 2),
            (neighbour_hbm.at[0:2], neighbour_ref, 3),
        ],
        sems,
        error_ref.shape[1],
    )
    near_sweep(
        wide_ref,
        neighbour_ref,
        diag_ref,
        right_ref,
        dissipation_ref,
        omega_ref,
        error_ref,
        loads,
    )


def near_kernel(*refs):
    near_sweep(*refs, None)


def near_sweep(
    wide_ref, neighbour_ref, diag_ref, right_ref, dissipation_ref, omega_ref, error_ref, loads
):
    rows, planes, span, lanes = error_ref.shape
    nv = rows // 2
    if loads is not None:
        loads.start()

    def plane(p, carry):
        if loads is not None:
            loads.ready(p)
        omega = omega_ref[p]
        spread = dissipation_ref[0, p]
        total = []
        for k in range(rows):
            other = wide_ref[(k + nv) % rows, p + WIDTH]
            turned = -omega * other if k < nv else omega * other
            far = wide_ref[k, p] + wide_ref[k, p + 2 * WIDTH]
            total.append((turned - right_ref[k, p]) + spread * far)
        for j in range(nv):
            for at, blocks in (
                (2, lambda i: diag_ref[i, j, p]),
                (1, lambda i: neighbour_ref[0, i, j, p]),
                (3, lambda i: neighbour_ref[1, i, j, p]),
            ):
                real = wide_ref[j, p + at]
                imag = wide_ref[nv + j, p + at]
                for i in range(nv):
                    block = blocks(i).astype(jnp.float32)
                    total[i] = total[i] + block * real
                    total[nv + i] = total[nv + i] + block * imag
        for k in range(rows):
            error_ref[k, p] = total[k]
        return carry

    lax.fori_loop(0, planes, plane, 0)


def far_loading_kernel(
    wide_ref,
    span_even_ref,
    span_odd_ref,
    axial_even_ref,
    axial_odd_ref,
    neighbour_hbm,
    dissipation_ref,
    step_hbm,
    error_in_ref,
    error_ref,
    next_ref,
    square_ref,
    neighbour_ref,
    step_ref,
    span_buf,
    axial_buf,
    sems,
):
    loads = Loads(
        [(step_hbm, step_ref, 0), (neighbour_hbm.at[2:6], neighbour_ref, 3)],
        sems,
        step_ref.shape[0],
    )
    far_sweep(
        wide_ref,
        span_even_ref,
        span_odd_ref,
        axial_even_ref,
        axial_odd_ref,
        neighbour_ref,
        dissipation_ref,
        step_ref,
        error_in_ref,
        error_ref,
        next_ref,
        square_ref,
        span_buf,
        axial_buf,
        loads,
    )


def far_kernel(*refs):
    far_sweep(*refs, None)


def far_sweep(
    wide_ref,
    span_even_ref,
    span_odd_ref,
    axial_even_ref,
    axial_odd_ref,
    neighbour_ref,
    dissipation_ref,
    step_ref,
    error_in_ref,
    error_ref,
    next_ref,
    square_ref,
    span_buf,
    axial_buf,
    loads,
):
    rows, wide, span, lanes = wide_ref.shape
    planes = wide - 2 * WIDTH
    nv = rows // 2
    if loads is not None:
        loads.start()
    span_even = lax.axis_index("span") % 2 == 0
    axial_even = lax.axis_index("axial") % 2 == 0
    lane = lax.broadcasted_iota(jnp.int32, (span, lanes), 1)
    from_even = (lane % (2 * WIDTH) >= WIDTH) == axial_even
    for group in range(axial_buf.shape[0]):
        axial_buf[group] = jnp.where(from_even, axial_even_ref[group], axial_odd_ref[group])
    for k in range(rows):
        for p in (0, 1, wide - 2, wide - 1):
            next_ref[k, p] = jnp.zeros((span, lanes), jnp.float32)
    square_ref[...] = jnp.zeros_like(square_ref)

    def plane(p, carry):
        if loads is not None:
            loads.ready(p)
        for k in range(rows):
            at_even = span_even_ref[k, p]
            at_odd = span_odd_ref[k, p]
            span_buf[k, PAD - WIDTH : PAD] = jnp.where(span_even, at_odd, at_even)
            span_buf[k, PAD : PAD + span] = wide_ref[k, p + WIDTH]
            span_buf[k, PAD + span : PAD + span + WIDTH] = jnp.where(span_even, at_even, at_odd)
        total = [error_in_ref[k, p] for k in range(rows)]
        spread_span = dissipation_ref[1, p]
        spread_axial = dissipation_ref[2, p]

        def column(direction, j, real, imag):
            for i in range(nv):
                block = neighbour_ref[direction, i, j, p].astype(jnp.float32)
                total[i] = total[i] + block * real
                total[nv + i] = total[nv + i] + block * imag

        for j in range(nv):
            pair = (j, nv + j)
            column(0, j, *[span_buf[k, PAD - 1 : PAD - 1 + span] for k in pair])
            column(1, j, *[span_buf[k, PAD + 1 : PAD + 1 + span] for k in pair])
            lower = []
            upper = []
            for k in pair:
                cells = wide_ref[k, p + WIDTH]
                group, base = lane_place(k, planes, lanes)
                shift = lanes - WIDTH - 2 * WIDTH * base - 2 * WIDTH * p
                halo = pltpu.roll(axial_buf[group], shift, axis=1)
                low_near = jnp.where(lane >= lanes - 1, halo, cells)
                high_near = jnp.where(lane < 1, halo, cells)
                low_far = jnp.where(lane >= lanes - WIDTH, halo, cells)
                high_far = jnp.where(lane < WIDTH, halo, cells)
                lower.append(pltpu.roll(low_near, 1, axis=1))
                upper.append(pltpu.roll(high_near, lanes - 1, axis=1))
                far = pltpu.roll(low_far, 2, axis=1) + pltpu.roll(high_far, lanes - 2, axis=1)
                total[k] = total[k] + spread_axial * far
                far = (
                    span_buf[k, PAD - 2 : PAD - 2 + span] + span_buf[k, PAD + 2 : PAD + 2 + span]
                )
                total[k] = total[k] + spread_span * far
            column(2, j, *lower)
            column(3, j, *upper)
        step = step_ref[p]
        square = None
        for k in range(rows):
            error = total[k]
            error_ref[k, p] = error
            next_ref[k, p + WIDTH] = wide_ref[k, p + WIDTH] - step * error
            square = error * error if square is None else square + error * error
        inner = jnp.logical_and(p >= WIDTH, p < planes - WIDTH)
        square_ref[...] += jnp.where(inner, square, 0.0)
        return carry

    lax.fori_loop(0, planes, plane, 0)


def pitch_terms(halo_ref, phase_ref, neighbour_ref, dissipation_ref, error_ref, store):
    rows, planes, span, lanes = error_ref.shape
    nv = rows // 2
    pitch_at = lax.axis_index("pitch")
    angle = jnp.full((span, lanes), phase_ref[0], jnp.float32)
    cosine_end = jnp.cos(angle)
    sine_end = jnp.sin(angle)
    for side in range(2):
        at_end = pitch_at == (0 if side == 0 else lax.axis_size("pitch") - 1)
        cosine = jnp.where(at_end, cosine_end, 1.0)
        sine_part = jnp.where(at_end, -sine_end if side == 0 else sine_end, 0.0)
        near_at, far_at = (1, 0) if side == 0 else (0, 1)
        edge, inside = (0, 1) if side == 0 else (planes - 1, planes - 2)

        def turned(j, at):
            real = halo_ref[side, j, at]
            imag = halo_ref[side, nv + j, at]
            return (cosine * real - sine_part * imag, sine_part * real + cosine * imag)

        total = [error_ref[k, edge] for k in range(rows)]
        spread_edge = dissipation_ref[0, edge]
        spread_inside = dissipation_ref[0, inside]
        for j in range(nv):
            near = turned(j, near_at)
            far = turned(j, far_at)
            for c in range(2):
                k = c * nv + j
                total[k] = total[k] + spread_edge * far[c]
                store(k, inside, error_ref[k, inside] + spread_inside * near[c])
            for i in range(nv):
                block = neighbour_ref[side, i, j, edge].astype(jnp.float32)
                for c in range(2):
                    total[c * nv + i] = total[c * nv + i] + block * near[c]
        for k in range(rows):
            store(k, edge, total[k])


def turn_kernel(
    halo_ref,
    phase_ref,
    neighbour_ref,
    dissipation_ref,
    step_ref,
    wide_ref,
    error_ref,
    square_in_ref,
    next_in_ref,
    next_ref,
    faces_ref,
    square_ref,
):
    planes = error_ref.shape[1]
    square_ref[...] = square_in_ref[...]

    def store(k, p, error):
        value = wide_ref[k, p + WIDTH] - step_ref[p] * error
        next_ref[k, p + WIDTH] = value
        if p < WIDTH:
            faces_ref[1, k, p] = value
        else:
            faces_ref[0, k, p - (planes - WIDTH)] = value
        square_ref[...] += error * error

    pitch_terms(halo_ref, phase_ref, neighbour_ref, dissipation_ref, error_ref, store)


def last_kernel(
    halo_ref,
    phase_ref,
    neighbour_ref,
    dissipation_ref,
    step_ref,
    wide_ref,
    error_ref,
    next_ref,
    first_square_ref,
    square_in_ref,
    out_ref,
    share_ref,
    edge_buf,
    square_buf,
    sems,
):
    planes = error_ref.shape[1]
    span, lanes = square_buf.shape
    inner = pltpu.make_async_copy(
        next_ref.at[:, 2 * WIDTH : planes], out_ref.at[:, WIDTH : planes - WIDTH], sems.at[0]
    )
    inner.start()
    square_buf[...] = square_in_ref[...]

    def store(k, p, error):
        at = p if p < WIDTH else p - (planes - 2 * WIDTH)
        edge_buf[k, at] = wide_ref[k, p + WIDTH] - step_ref[p] * error
        square_buf[...] += error * error

    pitch_terms(halo_ref, phase_ref, neighbour_ref, dissipation_ref, error_ref, store)
    low = pltpu.make_async_copy(
        edge_buf.at[:, 0:WIDTH], out_ref.at[:, 0:WIDTH], sems.at[1]
    )
    high = pltpu.make_async_copy(
        edge_buf.at[:, WIDTH : 2 * WIDTH], out_ref.at[:, planes - WIDTH : planes], sems.at[2]
    )
    low.start()
    high.start()
    first = jnp.sum(first_square_ref[...], axis=(0, 1), keepdims=True)
    second = jnp.sum(square_buf[...], axis=(0, 1), keepdims=True)
    lane = lax.broadcasted_iota(jnp.int32, share_ref.shape, 2)
    share_ref[...] = jnp.where(
        lane == 0, first.reshape(1, 1, 1), jnp.where(lane == 1, second.reshape(1, 1, 1), 0.0)
    )
    inner.wait()
    low.wait()
    high.wait()


def body(
    guess, right_side, diag_block, neighbour_blocks, dissipation, omega_volume, pseudo_step, phase
):
    parts, nv, planes, span, lanes = guess.shape
    rows = parts * nv
    pitch_count = lax.axis_size("pitch")
    span_count = lax.axis_size("span")
    axial_count = lax.axis_size("axial")
    devices = pitch_count * span_count * axial_count
    wide = (rows, planes + 2 * WIDTH, span, lanes)
    block = (rows, planes, span, lanes)
    faces_shape = (2, rows, WIDTH, span, lanes)
    edge_shape = (rows, planes, WIDTH, lanes)
    axial_shape = (lane_groups(rows, planes, lanes), span, lanes)
    guess = guess.reshape(block)
    right_side = right_side.reshape(block)

    guess = pltpu.with_memory_space_constraint(guess, pltpu.HBM)

    def exchange_pitch(faces):
        up = [(i, (i + 1) % pitch_count) for i in range(pitch_count)]
        down = [(j, i) for i, j in up]
        if sorted(up) == sorted(down):
            return lax.ppermute(faces, "pitch", up)
        return jnp.stack(
            [lax.ppermute(faces[0], "pitch", up), lax.ppermute(faces[1], "pitch", down)]
        )

    def swap(values, axis, start):
        ends = [(i, i + 1) for i in range(start, lax.axis_size(axis) - 1, 2)]
        return resident(lax.ppermute(values, axis, ends + [(j, i) for i, j in ends]))

    def exchange_rest(even, odd, axial):
        return (
            swap(even, "span", 0),
            swap(odd, "span", 1),
            swap(axial, "axial", 0),
            swap(axial, "axial", 1),
        )

    faces = pl.pallas_call(
        pitch_faces_kernel,
        out_shape=kept(faces_shape),
        in_specs=[ANY],
        out_specs=VMEM,
        scratch_shapes=[pltpu.SemaphoreType.DMA((2,))],
        compiler_params=params(),
        name="pitch_faces",
    )(guess)
    state, even, odd, axial = pl.pallas_call(
        first_pack_kernel,
        out_shape=(kept(wide), kept(edge_shape), kept(edge_shape), kept(axial_shape)),
        in_specs=[ANY],
        out_specs=(VMEM,) * 4,
        scratch_shapes=[pltpu.SemaphoreType.DMA],
        compiler_params=params(),
        name="first_pack",
    )(guess)

    hbm = functools.partial(pltpu.with_memory_space_constraint, memory_space=pltpu.HBM)
    groups = GROUPS if planes % GROUPS == 0 else 1
    sources = (neighbour_blocks, diag_block, right_side, dissipation, omega_volume)
    near_shape = (2,) + neighbour_blocks.shape[1:]
    far_shape = (4,) + neighbour_blocks.shape[1:]
    squares = []
    for iteration in range(ITERS):
        halo = resident(exchange_pitch(faces))
        around = exchange_rest(even, odd, axial)
        far_results = (kept(block), kept(wide), kept((span, lanes)))
        far_scratch = [
            pltpu.VMEM((rows, span + 2 * PAD, lanes), jnp.float32),
            pltpu.VMEM(axial_shape, jnp.float32),
        ]
        if iteration == 0:
            error, *near_constants = pl.pallas_call(
                near_loading_kernel,
                out_shape=(
                    kept(block),
                    pltpu.VMEM(near_shape, neighbour_blocks.dtype),
                    *[pltpu.VMEM(c.shape, c.dtype) for c in sources[1:]],
                ),
                in_specs=[VMEM] + [ANY] * 5,
                out_specs=(VMEM,) * 6,
                scratch_shapes=[pltpu.SemaphoreType.DMA((5, groups))],
                compiler_params=params(),
                name="first_near",
            )(state, *[hbm(c) for c in sources])
            near_blocks, _, _, dissipation, _ = near_constants
            error, following, square, far_blocks, pseudo_step = pl.pallas_call(
                far_loading_kernel,
                out_shape=far_results
                + (
                    pltpu.VMEM(far_shape, neighbour_blocks.dtype),
                    pltpu.VMEM(pseudo_step.shape, pseudo_step.dtype),
                ),
                in_specs=[VMEM] * 5 + [ANY, VMEM, ANY, VMEM],
                out_specs=(VMEM,) * 5,
                input_output_aliases={8: 0},
                scratch_shapes=far_scratch + [pltpu.SemaphoreType.DMA((2, groups))],
                compiler_params=params(),
                name="first_far",
            )(state, *around, hbm(neighbour_blocks), dissipation, hbm(pseudo_step), error)
        else:
            error = pl.pallas_call(
                near_kernel,
                out_shape=kept(block),
                in_specs=[VMEM] * 6,
                out_specs=VMEM,
                compiler_params=params(),
                name="near",
            )(state, *near_constants)
            error, following, square = pl.pallas_call(
                far_kernel,
                out_shape=far_results,
                in_specs=[VMEM] * 9,
                out_specs=(VMEM,) * 3,
                input_output_aliases={8: 0},
                scratch_shapes=far_scratch,
                compiler_params=params(),
                name="far",
            )(state, *around, far_blocks, dissipation, pseudo_step, error)
        if iteration < ITERS - 1:
            state, faces, square = pl.pallas_call(
                turn_kernel,
                out_shape=(kept(wide), kept(faces_shape), kept((span, lanes))),
                in_specs=[VMEM, SMEM] + [VMEM] * 7,
                out_specs=(VMEM,) * 3,
                input_output_aliases={8: 0},
                compiler_params=params(),
                name="pitch_terms",
            )(
                halo,
                phase,
                near_blocks,
                dissipation,
                pseudo_step,
                state,
                error,
                square,
                following,
            )
            squares.append(square)
            even, odd, axial = pl.pallas_call(
                pack_kernel,
                out_shape=(kept(edge_shape), kept(edge_shape), kept(axial_shape)),
                in_specs=[VMEM],
                out_specs=(VMEM,) * 3,
                compiler_params=params(),
                name="pack",
            )(state)
        else:
            out, share = pl.pallas_call(
                last_kernel,
                out_shape=(
                    jax.ShapeDtypeStruct(block, jnp.float32),
                    kept((devices, 1, lanes)),
                ),
                in_specs=[VMEM, SMEM] + [VMEM] * 8,
                out_specs=(ANY, VMEM),
                scratch_shapes=[
                    pltpu.VMEM((rows, 2 * WIDTH, span, lanes), jnp.float32),
                    pltpu.VMEM((span, lanes), jnp.float32),
                    pltpu.SemaphoreType.DMA((3,)),
                ],
                compiler_params=params(),
                name="last_pitch_terms",
            )(
                halo,
                phase,
                near_blocks,
                dissipation,
                pseudo_step,
                state,
                error,
                following,
                squares[0],
                square,
            )
    shares = lax.all_to_all(share, ("pitch", "span", "axial"), 0, 0, tiled=True)
    totals = jnp.sum(shares, axis=(0, 1))[:ITERS]
    cell_count = float(rows * planes * span * lanes * devices)
    norms = jnp.sqrt(totals / cell_count)
    return (out.reshape(parts, nv, planes, span, lanes), norms)


def solution(mesh):
    placed = (
        P(None, None, "pitch", "span", "axial"),
        P(None, None, "pitch", "span", "axial"),
        P(None, None, "pitch", "span", "axial"),
        P(None, None, None, "pitch", "span", "axial"),
        P(None, "pitch", "span", "axial"),
        P("pitch", "span", "axial"),
        P("pitch", "span", "axial"),
        P(),
    )
    return jax.shard_map(
        body,
        mesh=mesh,
        in_specs=placed,
        out_specs=(P(None, None, "pitch", "span", "axial"), P()),
        check_vma=False,
    )
```

```python
import functools

import jax
import jax.numpy as jnp
from jax import lax
from jax.experimental import pallas as pl
from jax.experimental.pallas import tpu as pltpu
from jax.sharding import PartitionSpec as P

ITERS = 2
WIDTH = 2
PAD = 8
GROUPS = 4
VMEM = pl.BlockSpec(memory_space=pltpu.VMEM)
SMEM = pl.BlockSpec(memory_space=pltpu.SMEM)
ANY = pl.BlockSpec(memory_space=pl.ANY)
VMEM_LIMIT = 4 * 1024 * 1024


def resident(values):
    return pltpu.with_memory_space_constraint(values, pltpu.VMEM)


def outside(values):
    return pltpu.with_memory_space_constraint(values, pltpu.HBM)


def kept(shape, dtype=jnp.float32):
    return pltpu.VMEM(shape, dtype)


def call(kernel, name, out_shape, in_specs, scratch_shapes=(), aliases=None):
    return pl.pallas_call(
        kernel,
        out_shape=out_shape,
        in_specs=in_specs,
        out_specs=(VMEM,) * len(out_shape),
        scratch_shapes=scratch_shapes,
        input_output_aliases=aliases or {},
        compiler_params=pltpu.CompilerParams(vmem_limit_bytes=VMEM_LIMIT),
        name=name,
    )


def lane_place(k, planes, lanes):
    per_group = (lanes // (2 * WIDTH)) // planes
    return k // per_group, (k % per_group) * planes


def lane_groups(rows, planes, lanes):
    return lane_place(rows - 1, planes, lanes)[0] + 1


def pack_faces(wide_ref, even_ref, odd_ref, axial_ref):
    rows, wide, span, lanes = wide_ref.shape
    planes = wide - 2 * WIDTH
    span_even = lax.axis_index("span") % 2 == 0
    lane = lax.broadcasted_iota(jnp.int32, (span, lanes), 1)
    packed = None
    for k in range(rows):
        group, base = lane_place(k, planes, lanes)
        for p in range(planes):
            cells = wide_ref[k, p + WIDTH]
            low = cells[:WIDTH]
            high = cells[span - WIDTH :]
            even_ref[k, p] = jnp.where(span_even, high, low)
            odd_ref[k, p] = jnp.where(span_even, low, high)
            place = base + p
            moved = pltpu.roll(cells, (2 * WIDTH * place + WIDTH) % lanes, axis=1)
            if place == 0:
                packed = moved
            else:
                packed = jnp.where(lane >= 2 * WIDTH * place, moved, packed)
        if k == rows - 1 or lane_place(k + 1, planes, lanes)[0] != group:
            axial_ref[group] = packed


class Loads:
    def __init__(self, pairs, sems, first, size):
        self.pairs = pairs
        self.sems = sems
        self.first = first
        self.size = size

    def copies(self, group):
        planes = pl.ds(self.first + group * self.size, self.size)
        return [
            pltpu.make_async_copy(
                source.at[(slice(None),) * dim + (planes,)],
                target.at[(slice(None),) * dim + (planes,)],
                self.sems.at[at, group],
            )
            for at, (source, target, dim) in enumerate(self.pairs)
        ]

    def start(self):
        for group in range(self.sems.shape[1]):
            for copy in self.copies(group):
                copy.start()

    def ready(self, p):
        @pl.when(jnp.logical_and(p >= self.first, (p - self.first) % self.size == 0))
        def _():
            for copy in self.copies((p - self.first) // self.size):
                copy.wait()

    def wait(self):
        for group in range(self.sems.shape[1]):
            for copy in self.copies(group):
                copy.wait()


def open_kernel(
    guess_hbm,
    right_hbm,
    dissipation_hbm,
    omega_hbm,
    step_hbm,
    diag_hbm,
    wide_ref,
    faces_ref,
    even_ref,
    odd_ref,
    axial_ref,
    right_ref,
    dissipation_ref,
    omega_ref,
    step_ref,
    diag_ref,
    sems,
):
    rows, wide, span, lanes = wide_ref.shape
    planes = wide - 2 * WIDTH
    pairs = (
        (guess_hbm, wide_ref.at[:, WIDTH : WIDTH + planes]),
        (dissipation_hbm, dissipation_ref),
        (omega_hbm, omega_ref),
        (step_hbm, step_ref),
        (right_hbm, right_ref),
        (diag_hbm, diag_ref),
    )
    copies = [pltpu.make_async_copy(*pair, sems.at[at]) for at, pair in enumerate(pairs)]
    for copy in copies:
        copy.start()
    for k in range(rows):
        for p in (0, 1, wide - 2, wide - 1):
            wide_ref[k, p] = jnp.zeros((span, lanes), jnp.float32)
    copies[0].wait()
    for k in range(rows):
        for at in range(WIDTH):
            faces_ref[0, k, at] = wide_ref[k, planes + at]
            faces_ref[1, k, at] = wide_ref[k, WIDTH + at]
    pack_faces(wide_ref, even_ref, odd_ref, axial_ref)
    for copy in copies[1:]:
        copy.wait()


def near_loading_kernel(
    wide_ref,
    neighbour_hbm,
    diag_ref,
    right_ref,
    dissipation_ref,
    omega_ref,
    error_ref,
    lower_ref,
    upper_ref,
    spaced_ref,
    neighbour_ref,
    far_ref,
    near_sems,
    far_sems,
):
    planes = error_ref.shape[1]
    groups = near_sems.shape[1]
    loads = Loads([(neighbour_hbm.at[0:2], neighbour_ref, 3)], near_sems, 0, planes // groups)
    later = Loads([(neighbour_hbm.at[2:6], far_ref, 3)], far_sems, 0, planes // 2)
    loads.start()
    later.start()
    near_sweep(
        wide_ref,
        neighbour_ref,
        diag_ref,
        right_ref,
        dissipation_ref,
        omega_ref,
        error_ref,
        lower_ref,
        upper_ref,
        spaced_ref,
        loads,
    )
    later.wait()


def near_kernel(*refs):
    near_sweep(*refs, None)


def near_sweep(
    wide_ref,
    neighbour_ref,
    diag_ref,
    right_ref,
    dissipation_ref,
    omega_ref,
    error_ref,
    lower_ref,
    upper_ref,
    spaced_ref,
    loads,
):
    rows, planes, span, lanes = error_ref.shape
    nv = rows // 2
    lane = lax.broadcasted_iota(jnp.int32, (span, lanes), 1)
    edge = jnp.logical_or(lane < WIDTH, lane >= lanes - WIDTH)

    def plane(p, carry):
        if loads is not None:
            loads.ready(p)
        omega = omega_ref[p]
        spread = dissipation_ref[0, p]
        total = []
        for k in range(rows):
            other = wide_ref[(k + nv) % rows, p + WIDTH]
            turned = -omega * other if k < nv else omega * other
            far = wide_ref[k, p] + wide_ref[k, p + 2 * WIDTH]
            total.append((turned - right_ref[k, p]) + spread * far)
        for j in range(nv):
            for at, blocks in (
                (2, lambda i: diag_ref[i, j, p]),
                (1, lambda i: neighbour_ref[0, i, j, p]),
                (3, lambda i: neighbour_ref[1, i, j, p]),
            ):
                real = wide_ref[j, p + at]
                imag = wide_ref[nv + j, p + at]
                for i in range(nv):
                    block = blocks(i).astype(jnp.float32)
                    total[i] = total[i] + block * real
                    total[nv + i] = total[nv + i] + block * imag
            for k in (j, nv + j):
                cells = wide_ref[k, p + WIDTH]
                lower_ref[k, p] = pltpu.roll(cells, 1, axis=1)
                upper_ref[k, p] = pltpu.roll(cells, lanes - 1, axis=1)
                spaced = pltpu.roll(cells, 2, axis=1) + pltpu.roll(cells, lanes - 2, axis=1)
                low = pltpu.roll(cells, 2, axis=1)
                high = pltpu.roll(cells, lanes - 2, axis=1)
                spaced_ref[k, p] = jnp.where(
                    edge, jnp.where(lane < WIDTH, high, low), spaced
                )
        for k in range(rows):
            error_ref[k, p] = total[k]
        return carry

    lax.fori_loop(0, planes, plane, 0)


def far_loading_kernel(
    wide_in_ref,
    error_in_ref,
    neighbour_in_ref,
    neighbour_hbm,
    span_even_ref,
    span_odd_ref,
    axial_even_ref,
    axial_odd_ref,
    lower_ref,
    upper_ref,
    spaced_ref,
    dissipation_ref,
    step_ref,
    wide_ref,
    error_ref,
    neighbour_ref,
    square_ref,
    span_buf,
    axial_buf,
    sems,
):
    planes = error_ref.shape[1]
    half = planes // 2
    loads = Loads(
        [(neighbour_hbm.at[2:6], neighbour_ref, 3)], sems, half, (planes - half) // sems.shape[1]
    )
    loads.start()
    far_sweep(
        neighbour_ref,
        span_even_ref,
        span_odd_ref,
        axial_even_ref,
        axial_odd_ref,
        lower_ref,
        upper_ref,
        spaced_ref,
        dissipation_ref,
        step_ref,
        wide_ref,
        error_ref,
        square_ref,
        span_buf,
        axial_buf,
        loads,
    )


def far_kernel(wide_in_ref, error_in_ref, *refs):
    far_sweep(*refs, None)


def far_sweep(
    neighbour_ref,
    span_even_ref,
    span_odd_ref,
    axial_even_ref,
    axial_odd_ref,
    lower_ref,
    upper_ref,
    spaced_ref,
    dissipation_ref,
    step_ref,
    wide_ref,
    error_ref,
    square_ref,
    span_buf,
    axial_buf,
    loads,
):
    rows, planes, span, lanes = error_ref.shape
    nv = rows // 2
    span_even = lax.axis_index("span") % 2 == 0
    axial_even = lax.axis_index("axial") % 2 == 0
    lane = lax.broadcasted_iota(jnp.int32, (span, lanes), 1)
    edge = jnp.logical_or(lane < WIDTH, lane >= lanes - WIDTH)
    from_below = lane % (2 * WIDTH) >= WIDTH
    for group in range(axial_buf.shape[0]):
        at_even = axial_even_ref[group]
        at_odd = axial_odd_ref[group]
        below = pltpu.roll(jnp.where(axial_even, at_odd, at_even), WIDTH, axis=1)
        above = pltpu.roll(jnp.where(axial_even, at_even, at_odd), lanes - WIDTH, axis=1)
        axial_buf[group] = jnp.where(from_below, below, above)
    square_ref[...] = jnp.zeros_like(square_ref)

    def plane(p, carry):
        if loads is not None:
            loads.ready(p)
        for k in range(rows):
            at_even = span_even_ref[k, p]
            at_odd = span_odd_ref[k, p]
            span_buf[k, PAD - WIDTH : PAD] = jnp.where(span_even, at_odd, at_even)
            span_buf[k, PAD : PAD + span] = wide_ref[k, p + WIDTH]
            span_buf[k, PAD + span : PAD + span + WIDTH] = jnp.where(span_even, at_even, at_odd)
        total = [error_ref[k, p] for k in range(rows)]
        spread_span = dissipation_ref[1, p]
        spread_axial = dissipation_ref[2, p]

        def column(direction, j, real, imag):
            for i in range(nv):
                block = neighbour_ref[direction, i, j, p].astype(jnp.float32)
                total[i] = total[i] + block * real
                total[nv + i] = total[nv + i] + block * imag

        for j in range(nv):
            pair = (j, nv + j)
            column(0, j, *[span_buf[k, PAD - 1 : PAD - 1 + span] for k in pair])
            column(1, j, *[span_buf[k, PAD + 1 : PAD + 1 + span] for k in pair])
            lower = []
            upper = []
            for k in pair:
                group, base = lane_place(k, planes, lanes)
                packed = axial_buf[group]
                shift = lanes - WIDTH - 2 * WIDTH * base - 2 * WIDTH * p
                below = pltpu.roll(packed, shift - 1, axis=1)
                above = pltpu.roll(packed, shift + 1, axis=1)
                beyond = pltpu.roll(packed, shift, axis=1)
                lower.append(jnp.where(lane < 1, below, lower_ref[k, p]))
                upper.append(jnp.where(lane >= lanes - 1, above, upper_ref[k, p]))
                far = spaced_ref[k, p] + jnp.where(edge, beyond, 0.0)
                total[k] = total[k] + spread_axial * far
                far = (
                    span_buf[k, PAD - 2 : PAD - 2 + span] + span_buf[k, PAD + 2 : PAD + 2 + span]
                )
                total[k] = total[k] + spread_span * far
            column(2, j, *lower)
            column(3, j, *upper)
        step = step_ref[p]
        square = None
        for k in range(rows):
            error = total[k]
            error_ref[k, p] = error
            wide_ref[k, p + WIDTH] = wide_ref[k, p + WIDTH] - step * error
            square = error * error if square is None else square + error * error
        inner = jnp.logical_and(p >= WIDTH, p < planes - WIDTH)
        square_ref[...] += jnp.where(inner, square, 0.0)
        return carry

    lax.fori_loop(0, planes, plane, 0)


def pitch_terms(halo_ref, phase_ref, neighbour_ref, dissipation_ref, error_ref, store):
    rows, planes, span, lanes = error_ref.shape
    nv = rows // 2
    pitch_at = lax.axis_index("pitch")
    angle = jnp.full((span, lanes), phase_ref[0], jnp.float32)
    cosine_end = jnp.cos(angle)
    sine_end = jnp.sin(angle)
    for side in range(2):
        at_end = pitch_at == (0 if side == 0 else lax.axis_size("pitch") - 1)
        cosine = jnp.where(at_end, cosine_end, 1.0)
        sine_part = jnp.where(at_end, -sine_end if side == 0 else sine_end, 0.0)
        near_at, far_at = (1, 0) if side == 0 else (0, 1)
        edge, inside = (0, 1) if side == 0 else (planes - 1, planes - 2)

        def turned(j, at):
            real = halo_ref[side, j, at]
            imag = halo_ref[side, nv + j, at]
            return (cosine * real - sine_part * imag, sine_part * real + cosine * imag)

        total = [None] * rows

        def add(k, value):
            total[k] = value if total[k] is None else total[k] + value

        spread_edge = dissipation_ref[0, edge]
        spread_inside = dissipation_ref[0, inside]
        for j in range(nv):
            near = turned(j, near_at)
            far = turned(j, far_at)
            for c in range(2):
                k = c * nv + j
                add(k, spread_edge * far[c])
                store(k, inside, spread_inside * near[c])
            for i in range(nv):
                block = neighbour_ref[side, i, j, edge].astype(jnp.float32)
                for c in range(2):
                    add(c * nv + i, block * near[c])
        for k in range(rows):
            store(k, edge, total[k])


def turn_kernel(
    wide_in_ref,
    halo_ref,
    phase_ref,
    neighbour_ref,
    dissipation_ref,
    step_ref,
    error_ref,
    square_in_ref,
    wide_ref,
    faces_ref,
    even_ref,
    odd_ref,
    axial_ref,
    square_ref,
):
    planes = error_ref.shape[1]
    square_ref[...] = square_in_ref[...]

    def store(k, p, change):
        value = wide_ref[k, p + WIDTH] - step_ref[p] * change
        wide_ref[k, p + WIDTH] = value
        if p < WIDTH:
            faces_ref[1, k, p] = value
        else:
            faces_ref[0, k, p - (planes - WIDTH)] = value
        error = error_ref[k, p] + change
        square_ref[...] += error * error

    pitch_terms(halo_ref, phase_ref, neighbour_ref, dissipation_ref, error_ref, store)
    pack_faces(wide_ref, even_ref, odd_ref, axial_ref)


def last_kernel(
    wide_ref,
    halo_ref,
    phase_ref,
    neighbour_ref,
    dissipation_ref,
    step_ref,
    error_ref,
    square_in_ref,
    first_square_ref,
    out_ref,
    share_ref,
    square_buf,
):
    rows, planes, _, _ = error_ref.shape
    square_buf[...] = square_in_ref[...]
    for k in range(rows):
        for p in range(WIDTH, planes - WIDTH):
            out_ref[k, p] = wide_ref[k, p + WIDTH]

    def store(k, p, change):
        out_ref[k, p] = wide_ref[k, p + WIDTH] - step_ref[p] * change
        error = error_ref[k, p] + change
        square_buf[...] += error * error

    pitch_terms(halo_ref, phase_ref, neighbour_ref, dissipation_ref, error_ref, store)
    first = jnp.sum(first_square_ref[...], axis=(0, 1), keepdims=True)
    second = jnp.sum(square_buf[...], axis=(0, 1), keepdims=True)
    lane = lax.broadcasted_iota(jnp.int32, share_ref.shape, 2)
    share_ref[...] = jnp.where(
        lane == 0, first.reshape(1, 1, 1), jnp.where(lane == 1, second.reshape(1, 1, 1), 0.0)
    )


def body(
    guess, right_side, diag_block, neighbour_blocks, dissipation, omega_volume, pseudo_step, phase
):
    parts, nv, planes, span, lanes = guess.shape
    rows = parts * nv
    pitch_count = lax.axis_size("pitch")
    devices = pitch_count * lax.axis_size("span") * lax.axis_size("axial")
    wide = (rows, planes + 2 * WIDTH, span, lanes)
    block = (rows, planes, span, lanes)
    tile = (span, lanes)
    face_shapes = (
        kept((2, rows, WIDTH, span, lanes)),
        kept((rows, planes, WIDTH, lanes)),
        kept((rows, planes, WIDTH, lanes)),
        kept((lane_groups(rows, planes, lanes), span, lanes)),
    )
    groups = GROUPS if planes % GROUPS == 0 else 1
    half_groups = 2 if planes % 4 == 0 else 1
    dma = pltpu.SemaphoreType.DMA

    def exchange_pitch(faces):
        up = [(i, (i + 1) % pitch_count) for i in range(pitch_count)]
        down = [(j, i) for i, j in up]
        if sorted(up) == sorted(down):
            return lax.ppermute(faces, "pitch", up)
        return jnp.stack(
            [lax.ppermute(faces[0], "pitch", up), lax.ppermute(faces[1], "pitch", down)]
        )

    def swap(values, axis, start):
        ends = [(i, i + 1) for i in range(start, lax.axis_size(axis) - 1, 2)]
        return resident(lax.ppermute(values, axis, ends + [(j, i) for i, j in ends]))

    def exchange_rest(even, odd, axial):
        return (
            swap(even, "span", 0),
            swap(odd, "span", 1),
            swap(axial, "axial", 0),
            swap(axial, "axial", 1),
        )

    neighbour_blocks = outside(neighbour_blocks)
    sources = (right_side.reshape(block), dissipation, omega_volume, pseudo_step, diag_block)
    state, faces, even, odd, axial, right, dissipation, omega, step, diag = call(
        open_kernel,
        "open",
        (kept(wide),)
        + face_shapes
        + tuple(kept(c.shape, c.dtype) for c in sources),
        [ANY] * 6,
        [dma((6,))],
    )(outside(guess.reshape(block)), *[outside(c) for c in sources])

    squares = []
    for iteration in range(ITERS):
        halo = resident(exchange_pitch(faces))
        around = exchange_rest(even, odd, axial)
        near_results = (kept(block),) * 4
        far_results = (kept(wide), kept(block))
        far_scratch = [pltpu.VMEM((rows, span + 2 * PAD, lanes), jnp.float32)] + [
            pltpu.VMEM(face_shapes[3].shape, jnp.float32)
        ]
        if iteration == 0:
            near_blocks = kept((2,) + neighbour_blocks.shape[1:], neighbour_blocks.dtype)
            far_blocks = kept((4,) + neighbour_blocks.shape[1:], neighbour_blocks.dtype)
            error, lower, upper, spaced, near_blocks, far_half = call(
                near_loading_kernel,
                "first_near",
                near_results + (near_blocks, far_blocks),
                [VMEM, ANY] + [VMEM] * 4,
                [dma((1, groups)), dma((1, 1))],
            )(state, neighbour_blocks, diag, right, dissipation, omega)
            state, error, far_blocks, square = call(
                far_loading_kernel,
                "first_far",
                far_results + (far_blocks, kept(tile)),
                [VMEM] * 3 + [ANY] + [VMEM] * 9,
                far_scratch + [dma((1, half_groups))],
                {0: 0, 1: 1, 2: 2},
            )(
                state,
                error,
                far_half,
                neighbour_blocks,
                *around,
                lower,
                upper,
                spaced,
                dissipation,
                step,
            )
        else:
            error, lower, upper, spaced = call(
                near_kernel, "near", near_results, [VMEM] * 6
            )(state, near_blocks, diag, right, dissipation, omega)
            state, error, square = call(
                far_kernel,
                "far",
                far_results + (kept(tile),),
                [VMEM] * 12,
                far_scratch,
                {0: 0, 1: 1},
            )(state, error, far_blocks, *around, lower, upper, spaced, dissipation, step)
        terms = (state, halo, phase, near_blocks, dissipation, step, error, square)
        if iteration < ITERS - 1:
            state, faces, even, odd, axial, square = call(
                turn_kernel,
                "pitch_terms",
                (kept(wide),) + face_shapes + (kept(tile),),
                [VMEM] * 2 + [SMEM] + [VMEM] * 5,
                aliases={0: 0},
            )(*terms)
            squares.append(square)
        else:
            out, share = call(
                last_kernel,
                "last_pitch_terms",
                (kept(block), kept((devices, 1, lanes))),
                [VMEM] * 2 + [SMEM] + [VMEM] * 6,
                [pltpu.VMEM(tile, jnp.float32)],
            )(*terms, squares[0])
    shares = lax.all_to_all(share, ("pitch", "span", "axial"), 0, 0, tiled=True)
    totals = jnp.sum(shares, axis=(0, 1))[:ITERS]
    cell_count = float(rows * planes * span * lanes * devices)
    norms = jnp.sqrt(totals / cell_count)
    return (out.reshape(parts, nv, planes, span, lanes), norms)


def solution(mesh):
    placed = (
        P(None, None, "pitch", "span", "axial"),
        P(None, None, "pitch", "span", "axial"),
        P(None, None, "pitch", "span", "axial"),
        P(None, None, None, "pitch", "span", "axial"),
        P(None, "pitch", "span", "axial"),
        P("pitch", "span", "axial"),
        P("pitch", "span", "axial"),
        P(),
    )
    return jax.shard_map(
        body,
        mesh=mesh,
        in_specs=placed,
        out_specs=(P(None, None, "pitch", "span", "axial"), P()),
        check_vma=False,
    )
```

```python
import functools

import jax
import jax.numpy as jnp
from jax import lax
from jax.experimental import pallas as pl
from jax.experimental.pallas import tpu as pltpu
from jax.sharding import PartitionSpec as P

ITERS = 2
WIDTH = 2
PAD = 8
GROUPS = 4
VMEM = pl.BlockSpec(memory_space=pltpu.VMEM)
SMEM = pl.BlockSpec(memory_space=pltpu.SMEM)
ANY = pl.BlockSpec(memory_space=pl.ANY)
VMEM_LIMIT = 4 * 1024 * 1024


def resident(values):
    return pltpu.with_memory_space_constraint(values, pltpu.VMEM)


def outside(values):
    return pltpu.with_memory_space_constraint(values, pltpu.HBM)


def kept(shape, dtype=jnp.float32):
    return pltpu.VMEM(shape, dtype)


def call(kernel, name, out_shape, in_specs, scratch_shapes=(), aliases=None):
    return pl.pallas_call(
        kernel,
        out_shape=out_shape,
        in_specs=in_specs,
        out_specs=(VMEM,) * len(out_shape),
        scratch_shapes=scratch_shapes,
        input_output_aliases=aliases or {},
        compiler_params=pltpu.CompilerParams(vmem_limit_bytes=VMEM_LIMIT),
        name=name,
    )


def lane_place(k, planes, lanes):
    per_group = (lanes // (2 * WIDTH)) // planes
    return k // per_group, (k % per_group) * planes


def lane_groups(rows, planes, lanes):
    return lane_place(rows - 1, planes, lanes)[0] + 1


def pack_faces(wide_ref, even_ref, odd_ref, axial_ref):
    rows, wide, span, lanes = wide_ref.shape
    planes = wide - 2 * WIDTH
    span_even = lax.axis_index("span") % 2 == 0
    lane = lax.broadcasted_iota(jnp.int32, (span, lanes), 1)
    packed = None
    for k in range(rows):
        group, base = lane_place(k, planes, lanes)
        for p in range(planes):
            cells = wide_ref[k, p + WIDTH]
            low = cells[:WIDTH]
            high = cells[span - WIDTH :]
            even_ref[k, p] = jnp.where(span_even, high, low)
            odd_ref[k, p] = jnp.where(span_even, low, high)
            place = base + p
            moved = pltpu.roll(cells, (2 * WIDTH * place + WIDTH) % lanes, axis=1)
            if place == 0:
                packed = moved
            else:
                packed = jnp.where(lane >= 2 * WIDTH * place, moved, packed)
        if k == rows - 1 or lane_place(k + 1, planes, lanes)[0] != group:
            axial_ref[group] = packed


def alone(axis):
    at = lax.axis_index(axis)
    count = lax.axis_size(axis)
    return jnp.logical_or(at == 0, jnp.logical_and(at == count - 1, count % 2 == 0))


class Loads:
    def __init__(self, pairs, sems, first, size):
        self.pairs = pairs
        self.sems = sems
        self.first = first
        self.size = size

    def copies(self, group):
        planes = pl.ds(self.first + group * self.size, self.size)
        return [
            pltpu.make_async_copy(
                source.at[(slice(None),) * dim + (planes,)],
                target.at[(slice(None),) * dim + (planes,)],
                self.sems.at[at, group],
            )
            for at, (source, target, dim) in enumerate(self.pairs)
        ]

    def start(self):
        for group in range(self.sems.shape[1]):
            for copy in self.copies(group):
                copy.start()

    def ready(self, p):
        @pl.when(jnp.logical_and(p >= self.first, (p - self.first) % self.size == 0))
        def _():
            for copy in self.copies((p - self.first) // self.size):
                copy.wait()

    def wait(self):
        for group in range(self.sems.shape[1]):
            for copy in self.copies(group):
                copy.wait()


def open_kernel(
    guess_hbm,
    right_hbm,
    dissipation_hbm,
    omega_hbm,
    step_hbm,
    diag_hbm,
    wide_ref,
    faces_ref,
    even_ref,
    odd_ref,
    axial_ref,
    right_ref,
    dissipation_ref,
    omega_ref,
    step_ref,
    diag_ref,
    sems,
):
    rows, wide, span, lanes = wide_ref.shape
    planes = wide - 2 * WIDTH
    pairs = (
        (guess_hbm, wide_ref.at[:, WIDTH : WIDTH + planes]),
        (dissipation_hbm, dissipation_ref),
        (omega_hbm, omega_ref),
        (step_hbm, step_ref),
        (right_hbm, right_ref),
        (diag_hbm, diag_ref),
    )
    copies = [pltpu.make_async_copy(*pair, sems.at[at]) for at, pair in enumerate(pairs)]
    for copy in copies:
        copy.start()
    for k in range(rows):
        for p in (0, 1, wide - 2, wide - 1):
            wide_ref[k, p] = jnp.zeros((span, lanes), jnp.float32)
    copies[0].wait()
    for k in range(rows):
        for at in range(WIDTH):
            faces_ref[0, k, at] = wide_ref[k, planes + at]
            faces_ref[1, k, at] = wide_ref[k, WIDTH + at]
    pack_faces(wide_ref, even_ref, odd_ref, axial_ref)
    for copy in copies[1:]:
        copy.wait()


def near_loading_kernel(
    wide_ref,
    neighbour_hbm,
    diag_ref,
    right_ref,
    dissipation_ref,
    omega_ref,
    error_ref,
    lower_ref,
    upper_ref,
    spaced_ref,
    neighbour_ref,
    far_ref,
    near_sems,
    far_sems,
):
    planes = error_ref.shape[1]
    groups = near_sems.shape[1]
    loads = Loads([(neighbour_hbm.at[0:2], neighbour_ref, 3)], near_sems, 0, planes // groups)
    later = Loads([(neighbour_hbm.at[2:6], far_ref, 3)], far_sems, 0, planes // 2)
    loads.start()
    later.start()
    near_sweep(
        wide_ref,
        neighbour_ref,
        diag_ref,
        right_ref,
        dissipation_ref,
        omega_ref,
        error_ref,
        lower_ref,
        upper_ref,
        spaced_ref,
        loads,
    )
    later.wait()


def near_kernel(*refs):
    near_sweep(*refs, None)


def near_sweep(
    wide_ref,
    neighbour_ref,
    diag_ref,
    right_ref,
    dissipation_ref,
    omega_ref,
    error_ref,
    lower_ref,
    upper_ref,
    spaced_ref,
    loads,
):
    rows, planes, span, lanes = error_ref.shape
    nv = rows // 2
    lane = lax.broadcasted_iota(jnp.int32, (span, lanes), 1)
    edge = jnp.logical_or(lane < WIDTH, lane >= lanes - WIDTH)

    def plane(p, carry):
        if loads is not None:
            loads.ready(p)
        omega = omega_ref[p]
        spread = dissipation_ref[0, p]
        total = []
        for k in range(rows):
            other = wide_ref[(k + nv) % rows, p + WIDTH]
            turned = -omega * other if k < nv else omega * other
            far = wide_ref[k, p] + wide_ref[k, p + 2 * WIDTH]
            total.append((turned - right_ref[k, p]) + spread * far)
        for j in range(nv):
            for at, blocks in (
                (2, lambda i: diag_ref[i, j, p]),
                (1, lambda i: neighbour_ref[0, i, j, p]),
                (3, lambda i: neighbour_ref[1, i, j, p]),
            ):
                real = wide_ref[j, p + at]
                imag = wide_ref[nv + j, p + at]
                for i in range(nv):
                    block = blocks(i).astype(jnp.float32)
                    total[i] = total[i] + block * real
                    total[nv + i] = total[nv + i] + block * imag
            for k in (j, nv + j):
                cells = wide_ref[k, p + WIDTH]
                lower_ref[k, p] = pltpu.roll(cells, 1, axis=1)
                upper_ref[k, p] = pltpu.roll(cells, lanes - 1, axis=1)
                spaced = pltpu.roll(cells, 2, axis=1) + pltpu.roll(cells, lanes - 2, axis=1)
                low = pltpu.roll(cells, 2, axis=1)
                high = pltpu.roll(cells, lanes - 2, axis=1)
                spaced_ref[k, p] = jnp.where(
                    edge, jnp.where(lane < WIDTH, high, low), spaced
                )
        for k in range(rows):
            error_ref[k, p] = total[k]
        return carry

    lax.fori_loop(0, planes, plane, 0)


def far_loading_kernel(
    wide_in_ref,
    error_in_ref,
    neighbour_in_ref,
    neighbour_hbm,
    span_even_ref,
    span_odd_ref,
    axial_even_ref,
    axial_odd_ref,
    lower_ref,
    upper_ref,
    spaced_ref,
    dissipation_ref,
    step_ref,
    wide_ref,
    error_ref,
    neighbour_ref,
    square_ref,
    span_buf,
    axial_buf,
    sems,
):
    planes = error_ref.shape[1]
    half = planes // 2
    loads = Loads(
        [(neighbour_hbm.at[2:6], neighbour_ref, 3)], sems, half, (planes - half) // sems.shape[1]
    )
    loads.start()
    far_sweep(
        neighbour_ref,
        span_even_ref,
        span_odd_ref,
        axial_even_ref,
        axial_odd_ref,
        lower_ref,
        upper_ref,
        spaced_ref,
        dissipation_ref,
        step_ref,
        wide_ref,
        error_ref,
        square_ref,
        span_buf,
        axial_buf,
        loads,
    )


def far_kernel(wide_in_ref, error_in_ref, *refs):
    far_sweep(*refs, None)


def far_sweep(
    neighbour_ref,
    span_even_ref,
    span_odd_ref,
    axial_even_ref,
    axial_odd_ref,
    lower_ref,
    upper_ref,
    spaced_ref,
    dissipation_ref,
    step_ref,
    wide_ref,
    error_ref,
    square_ref,
    span_buf,
    axial_buf,
    loads,
):
    rows, planes, span, lanes = error_ref.shape
    nv = rows // 2
    span_even = lax.axis_index("span") % 2 == 0
    axial_even = lax.axis_index("axial") % 2 == 0
    span_alone = alone("span")
    axial_alone = alone("axial")
    lane = lax.broadcasted_iota(jnp.int32, (span, lanes), 1)
    edge = jnp.logical_or(lane < WIDTH, lane >= lanes - WIDTH)
    from_below = lane % (2 * WIDTH) >= WIDTH
    for group in range(axial_buf.shape[0]):
        at_even = axial_even_ref[group]
        at_odd = jnp.where(axial_alone, 0.0, axial_odd_ref[group])
        below = pltpu.roll(jnp.where(axial_even, at_odd, at_even), WIDTH, axis=1)
        above = pltpu.roll(jnp.where(axial_even, at_even, at_odd), lanes - WIDTH, axis=1)
        axial_buf[group] = jnp.where(from_below, below, above)
    square_ref[...] = jnp.zeros_like(square_ref)

    def plane(p, carry):
        if loads is not None:
            loads.ready(p)
        for k in range(rows):
            at_even = span_even_ref[k, p]
            at_odd = jnp.where(span_alone, 0.0, span_odd_ref[k, p])
            span_buf[k, PAD - WIDTH : PAD] = jnp.where(span_even, at_odd, at_even)
            span_buf[k, PAD : PAD + span] = wide_ref[k, p + WIDTH]
            span_buf[k, PAD + span : PAD + span + WIDTH] = jnp.where(span_even, at_even, at_odd)
        total = [error_ref[k, p] for k in range(rows)]
        spread_span = dissipation_ref[1, p]
        spread_axial = dissipation_ref[2, p]

        def column(direction, j, real, imag):
            for i in range(nv):
                block = neighbour_ref[direction, i, j, p].astype(jnp.float32)
                total[i] = total[i] + block * real
                total[nv + i] = total[nv + i] + block * imag

        for j in range(nv):
            pair = (j, nv + j)
            column(0, j, *[span_buf[k, PAD - 1 : PAD - 1 + span] for k in pair])
            column(1, j, *[span_buf[k, PAD + 1 : PAD + 1 + span] for k in pair])
            lower = []
            upper = []
            for k in pair:
                group, base = lane_place(k, planes, lanes)
                packed = axial_buf[group]
                shift = lanes - WIDTH - 2 * WIDTH * base - 2 * WIDTH * p
                below = pltpu.roll(packed, shift - 1, axis=1)
                above = pltpu.roll(packed, shift + 1, axis=1)
                beyond = pltpu.roll(packed, shift, axis=1)
                lower.append(jnp.where(lane < 1, below, lower_ref[k, p]))
                upper.append(jnp.where(lane >= lanes - 1, above, upper_ref[k, p]))
                far = spaced_ref[k, p] + jnp.where(edge, beyond, 0.0)
                total[k] = total[k] + spread_axial * far
                far = (
                    span_buf[k, PAD - 2 : PAD - 2 + span] + span_buf[k, PAD + 2 : PAD + 2 + span]
                )
                total[k] = total[k] + spread_span * far
            column(2, j, *lower)
            column(3, j, *upper)
        step = step_ref[p]
        square = None
        for k in range(rows):
            error = total[k]
            error_ref[k, p] = error
            wide_ref[k, p + WIDTH] = wide_ref[k, p + WIDTH] - step * error
            square = error * error if square is None else square + error * error
        inner = jnp.logical_and(p >= WIDTH, p < planes - WIDTH)
        square_ref[...] += jnp.where(inner, square, 0.0)
        return carry

    lax.fori_loop(0, planes, plane, 0)


def pitch_terms(halo_ref, phase_ref, neighbour_ref, dissipation_ref, error_ref, store):
    rows, planes, span, lanes = error_ref.shape
    nv = rows // 2
    pitch_at = lax.axis_index("pitch")
    angle = jnp.full((span, lanes), phase_ref[0], jnp.float32)
    cosine_end = jnp.cos(angle)
    sine_end = jnp.sin(angle)
    for side in range(2):
        at_end = pitch_at == (0 if side == 0 else lax.axis_size("pitch") - 1)
        cosine = jnp.where(at_end, cosine_end, 1.0)
        sine_part = jnp.where(at_end, -sine_end if side == 0 else sine_end, 0.0)
        near_at, far_at = (1, 0) if side == 0 else (0, 1)
        edge, inside = (0, 1) if side == 0 else (planes - 1, planes - 2)

        def turned(j, at):
            real = halo_ref[side, j, at]
            imag = halo_ref[side, nv + j, at]
            return (cosine * real - sine_part * imag, sine_part * real + cosine * imag)

        total = [None] * rows

        def add(k, value):
            total[k] = value if total[k] is None else total[k] + value

        spread_edge = dissipation_ref[0, edge]
        spread_inside = dissipation_ref[0, inside]
        for j in range(nv):
            near = turned(j, near_at)
            far = turned(j, far_at)
            for c in range(2):
                k = c * nv + j
                add(k, spread_edge * far[c])
                store(k, inside, spread_inside * near[c])
            for i in range(nv):
                block = neighbour_ref[side, i, j, edge].astype(jnp.float32)
                for c in range(2):
                    add(c * nv + i, block * near[c])
        for k in range(rows):
            store(k, edge, total[k])


def turn_kernel(
    wide_in_ref,
    halo_ref,
    phase_ref,
    neighbour_ref,
    dissipation_ref,
    step_ref,
    error_ref,
    square_in_ref,
    wide_ref,
    faces_ref,
    even_ref,
    odd_ref,
    axial_ref,
    square_ref,
):
    planes = error_ref.shape[1]
    square_ref[...] = square_in_ref[...]

    def store(k, p, change):
        value = wide_ref[k, p + WIDTH] - step_ref[p] * change
        wide_ref[k, p + WIDTH] = value
        if p < WIDTH:
            faces_ref[1, k, p] = value
        else:
            faces_ref[0, k, p - (planes - WIDTH)] = value
        error = error_ref[k, p] + change
        square_ref[...] += error * error

    pitch_terms(halo_ref, phase_ref, neighbour_ref, dissipation_ref, error_ref, store)
    pack_faces(wide_ref, even_ref, odd_ref, axial_ref)


def last_kernel(
    wide_ref,
    halo_ref,
    phase_ref,
    neighbour_ref,
    dissipation_ref,
    step_ref,
    error_ref,
    square_in_ref,
    first_square_ref,
    out_ref,
    share_ref,
    square_buf,
):
    rows, planes, _, _ = error_ref.shape
    square_buf[...] = square_in_ref[...]
    for k in range(rows):
        for p in range(WIDTH, planes - WIDTH):
            out_ref[k, p] = wide_ref[k, p + WIDTH]

    def store(k, p, change):
        out_ref[k, p] = wide_ref[k, p + WIDTH] - step_ref[p] * change
        error = error_ref[k, p] + change
        square_buf[...] += error * error

    pitch_terms(halo_ref, phase_ref, neighbour_ref, dissipation_ref, error_ref, store)
    first = jnp.sum(first_square_ref[...], axis=(0, 1), keepdims=True)
    second = jnp.sum(square_buf[...], axis=(0, 1), keepdims=True)
    lane = lax.broadcasted_iota(jnp.int32, share_ref.shape, 2)
    share_ref[...] = jnp.where(
        lane == 0, first.reshape(1, 1, 1), jnp.where(lane == 1, second.reshape(1, 1, 1), 0.0)
    )


def body(
    guess, right_side, diag_block, neighbour_blocks, dissipation, omega_volume, pseudo_step, phase
):
    parts, nv, planes, span, lanes = guess.shape
    rows = parts * nv
    pitch_count = lax.axis_size("pitch")
    devices = pitch_count * lax.axis_size("span") * lax.axis_size("axial")
    wide = (rows, planes + 2 * WIDTH, span, lanes)
    block = (rows, planes, span, lanes)
    tile = (span, lanes)
    face_shapes = (
        kept((2, rows, WIDTH, span, lanes)),
        kept((rows, planes, WIDTH, lanes)),
        kept((rows, planes, WIDTH, lanes)),
        kept((lane_groups(rows, planes, lanes), span, lanes)),
    )
    groups = GROUPS if planes % GROUPS == 0 else 1
    half_groups = 2 if planes % 4 == 0 else 1
    dma = pltpu.SemaphoreType.DMA

    def exchange_pitch(faces):
        up = [(i, (i + 1) % pitch_count) for i in range(pitch_count)]
        down = [(j, i) for i, j in up]
        if sorted(up) == sorted(down):
            return lax.ppermute(faces, "pitch", up)
        return jnp.stack(
            [lax.ppermute(faces[0], "pitch", up), lax.ppermute(faces[1], "pitch", down)]
        )

    span_count = lax.axis_size("span")
    axial_count = lax.axis_size("axial")

    def span_swap(values, start):
        partner = {}
        for i in range(start, span_count - 1, 2):
            partner.update({i: i + 1, i + 1: i})
        pairs = []
        for i in range(span_count):
            for j in range(axial_count):
                if i in partner:
                    pairs.append((i * axial_count + j, partner[i] * axial_count + j))
                elif axial_count % 2 == 0:
                    pairs.append((i * axial_count + j, i * axial_count + (j ^ 1)))
        return resident(lax.ppermute(values, ("span", "axial"), pairs))

    def axial_swap(values, start):
        pairs = [(i, i + 1) for i in range(start, axial_count - 1, 2)]
        if start == 1 and axial_count % 2 == 0:
            pairs.append((0, axial_count - 1))
        return resident(lax.ppermute(values, "axial", pairs + [(j, i) for i, j in pairs]))

    def exchange_rest(even, odd, axial):
        return (
            span_swap(even, 0),
            span_swap(odd, 1),
            axial_swap(axial, 0),
            axial_swap(axial, 1),
        )

    neighbour_blocks = outside(neighbour_blocks)
    sources = (right_side.reshape(block), dissipation, omega_volume, pseudo_step, diag_block)
    state, faces, even, odd, axial, right, dissipation, omega, step, diag = call(
        open_kernel,
        "open",
        (kept(wide),)
        + face_shapes
        + tuple(kept(c.shape, c.dtype) for c in sources),
        [ANY] * 6,
        [dma((6,))],
    )(outside(guess.reshape(block)), *[outside(c) for c in sources])

    squares = []
    for iteration in range(ITERS):
        halo = resident(exchange_pitch(faces))
        around = exchange_rest(even, odd, axial)
        near_results = (kept(block),) * 4
        far_results = (kept(wide), kept(block))
        far_scratch = [pltpu.VMEM((rows, span + 2 * PAD, lanes), jnp.float32)] + [
            pltpu.VMEM(face_shapes[3].shape, jnp.float32)
        ]
        if iteration == 0:
            near_blocks = kept((2,) + neighbour_blocks.shape[1:], neighbour_blocks.dtype)
            far_blocks = kept((4,) + neighbour_blocks.shape[1:], neighbour_blocks.dtype)
            error, lower, upper, spaced, near_blocks, far_half = call(
                near_loading_kernel,
                "first_near",
                near_results + (near_blocks, far_blocks),
                [VMEM, ANY] + [VMEM] * 4,
                [dma((1, groups)), dma((1, 1))],
            )(state, neighbour_blocks, diag, right, dissipation, omega)
            state, error, far_blocks, square = call(
                far_loading_kernel,
                "first_far",
                far_results + (far_blocks, kept(tile)),
                [VMEM] * 3 + [ANY] + [VMEM] * 9,
                far_scratch + [dma((1, half_groups))],
                {0: 0, 1: 1, 2: 2},
            )(
                state,
                error,
                far_half,
                neighbour_blocks,
                *around,
                lower,
                upper,
                spaced,
                dissipation,
                step,
            )
        else:
            error, lower, upper, spaced = call(
                near_kernel, "near", near_results, [VMEM] * 6
            )(state, near_blocks, diag, right, dissipation, omega)
            state, error, square = call(
                far_kernel,
                "far",
                far_results + (kept(tile),),
                [VMEM] * 12,
                far_scratch,
                {0: 0, 1: 1},
            )(state, error, far_blocks, *around, lower, upper, spaced, dissipation, step)
        terms = (state, halo, phase, near_blocks, dissipation, step, error, square)
        if iteration < ITERS - 1:
            state, faces, even, odd, axial, square = call(
                turn_kernel,
                "pitch_terms",
                (kept(wide),) + face_shapes + (kept(tile),),
                [VMEM] * 2 + [SMEM] + [VMEM] * 5,
                aliases={0: 0},
            )(*terms)
            squares.append(square)
        else:
            out, share = call(
                last_kernel,
                "last_pitch_terms",
                (kept(block), kept((devices, 1, lanes))),
                [VMEM] * 2 + [SMEM] + [VMEM] * 6,
                [pltpu.VMEM(tile, jnp.float32)],
            )(*terms, squares[0])
    shares = lax.all_to_all(share, ("pitch", "span", "axial"), 0, 0, tiled=True)
    totals = jnp.sum(shares, axis=(0, 1))[:ITERS]
    cell_count = float(rows * planes * span * lanes * devices)
    norms = jnp.sqrt(totals / cell_count)
    return (out.reshape(parts, nv, planes, span, lanes), norms)


def solution(mesh):
    placed = (
        P(None, None, "pitch", "span", "axial"),
        P(None, None, "pitch", "span", "axial"),
        P(None, None, "pitch", "span", "axial"),
        P(None, None, None, "pitch", "span", "axial"),
        P(None, "pitch", "span", "axial"),
        P("pitch", "span", "axial"),
        P("pitch", "span", "axial"),
        P(),
    )
    return jax.shard_map(
        body,
        mesh=mesh,
        in_specs=placed,
        out_specs=(P(None, None, "pitch", "span", "axial"), P()),
        check_vma=False,
    )
```

```python
import functools

import jax
import jax.numpy as jnp
from jax import lax
from jax.experimental import pallas as pl
from jax.experimental.pallas import tpu as pltpu
from jax.sharding import PartitionSpec as P

ITERS = 2
WIDTH = 2
PAD = 8
GROUPS = 4
VMEM = pl.BlockSpec(memory_space=pltpu.VMEM)
SMEM = pl.BlockSpec(memory_space=pltpu.SMEM)
ANY = pl.BlockSpec(memory_space=pl.ANY)
VMEM_LIMIT = 4 * 1024 * 1024


def resident(values):
    return pltpu.with_memory_space_constraint(values, pltpu.VMEM)


def outside(values):
    return pltpu.with_memory_space_constraint(values, pltpu.HBM)


def kept(shape, dtype=jnp.float32):
    return pltpu.VMEM(shape, dtype)


def call(kernel, name, out_shape, in_specs, scratch_shapes=(), aliases=None, out_specs=None):
    return pl.pallas_call(
        kernel,
        out_shape=out_shape,
        in_specs=in_specs,
        out_specs=out_specs or (VMEM,) * len(out_shape),
        scratch_shapes=scratch_shapes,
        input_output_aliases=aliases or {},
        compiler_params=pltpu.CompilerParams(vmem_limit_bytes=VMEM_LIMIT),
        name=name,
    )


def lane_place(k, planes, lanes):
    per_group = (lanes // (2 * WIDTH)) // planes
    return k // per_group, (k % per_group) * planes


def lane_groups(rows, planes, lanes):
    return lane_place(rows - 1, planes, lanes)[0] + 1


def pack_faces(wide_ref, even_ref, odd_ref, axial_ref):
    rows, wide, span, lanes = wide_ref.shape
    planes = wide - 2 * WIDTH
    span_even = lax.axis_index("span") % 2 == 0
    lane = lax.broadcasted_iota(jnp.int32, (span, lanes), 1)
    packed = None
    for k in range(rows):
        group, base = lane_place(k, planes, lanes)
        for p in range(planes):
            cells = wide_ref[k, p + WIDTH]
            low = cells[:WIDTH]
            high = cells[span - WIDTH :]
            even_ref[k, p] = jnp.where(span_even, high, low)
            odd_ref[k, p] = jnp.where(span_even, low, high)
            place = base + p
            moved = pltpu.roll(cells, (2 * WIDTH * place + WIDTH) % lanes, axis=1)
            if place == 0:
                packed = moved
            else:
                packed = jnp.where(lane >= 2 * WIDTH * place, moved, packed)
        if k == rows - 1 or lane_place(k + 1, planes, lanes)[0] != group:
            axial_ref[group] = packed


def alone(axis):
    at = lax.axis_index(axis)
    count = lax.axis_size(axis)
    return jnp.logical_or(at == 0, jnp.logical_and(at == count - 1, count % 2 == 0))


class Loads:
    def __init__(self, pairs, sems, first, size):
        self.pairs = pairs
        self.sems = sems
        self.first = first
        self.size = size

    def copies(self, group):
        planes = pl.ds(self.first + group * self.size, self.size)
        return [
            pltpu.make_async_copy(
                source.at[(slice(None),) * dim + (planes,)],
                target.at[(slice(None),) * dim + (planes,)],
                self.sems.at[at, group],
            )
            for at, (source, target, dim) in enumerate(self.pairs)
        ]

    def start(self):
        for group in range(self.sems.shape[1]):
            for copy in self.copies(group):
                copy.start()

    def ready(self, p):
        @pl.when(jnp.logical_and(p >= self.first, (p - self.first) % self.size == 0))
        def _():
            for copy in self.copies((p - self.first) // self.size):
                copy.wait()

    def wait(self):
        for group in range(self.sems.shape[1]):
            for copy in self.copies(group):
                copy.wait()


def faces_kernel(guess_hbm, faces_ref, sems):
    planes = guess_hbm.shape[1]
    tail = pltpu.make_async_copy(
        guess_hbm.at[:, planes - WIDTH : planes], faces_ref.at[0], sems.at[0]
    )
    head = pltpu.make_async_copy(guess_hbm.at[:, 0:WIDTH], faces_ref.at[1], sems.at[1])
    tail.start()
    head.start()
    tail.wait()
    head.wait()


def open_kernel(
    guess_hbm,
    right_hbm,
    dissipation_hbm,
    omega_hbm,
    step_hbm,
    diag_hbm,
    wide_ref,
    even_ref,
    odd_ref,
    axial_ref,
    right_ref,
    dissipation_ref,
    omega_ref,
    step_ref,
    diag_ref,
    sems,
):
    rows, wide, span, lanes = wide_ref.shape
    planes = wide - 2 * WIDTH
    pairs = (
        (guess_hbm, wide_ref.at[:, WIDTH : WIDTH + planes]),
        (dissipation_hbm, dissipation_ref),
        (omega_hbm, omega_ref),
        (step_hbm, step_ref),
        (right_hbm, right_ref),
        (diag_hbm, diag_ref),
    )
    copies = [pltpu.make_async_copy(*pair, sems.at[at]) for at, pair in enumerate(pairs)]
    for copy in copies:
        copy.start()
    for k in range(rows):
        for p in (0, 1, wide - 2, wide - 1):
            wide_ref[k, p] = jnp.zeros((span, lanes), jnp.float32)
    copies[0].wait()
    pack_faces(wide_ref, even_ref, odd_ref, axial_ref)
    for copy in copies[1:]:
        copy.wait()


def near_loading_kernel(
    wide_ref,
    neighbour_hbm,
    diag_ref,
    right_ref,
    dissipation_ref,
    omega_ref,
    error_ref,
    lower_ref,
    upper_ref,
    spaced_ref,
    neighbour_ref,
    axial_ref,
    near_sems,
    axial_sem,
):
    planes = error_ref.shape[1]
    groups = near_sems.shape[1]
    loads = Loads([(neighbour_hbm.at[0:2], neighbour_ref, 3)], near_sems, 0, planes // groups)
    later = pltpu.make_async_copy(neighbour_hbm.at[4:6], axial_ref, axial_sem)
    loads.start()
    later.start()
    shifts = (lower_ref, upper_ref)

    def own(p, carry):
        total = own_terms(wide_ref, right_ref, dissipation_ref, omega_ref, p)
        add_blocks(total, [(diag_ref, (), WIDTH)], wide_ref, p, shifts[:2], None)
        for k, value in enumerate(total):
            error_ref[k, p] = value
        return carry

    def pitch(p, carry):
        loads.ready(p)
        total = [error_ref[k, p] for k in range(error_ref.shape[0])]
        add_blocks(
            total,
            [(neighbour_ref, (0,), WIDTH - 1), (neighbour_ref, (1,), WIDTH + 1)],
            wide_ref,
            p,
            None,
            spaced_ref,
        )
        for k, value in enumerate(total):
            error_ref[k, p] = value
        return carry

    lax.fori_loop(0, planes, own, 0)
    lax.fori_loop(0, planes, pitch, 0)
    later.wait()


def near_kernel(
    wide_ref,
    neighbour_ref,
    diag_ref,
    right_ref,
    dissipation_ref,
    omega_ref,
    error_ref,
    lower_ref,
    upper_ref,
    spaced_ref,
):
    def plane(p, carry):
        total = own_terms(wide_ref, right_ref, dissipation_ref, omega_ref, p)
        add_blocks(
            total,
            [
                (diag_ref, (), WIDTH),
                (neighbour_ref, (0,), WIDTH - 1),
                (neighbour_ref, (1,), WIDTH + 1),
            ],
            wide_ref,
            p,
            (lower_ref, upper_ref),
            spaced_ref,
        )
        for k, value in enumerate(total):
            error_ref[k, p] = value
        return carry

    lax.fori_loop(0, error_ref.shape[1], plane, 0)


def own_terms(wide_ref, right_ref, dissipation_ref, omega_ref, p):
    rows = wide_ref.shape[0]
    nv = rows // 2
    omega = omega_ref[p]
    spread = dissipation_ref[0, p]
    total = []
    for k in range(rows):
        other = wide_ref[(k + nv) % rows, p + WIDTH]
        turned = -omega * other if k < nv else omega * other
        far = wide_ref[k, p] + wide_ref[k, p + 2 * WIDTH]
        total.append((turned - right_ref[k, p]) + spread * far)
    return total


def add_blocks(total, sources, wide_ref, p, near_refs, spaced_ref):
    _, _, span, lanes = wide_ref.shape
    nv = len(total) // 2
    lane = lax.broadcasted_iota(jnp.int32, (span, lanes), 1)
    for j in range(nv):
        for blocks_ref, lead, at in sources:
            real = wide_ref[j, p + at]
            imag = wide_ref[nv + j, p + at]
            for i in range(nv):
                block = blocks_ref[lead + (i, j, p)].astype(jnp.float32)
                total[i] = total[i] + block * real
                total[nv + i] = total[nv + i] + block * imag
        for k in (j, nv + j):
            cells = wide_ref[k, p + WIDTH]
            if near_refs is not None:
                near_refs[0][k, p] = pltpu.roll(cells, 1, axis=1)
                near_refs[1][k, p] = pltpu.roll(cells, lanes - 1, axis=1)
            if spaced_ref is not None:
                low = jnp.where(lane < WIDTH, 0.0, pltpu.roll(cells, 2, axis=1))
                high = pltpu.roll(cells, lanes - 2, axis=1)
                spaced_ref[k, p] = low + jnp.where(lane >= lanes - WIDTH, 0.0, high)


def first_axial_kernel(
    error_in_ref,
    even_ref,
    odd_ref,
    lower_ref,
    upper_ref,
    spaced_ref,
    neighbour_ref,
    dissipation_ref,
    phase_ref,
    neighbour_hbm,
    error_ref,
    span_ref,
    turn_ref,
    axial_buf,
    sem,
):
    later = pltpu.make_async_copy(neighbour_hbm.at[2:4], span_ref, sem)
    later.start()
    angle = jnp.full(turn_ref.shape[1:], phase_ref[0], jnp.float32)
    cosine = jnp.cos(angle)
    sine_part = jnp.sin(angle)
    pitch_at = lax.axis_index("pitch")
    first = pitch_at == 0
    last = pitch_at == lax.axis_size("pitch") - 1
    turn_ref[0] = jnp.where(first, cosine, 1.0)
    turn_ref[1] = jnp.where(first, -sine_part, 0.0)
    turn_ref[2] = jnp.where(last, cosine, 1.0)
    turn_ref[3] = jnp.where(last, sine_part, 0.0)
    axial_sweep(
        even_ref,
        odd_ref,
        lower_ref,
        upper_ref,
        spaced_ref,
        neighbour_ref,
        dissipation_ref,
        error_ref,
        axial_buf,
    )
    later.wait()


def axial_kernel(error_in_ref, *refs):
    axial_sweep(*refs)


def axial_sweep(
    even_ref,
    odd_ref,
    lower_ref,
    upper_ref,
    spaced_ref,
    neighbour_ref,
    dissipation_ref,
    error_ref,
    axial_buf,
):
    rows, planes, span, lanes = error_ref.shape
    nv = rows // 2
    axial_even = lax.axis_index("axial") % 2 == 0
    axial_alone = alone("axial")
    lane = lax.broadcasted_iota(jnp.int32, (span, lanes), 1)
    edge = jnp.logical_or(lane < WIDTH, lane >= lanes - WIDTH)
    from_below = lane % (2 * WIDTH) >= WIDTH
    for group in range(axial_buf.shape[0]):
        at_even = even_ref[group]
        at_odd = jnp.where(axial_alone, 0.0, odd_ref[group])
        below = pltpu.roll(jnp.where(axial_even, at_odd, at_even), WIDTH, axis=1)
        above = pltpu.roll(jnp.where(axial_even, at_even, at_odd), lanes - WIDTH, axis=1)
        axial_buf[group] = jnp.where(from_below, below, above)

    def plane(p, carry):
        total = [error_ref[k, p] for k in range(rows)]
        spread = dissipation_ref[2, p]
        for j in range(nv):
            lower = []
            upper = []
            for k in (j, nv + j):
                group, base = lane_place(k, planes, lanes)
                packed = axial_buf[group]
                shift = lanes - WIDTH - 2 * WIDTH * base - 2 * WIDTH * p
                below = pltpu.roll(packed, shift - 1, axis=1)
                above = pltpu.roll(packed, shift + 1, axis=1)
                beyond = pltpu.roll(packed, shift, axis=1)
                lower.append(jnp.where(lane < 1, below, lower_ref[k, p]))
                upper.append(jnp.where(lane >= lanes - 1, above, upper_ref[k, p]))
                far = spaced_ref[k, p] + jnp.where(edge, beyond, 0.0)
                total[k] = total[k] + spread * far
            for side, moved in enumerate((lower, upper)):
                for i in range(nv):
                    block = neighbour_ref[side, i, j, p].astype(jnp.float32)
                    total[i] = total[i] + block * moved[0]
                    total[nv + i] = total[nv + i] + block * moved[1]
        for k in range(rows):
            error_ref[k, p] = total[k]
        return carry

    lax.fori_loop(0, planes, plane, 0)


def span_sweep(
    even_ref,
    odd_ref,
    neighbour_ref,
    dissipation_ref,
    step_ref,
    wide_ref,
    error_ref,
    square_ref,
    span_buf,
    count,
    plane_of,
    after=None,
):
    rows, planes, span, _ = error_ref.shape
    nv = rows // 2
    span_even = lax.axis_index("span") % 2 == 0
    span_alone = alone("span")
    square_ref[...] = jnp.zeros_like(square_ref)

    def plane(at, carry):
        p = plane_of(at)
        for k in range(rows):
            at_even = even_ref[k, p]
            at_odd = jnp.where(span_alone, 0.0, odd_ref[k, p])
            span_buf[k, PAD - WIDTH : PAD] = jnp.where(span_even, at_odd, at_even)
            span_buf[k, PAD : PAD + span] = wide_ref[k, p + WIDTH]
            span_buf[k, PAD + span : PAD + span + WIDTH] = jnp.where(span_even, at_even, at_odd)

        def moved(k, by):
            return span_buf[k, PAD + by : PAD + by + span]

        spread = dissipation_ref[1, p]
        total = [
            error_ref[k, p] + spread * (moved(k, -WIDTH) + moved(k, WIDTH)) for k in range(rows)
        ]
        for j in range(nv):
            for side, by in enumerate((-1, 1)):
                real = moved(j, by)
                imag = moved(nv + j, by)
                for i in range(nv):
                    block = neighbour_ref[side, i, j, p].astype(jnp.float32)
                    total[i] = total[i] + block * real
                    total[nv + i] = total[nv + i] + block * imag
        step = step_ref[p]
        square = None
        for k in range(rows):
            error = total[k]
            error_ref[k, p] = error
            wide_ref[k, p + WIDTH] = wide_ref[k, p + WIDTH] - step * error
            square = error * error if square is None else square + error * error
        inner = jnp.logical_and(p >= WIDTH, p < planes - WIDTH)
        square_ref[...] += jnp.where(inner, square, 0.0)
        if after is not None:
            after(at)
        return carry

    lax.fori_loop(0, count, plane, 0)


def last_span_kernel(wide_in_ref, error_in_ref, *refs):
    planes = error_in_ref.shape[1]
    *args, wide_ref, error_ref, square_ref, out_ref, span_buf, sem = refs
    inner = planes - 2 * WIDTH
    copy = pltpu.make_async_copy(
        wide_ref.at[:, 2 * WIDTH : planes], out_ref.at[:, WIDTH : planes - WIDTH], sem
    )

    def plane_of(at):
        rim = at - inner
        return jnp.where(
            rim < 0, at + WIDTH, jnp.where(rim < WIDTH, rim, rim + planes - 2 * WIDTH)
        )

    def after(at):
        @pl.when(at == inner - 1)
        def _():
            copy.start()

    span_sweep(*args, wide_ref, error_ref, square_ref, span_buf, planes, plane_of, after)
    copy.wait()


def span_rim_kernel(wide_in_ref, error_in_ref, *refs):
    planes = error_in_ref.shape[1]
    span_sweep(
        *refs,
        2 * WIDTH,
        lambda at: jnp.where(at < WIDTH, at, at + planes - 2 * WIDTH),
    )


def span_core_kernel(
    wide_in_ref,
    error_in_ref,
    even_ref,
    odd_ref,
    neighbour_ref,
    dissipation_ref,
    step_ref,
    wide_ref,
    error_ref,
    square_ref,
    even_face_ref,
    odd_face_ref,
    axial_face_ref,
    span_buf,
):
    planes = error_ref.shape[1]
    span_sweep(
        even_ref,
        odd_ref,
        neighbour_ref,
        dissipation_ref,
        step_ref,
        wide_ref,
        error_ref,
        square_ref,
        span_buf,
        planes - 2 * WIDTH,
        lambda at: at + WIDTH,
    )
    pack_faces(wide_ref, even_face_ref, odd_face_ref, axial_face_ref)


def pitch_terms(halo_ref, turn_ref, neighbour_ref, dissipation_ref, error_ref, store):
    rows, planes, span, lanes = error_ref.shape
    nv = rows // 2
    for side in range(2):
        cosine = turn_ref[2 * side]
        sine_part = turn_ref[2 * side + 1]
        near_at, far_at = (1, 0) if side == 0 else (0, 1)
        edge, inside = (0, 1) if side == 0 else (planes - 1, planes - 2)

        def turned(j, at):
            real = halo_ref[side, j, at]
            imag = halo_ref[side, nv + j, at]
            return (cosine * real - sine_part * imag, sine_part * real + cosine * imag)

        total = [None] * rows

        def add(k, value):
            total[k] = value if total[k] is None else total[k] + value

        spread_edge = dissipation_ref[0, edge]
        spread_inside = dissipation_ref[0, inside]
        for j in range(nv):
            near = turned(j, near_at)
            far = turned(j, far_at)
            for c in range(2):
                k = c * nv + j
                add(k, spread_edge * far[c])
                store(k, inside, spread_inside * near[c])
            for i in range(nv):
                block = neighbour_ref[side, i, j, edge].astype(jnp.float32)
                for c in range(2):
                    add(c * nv + i, block * near[c])
        for k in range(rows):
            store(k, edge, total[k])


def rim_kernel(
    wide_in_ref,
    halo_ref,
    turn_ref,
    neighbour_ref,
    dissipation_ref,
    step_ref,
    error_ref,
    square_in_ref,
    wide_ref,
    faces_ref,
    square_ref,
):
    planes = error_ref.shape[1]
    square_ref[...] = square_in_ref[...]

    def store(k, p, change):
        value = wide_ref[k, p + WIDTH] - step_ref[p] * change
        wide_ref[k, p + WIDTH] = value
        if p < WIDTH:
            faces_ref[1, k, p] = value
        else:
            faces_ref[0, k, p - (planes - WIDTH)] = value
        error = error_ref[k, p] + change
        square_ref[...] += error * error

    pitch_terms(halo_ref, turn_ref, neighbour_ref, dissipation_ref, error_ref, store)


def last_kernel(
    wide_ref,
    halo_ref,
    turn_ref,
    neighbour_ref,
    dissipation_ref,
    step_ref,
    error_ref,
    square_in_ref,
    rim_square_ref,
    core_square_ref,
    rim_ref,
    share_ref,
    square_buf,
):
    planes = error_ref.shape[1]
    lanes = share_ref.shape[2]
    square_buf[...] = square_in_ref[...]

    def store(k, p, change):
        at = p if p < WIDTH else p - (planes - 2 * WIDTH)
        rim_ref[k, at] = wide_ref[k, p + WIDTH] - step_ref[p] * change
        error = error_ref[k, p] + change
        square_buf[...] += error * error

    pitch_terms(halo_ref, turn_ref, neighbour_ref, dissipation_ref, error_ref, store)
    lane = lax.broadcasted_iota(jnp.int32, (1, lanes), 1)
    first = jnp.sum(rim_square_ref[...] + core_square_ref[...], axis=0, keepdims=True)
    second = jnp.sum(square_buf[...], axis=0, keepdims=True)
    half = lanes // 2
    folded = jnp.where(
        lane < half,
        first + pltpu.roll(first, half, axis=1),
        second + pltpu.roll(second, half, axis=1),
    )
    share_ref[...] = jnp.broadcast_to(folded[None], share_ref.shape)


def close_kernel(cell_count, out_in_ref, rim_ref, share_ref, out_ref, norm_ref, norm_buf, sems):
    planes = out_ref.shape[1]
    lanes = share_ref.shape[2]
    copies = [
        pltpu.make_async_copy(rim_ref.at[:, 0:WIDTH], out_ref.at[:, 0:WIDTH], sems.at[0]),
        pltpu.make_async_copy(
            rim_ref.at[:, WIDTH : 2 * WIDTH], out_ref.at[:, planes - WIDTH : planes], sems.at[1]
        ),
    ]
    for copy in copies:
        copy.start()
    lane = lax.broadcasted_iota(jnp.int32, (1, lanes), 1)
    row = jnp.sum(share_ref[...], axis=0)
    first = jnp.sum(jnp.where(lane < lanes // 2, row, 0.0), axis=1, keepdims=True)
    second = jnp.sum(jnp.where(lane < lanes // 2, 0.0, row), axis=1, keepdims=True)
    norms = jnp.sqrt(jnp.where(lane == 0, first, second) / cell_count)
    norm_ref[...] = norms[0, 0:ITERS]
    for copy in copies:
        copy.wait()


def body(
    guess, right_side, diag_block, neighbour_blocks, dissipation, omega_volume, pseudo_step, phase
):
    parts, nv, planes, span, lanes = guess.shape
    rows = parts * nv
    pitch_count = lax.axis_size("pitch")
    devices = pitch_count * lax.axis_size("span") * lax.axis_size("axial")
    wide = (rows, planes + 2 * WIDTH, span, lanes)
    block = (rows, planes, span, lanes)
    tile = (span, lanes)
    face_shapes = (
        kept((2, rows, WIDTH, span, lanes)),
        kept((rows, planes, WIDTH, lanes)),
        kept((rows, planes, WIDTH, lanes)),
        kept((lane_groups(rows, planes, lanes), span, lanes)),
    )
    groups = GROUPS if planes % GROUPS == 0 else 1
    dma = pltpu.SemaphoreType.DMA

    def exchange_pitch(faces):
        up = [(i, (i + 1) % pitch_count) for i in range(pitch_count)]
        down = [(j, i) for i, j in up]
        if sorted(up) == sorted(down):
            return lax.ppermute(faces, "pitch", up)
        return jnp.stack(
            [lax.ppermute(faces[0], "pitch", up), lax.ppermute(faces[1], "pitch", down)]
        )

    span_count = lax.axis_size("span")
    axial_count = lax.axis_size("axial")

    def span_swap(values, start):
        partner = {}
        for i in range(start, span_count - 1, 2):
            partner.update({i: i + 1, i + 1: i})
        pairs = []
        for i in range(span_count):
            for j in range(axial_count):
                if i in partner:
                    pairs.append((i * axial_count + j, partner[i] * axial_count + j))
                elif axial_count % 2 == 0:
                    pairs.append((i * axial_count + j, i * axial_count + (j ^ 1)))
        return resident(lax.ppermute(values, ("span", "axial"), pairs))

    def axial_swap(values, start):
        pairs = [(i, i + 1) for i in range(start, axial_count - 1, 2)]
        if start == 1 and axial_count % 2 == 0:
            pairs.append((0, axial_count - 1))
        return resident(lax.ppermute(values, "axial", pairs + [(j, i) for i, j in pairs]))

    def exchange_rest(even, odd, axial):
        return (
            span_swap(even, 0),
            span_swap(odd, 1),
            axial_swap(axial, 0),
            axial_swap(axial, 1),
        )

    neighbour_blocks = outside(neighbour_blocks)
    sources = (right_side.reshape(block), dissipation, omega_volume, pseudo_step, diag_block)
    guess = outside(guess.reshape(block))
    (faces,) = call(faces_kernel, "pitch_faces", face_shapes[:1], [ANY], [dma((2,))])(guess)
    state, even, odd, axial, right, dissipation, omega, step, diag = call(
        open_kernel,
        "open",
        (kept(wide),)
        + face_shapes[1:]
        + tuple(kept(c.shape, c.dtype) for c in sources),
        [ANY] * 6,
        [dma((6,))],
    )(guess, *[outside(c) for c in sources])

    axial_buf = [pltpu.VMEM(face_shapes[3].shape, jnp.float32)]
    span_buf = [pltpu.VMEM((rows, span + 2 * PAD, lanes), jnp.float32)]
    pair = kept((2,) + neighbour_blocks.shape[1:], neighbour_blocks.dtype)
    sweep = (kept(wide), kept(block), kept(tile))
    for iteration in range(ITERS):
        halo = resident(exchange_pitch(faces))
        span_even, span_odd, axial_even, axial_odd = exchange_rest(even, odd, axial)
        if iteration == 0:
            error, *shifts, near_blocks, axial_blocks = call(
                near_loading_kernel,
                "first_near",
                (kept(block),) * 4 + (pair, pair),
                [VMEM, ANY] + [VMEM] * 4,
                [dma((1, groups)), dma],
            )(state, neighbour_blocks, diag, right, dissipation, omega)
            error, span_blocks, turn = call(
                first_axial_kernel,
                "first_axial",
                (kept(block), pair, kept((4,) + tile)),
                [VMEM] * 8 + [SMEM, ANY],
                axial_buf + [dma],
                {0: 0},
            )(
                error,
                axial_even,
                axial_odd,
                *shifts,
                axial_blocks,
                dissipation,
                phase,
                neighbour_blocks,
            )
        else:
            error, *shifts = call(near_kernel, "near", (kept(block),) * 4, [VMEM] * 6)(
                state, near_blocks, diag, right, dissipation, omega
            )
            (error,) = call(axial_kernel, "axial", (kept(block),), [VMEM] * 8, axial_buf, {0: 0})(
                error, axial_even, axial_odd, *shifts, axial_blocks, dissipation
            )
        rest = (span_even, span_odd, span_blocks, dissipation, step)
        terms = (halo, turn, near_blocks, dissipation, step)
        if iteration < ITERS - 1:
            state, error, square = call(
                span_rim_kernel, "span_rim", sweep, [VMEM] * 7, span_buf, {0: 0, 1: 1}
            )(state, error, *rest)
            state, faces, rim_square = call(
                rim_kernel,
                "pitch_terms",
                (kept(wide), face_shapes[0], kept(tile)),
                [VMEM] * 8,
                aliases={0: 0},
            )(state, *terms, error, square)
            state, _, core_square, even, odd, axial = call(
                span_core_kernel,
                "span_core",
                sweep + face_shapes[1:],
                [VMEM] * 7,
                span_buf,
                {0: 0, 1: 1},
            )(state, error, *rest)
        else:
            state, error, square, out = call(
                last_span_kernel,
                "span",
                sweep + (jax.ShapeDtypeStruct(block, jnp.float32),),
                [VMEM] * 7,
                span_buf + [dma],
                {0: 0, 1: 1},
                (VMEM,) * 3 + (ANY,),
            )(state, error, *rest)
            rim, share = call(
                last_kernel,
                "last_pitch_terms",
                (kept((rows, 2 * WIDTH, span, lanes)), kept((devices, 1, lanes))),
                [VMEM] * 10,
                [pltpu.VMEM(tile, jnp.float32)],
            )(state, *terms, error, square, rim_square, core_square)
    shares = lax.all_to_all(share, ("pitch", "span", "axial"), 0, 0, tiled=True)
    cell_count = float(rows * planes * span * lanes * devices)
    out, norms = call(
        functools.partial(close_kernel, cell_count),
        "close",
        (
            jax.ShapeDtypeStruct(block, jnp.float32),
            jax.ShapeDtypeStruct((ITERS,), jnp.float32),
        ),
        [ANY, VMEM, VMEM],
        [pltpu.VMEM((1, lanes), jnp.float32), dma((3,))],
        {0: 0},
        (ANY, VMEM),
    )(out, rim, resident(shares))
    return (out.reshape(parts, nv, planes, span, lanes), norms)


def solution(mesh):
    placed = (
        P(None, None, "pitch", "span", "axial"),
        P(None, None, "pitch", "span", "axial"),
        P(None, None, "pitch", "span", "axial"),
        P(None, None, None, "pitch", "span", "axial"),
        P(None, "pitch", "span", "axial"),
        P("pitch", "span", "axial"),
        P("pitch", "span", "axial"),
        P(),
    )
    return jax.shard_map(
        body,
        mesh=mesh,
        in_specs=placed,
        out_specs=(P(None, None, "pitch", "span", "axial"), P()),
        check_vma=False,
    )
```

```python
import functools

import jax
import jax.numpy as jnp
from jax import lax
from jax.experimental import pallas as pl
from jax.experimental.pallas import tpu as pltpu
from jax.sharding import PartitionSpec as P

ITERS = 2
WIDTH = 2
PAD = 8
GROUPS = 4
VMEM = pl.BlockSpec(memory_space=pltpu.VMEM)
SMEM = pl.BlockSpec(memory_space=pltpu.SMEM)
ANY = pl.BlockSpec(memory_space=pl.ANY)
VMEM_LIMIT = 4 * 1024 * 1024


def resident(values):
    return pltpu.with_memory_space_constraint(values, pltpu.VMEM)


def outside(values):
    return pltpu.with_memory_space_constraint(values, pltpu.HBM)


def kept(shape, dtype=jnp.float32):
    return pltpu.VMEM(shape, dtype)


def call(kernel, name, out_shape, in_specs, scratch_shapes=(), aliases=None, out_specs=None):
    return pl.pallas_call(
        kernel,
        out_shape=out_shape,
        in_specs=in_specs,
        out_specs=out_specs or (VMEM,) * len(out_shape),
        scratch_shapes=scratch_shapes,
        input_output_aliases=aliases or {},
        compiler_params=pltpu.CompilerParams(vmem_limit_bytes=VMEM_LIMIT),
        name=name,
    )


def lane_place(k, planes, lanes):
    per_group = (lanes // (2 * WIDTH)) // planes
    return k // per_group, (k % per_group) * planes


def lane_groups(rows, planes, lanes):
    return lane_place(rows - 1, planes, lanes)[0] + 1


def pack_faces(wide_ref, even_ref, odd_ref, axial_ref):
    rows, wide, span, lanes = wide_ref.shape
    planes = wide - 2 * WIDTH
    span_even = lax.axis_index("span") % 2 == 0
    lane = lax.broadcasted_iota(jnp.int32, (span, lanes), 1)
    packed = None
    for k in range(rows):
        group, base = lane_place(k, planes, lanes)
        for p in range(planes):
            cells = wide_ref[k, p + WIDTH]
            low = cells[:WIDTH]
            high = cells[span - WIDTH :]
            even_ref[k, p] = jnp.where(span_even, high, low)
            odd_ref[k, p] = jnp.where(span_even, low, high)
            place = base + p
            moved = pltpu.roll(cells, (2 * WIDTH * place + WIDTH) % lanes, axis=1)
            if place == 0:
                packed = moved
            else:
                packed = jnp.where(lane >= 2 * WIDTH * place, moved, packed)
        if k == rows - 1 or lane_place(k + 1, planes, lanes)[0] != group:
            axial_ref[group] = packed


def alone(axis):
    at = lax.axis_index(axis)
    count = lax.axis_size(axis)
    return jnp.logical_or(at == 0, jnp.logical_and(at == count - 1, count % 2 == 0))


class Loads:
    def __init__(self, pairs, sems, first, size):
        self.pairs = pairs
        self.sems = sems
        self.first = first
        self.size = size

    def copies(self, group):
        planes = pl.ds(self.first + group * self.size, self.size)
        return [
            pltpu.make_async_copy(
                source.at[(slice(None),) * dim + (planes,)],
                target.at[(slice(None),) * dim + (planes,)],
                self.sems.at[at, group],
            )
            for at, (source, target, dim) in enumerate(self.pairs)
        ]

    def start(self):
        for group in range(self.sems.shape[1]):
            for copy in self.copies(group):
                copy.start()

    def ready(self, p):
        @pl.when(jnp.logical_and(p >= self.first, (p - self.first) % self.size == 0))
        def _():
            for copy in self.copies((p - self.first) // self.size):
                copy.wait()

    def wait(self):
        for group in range(self.sems.shape[1]):
            for copy in self.copies(group):
                copy.wait()


def faces_kernel(guess_hbm, faces_ref, sems):
    planes = guess_hbm.shape[1]
    tail = pltpu.make_async_copy(
        guess_hbm.at[:, planes - WIDTH : planes], faces_ref.at[0], sems.at[0]
    )
    head = pltpu.make_async_copy(guess_hbm.at[:, 0:WIDTH], faces_ref.at[1], sems.at[1])
    tail.start()
    head.start()
    tail.wait()
    head.wait()


def open_kernel(
    guess_hbm,
    right_hbm,
    dissipation_hbm,
    omega_hbm,
    step_hbm,
    diag_hbm,
    wide_ref,
    even_ref,
    odd_ref,
    axial_ref,
    right_ref,
    dissipation_ref,
    omega_ref,
    step_ref,
    diag_ref,
    sems,
):
    rows, wide, span, lanes = wide_ref.shape
    planes = wide - 2 * WIDTH
    pairs = (
        (guess_hbm, wide_ref.at[:, WIDTH : WIDTH + planes]),
        (dissipation_hbm, dissipation_ref),
        (omega_hbm, omega_ref),
        (step_hbm, step_ref),
        (right_hbm, right_ref),
        (diag_hbm, diag_ref),
    )
    copies = [pltpu.make_async_copy(*pair, sems.at[at]) for at, pair in enumerate(pairs)]
    for copy in copies:
        copy.start()
    for k in range(rows):
        for p in (0, 1, wide - 2, wide - 1):
            wide_ref[k, p] = jnp.zeros((span, lanes), jnp.float32)
    copies[0].wait()
    pack_faces(wide_ref, even_ref, odd_ref, axial_ref)
    for copy in copies[1:]:
        copy.wait()


def near_loading_kernel(
    wide_ref,
    neighbour_hbm,
    diag_ref,
    right_ref,
    dissipation_ref,
    omega_ref,
    error_ref,
    lower_ref,
    upper_ref,
    spaced_ref,
    neighbour_ref,
    axial_ref,
    near_sems,
    axial_sem,
):
    planes = error_ref.shape[1]
    groups = near_sems.shape[1]
    loads = Loads([(neighbour_hbm.at[0:2], neighbour_ref, 3)], near_sems, 0, planes // groups)
    later = pltpu.make_async_copy(neighbour_hbm.at[4:6], axial_ref, axial_sem)
    loads.start()
    later.start()
    shifts = (lower_ref, upper_ref)

    def own(p, carry):
        total = own_terms(wide_ref, right_ref, dissipation_ref, omega_ref, p)
        add_blocks(total, [(diag_ref, (), WIDTH)], wide_ref, p, shifts[:2], None)
        for k, value in enumerate(total):
            error_ref[k, p] = value
        return carry

    def pitch(p, carry):
        loads.ready(p)
        total = [error_ref[k, p] for k in range(error_ref.shape[0])]
        add_blocks(
            total,
            [(neighbour_ref, (0,), WIDTH - 1), (neighbour_ref, (1,), WIDTH + 1)],
            wide_ref,
            p,
            None,
            spaced_ref,
        )
        for k, value in enumerate(total):
            error_ref[k, p] = value
        return carry

    lax.fori_loop(0, planes, own, 0)
    lax.fori_loop(0, planes, pitch, 0)
    later.wait()


def near_kernel(
    wide_ref,
    neighbour_ref,
    diag_ref,
    right_ref,
    dissipation_ref,
    omega_ref,
    error_ref,
    lower_ref,
    upper_ref,
    spaced_ref,
):
    def plane(p, carry):
        total = own_terms(wide_ref, right_ref, dissipation_ref, omega_ref, p)
        add_blocks(
            total,
            [
                (diag_ref, (), WIDTH),
                (neighbour_ref, (0,), WIDTH - 1),
                (neighbour_ref, (1,), WIDTH + 1),
            ],
            wide_ref,
            p,
            (lower_ref, upper_ref),
            spaced_ref,
        )
        for k, value in enumerate(total):
            error_ref[k, p] = value
        return carry

    lax.fori_loop(0, error_ref.shape[1], plane, 0)


def own_terms(wide_ref, right_ref, dissipation_ref, omega_ref, p):
    rows = wide_ref.shape[0]
    nv = rows // 2
    omega = omega_ref[p]
    spread = dissipation_ref[0, p]
    total = []
    for k in range(rows):
        other = wide_ref[(k + nv) % rows, p + WIDTH]
        turned = -omega * other if k < nv else omega * other
        far = wide_ref[k, p] + wide_ref[k, p + 2 * WIDTH]
        total.append((turned - right_ref[k, p]) + spread * far)
    return total


def add_blocks(total, sources, wide_ref, p, near_refs, spaced_ref):
    _, _, span, lanes = wide_ref.shape
    nv = len(total) // 2
    lane = lax.broadcasted_iota(jnp.int32, (span, lanes), 1)
    for j in range(nv):
        for blocks_ref, lead, at in sources:
            real = wide_ref[j, p + at]
            imag = wide_ref[nv + j, p + at]
            for i in range(nv):
                block = blocks_ref[lead + (i, j, p)].astype(jnp.float32)
                total[i] = total[i] + block * real
                total[nv + i] = total[nv + i] + block * imag
        for k in (j, nv + j):
            cells = wide_ref[k, p + WIDTH]
            if near_refs is not None:
                near_refs[0][k, p] = pltpu.roll(cells, 1, axis=1)
                near_refs[1][k, p] = pltpu.roll(cells, lanes - 1, axis=1)
            if spaced_ref is not None:
                low = jnp.where(lane < WIDTH, 0.0, pltpu.roll(cells, 2, axis=1))
                high = pltpu.roll(cells, lanes - 2, axis=1)
                spaced_ref[k, p] = low + jnp.where(lane >= lanes - WIDTH, 0.0, high)


def first_axial_kernel(
    error_in_ref,
    even_ref,
    odd_ref,
    lower_ref,
    upper_ref,
    spaced_ref,
    neighbour_ref,
    dissipation_ref,
    phase_ref,
    neighbour_hbm,
    error_ref,
    span_ref,
    turn_ref,
    axial_buf,
    sem,
):
    later = pltpu.make_async_copy(neighbour_hbm.at[2:4], span_ref, sem)
    later.start()
    angle = jnp.full(turn_ref.shape[1:], phase_ref[0], jnp.float32)
    cosine = jnp.cos(angle)
    sine_part = jnp.sin(angle)
    pitch_at = lax.axis_index("pitch")
    first = pitch_at == 0
    last = pitch_at == lax.axis_size("pitch") - 1
    turn_ref[0] = jnp.where(first, cosine, 1.0)
    turn_ref[1] = jnp.where(first, -sine_part, 0.0)
    turn_ref[2] = jnp.where(last, cosine, 1.0)
    turn_ref[3] = jnp.where(last, sine_part, 0.0)
    axial_sweep(
        even_ref,
        odd_ref,
        lower_ref,
        upper_ref,
        spaced_ref,
        neighbour_ref,
        dissipation_ref,
        error_ref,
        axial_buf,
    )
    later.wait()


def axial_kernel(error_in_ref, *refs):
    axial_sweep(*refs)


def axial_sweep(
    even_ref,
    odd_ref,
    lower_ref,
    upper_ref,
    spaced_ref,
    neighbour_ref,
    dissipation_ref,
    error_ref,
    axial_buf,
):
    rows, planes, span, lanes = error_ref.shape
    nv = rows // 2
    axial_even = lax.axis_index("axial") % 2 == 0
    axial_alone = alone("axial")
    lane = lax.broadcasted_iota(jnp.int32, (span, lanes), 1)
    edge = jnp.logical_or(lane < WIDTH, lane >= lanes - WIDTH)
    from_below = lane % (2 * WIDTH) >= WIDTH
    for group in range(axial_buf.shape[0]):
        at_even = even_ref[group]
        at_odd = jnp.where(axial_alone, 0.0, odd_ref[group])
        below = pltpu.roll(jnp.where(axial_even, at_odd, at_even), WIDTH, axis=1)
        above = pltpu.roll(jnp.where(axial_even, at_even, at_odd), lanes - WIDTH, axis=1)
        axial_buf[group] = jnp.where(from_below, below, above)

    def plane(p, carry):
        total = [error_ref[k, p] for k in range(rows)]
        spread = dissipation_ref[2, p]
        for j in range(nv):
            lower = []
            upper = []
            for k in (j, nv + j):
                group, base = lane_place(k, planes, lanes)
                packed = axial_buf[group]
                shift = lanes - WIDTH - 2 * WIDTH * base - 2 * WIDTH * p
                below = pltpu.roll(packed, shift - 1, axis=1)
                above = pltpu.roll(packed, shift + 1, axis=1)
                beyond = pltpu.roll(packed, shift, axis=1)
                lower.append(jnp.where(lane < 1, below, lower_ref[k, p]))
                upper.append(jnp.where(lane >= lanes - 1, above, upper_ref[k, p]))
                far = spaced_ref[k, p] + jnp.where(edge, beyond, 0.0)
                total[k] = total[k] + spread * far
            for side, moved in enumerate((lower, upper)):
                for i in range(nv):
                    block = neighbour_ref[side, i, j, p].astype(jnp.float32)
                    total[i] = total[i] + block * moved[0]
                    total[nv + i] = total[nv + i] + block * moved[1]
        for k in range(rows):
            error_ref[k, p] = total[k]
        return carry

    lax.fori_loop(0, planes, plane, 0)


def span_sweep(
    odd_ref,
    even_ref,
    neighbour_ref,
    dissipation_ref,
    step_ref,
    wide_ref,
    error_ref,
    square_ref,
    span_buf,
    count,
    plane_of,
    after=None,
):
    rows, planes, span, _ = error_ref.shape
    nv = rows // 2
    span_even = lax.axis_index("span") % 2 == 0
    span_alone = alone("span")
    square_ref[...] = jnp.zeros_like(square_ref)

    def plane(at, carry):
        p = plane_of(at)
        for k in range(rows):
            at_even = even_ref[k, p]
            at_odd = jnp.where(span_alone, 0.0, odd_ref[k, p])
            span_buf[k, PAD - WIDTH : PAD] = jnp.where(span_even, at_odd, at_even)
            span_buf[k, PAD : PAD + span] = wide_ref[k, p + WIDTH]
            span_buf[k, PAD + span : PAD + span + WIDTH] = jnp.where(span_even, at_even, at_odd)

        def moved(k, by):
            return span_buf[k, PAD + by : PAD + by + span]

        spread = dissipation_ref[1, p]
        total = [
            error_ref[k, p] + spread * (moved(k, -WIDTH) + moved(k, WIDTH)) for k in range(rows)
        ]
        for j in range(nv):
            for side, by in enumerate((-1, 1)):
                real = moved(j, by)
                imag = moved(nv + j, by)
                for i in range(nv):
                    block = neighbour_ref[side, i, j, p].astype(jnp.float32)
                    total[i] = total[i] + block * real
                    total[nv + i] = total[nv + i] + block * imag
        step = step_ref[p]
        square = None
        for k in range(rows):
            error = total[k]
            error_ref[k, p] = error
            wide_ref[k, p + WIDTH] = wide_ref[k, p + WIDTH] - step * error
            square = error * error if square is None else square + error * error
        inner = jnp.logical_and(p >= WIDTH, p < planes - WIDTH)
        square_ref[...] += jnp.where(inner, square, 0.0)
        if after is not None:
            after(at)
        return carry

    lax.fori_loop(0, count, plane, 0)


def last_span_kernel(wide_in_ref, error_in_ref, *refs):
    planes = error_in_ref.shape[1]
    *args, wide_ref, error_ref, square_ref, out_ref, span_buf, sem = refs
    inner = planes - 2 * WIDTH
    copy = pltpu.make_async_copy(
        wide_ref.at[:, 2 * WIDTH : planes], out_ref.at[:, WIDTH : planes - WIDTH], sem
    )

    def plane_of(at):
        rim = at - inner
        return jnp.where(
            rim < 0, at + WIDTH, jnp.where(rim < WIDTH, rim, rim + planes - 2 * WIDTH)
        )

    def after(at):
        @pl.when(at == inner - 1)
        def _():
            copy.start()

    span_sweep(*args, wide_ref, error_ref, square_ref, span_buf, planes, plane_of, after)
    copy.wait()


def span_rim_kernel(wide_in_ref, error_in_ref, *refs):
    planes = error_in_ref.shape[1]
    span_sweep(
        *refs,
        2 * WIDTH,
        lambda at: jnp.where(at < WIDTH, at, at + planes - 2 * WIDTH),
    )


def span_core_kernel(
    wide_in_ref,
    error_in_ref,
    odd_ref,
    even_ref,
    neighbour_ref,
    dissipation_ref,
    step_ref,
    wide_ref,
    error_ref,
    square_ref,
    even_face_ref,
    odd_face_ref,
    axial_face_ref,
    span_buf,
):
    planes = error_ref.shape[1]
    span_sweep(
        odd_ref,
        even_ref,
        neighbour_ref,
        dissipation_ref,
        step_ref,
        wide_ref,
        error_ref,
        square_ref,
        span_buf,
        planes - 2 * WIDTH,
        lambda at: at + WIDTH,
    )
    pack_faces(wide_ref, even_face_ref, odd_face_ref, axial_face_ref)


def pitch_terms(halo_ref, turn_ref, neighbour_ref, dissipation_ref, error_ref, store):
    rows, planes, span, lanes = error_ref.shape
    nv = rows // 2
    for side in range(2):
        cosine = turn_ref[2 * side]
        sine_part = turn_ref[2 * side + 1]
        near_at, far_at = (1, 0) if side == 0 else (0, 1)
        edge, inside = (0, 1) if side == 0 else (planes - 1, planes - 2)

        def turned(j, at):
            real = halo_ref[side, j, at]
            imag = halo_ref[side, nv + j, at]
            return (cosine * real - sine_part * imag, sine_part * real + cosine * imag)

        total = [None] * rows

        def add(k, value):
            total[k] = value if total[k] is None else total[k] + value

        spread_edge = dissipation_ref[0, edge]
        spread_inside = dissipation_ref[0, inside]
        for j in range(nv):
            near = turned(j, near_at)
            far = turned(j, far_at)
            for c in range(2):
                k = c * nv + j
                add(k, spread_edge * far[c])
                store(k, inside, spread_inside * near[c])
            for i in range(nv):
                block = neighbour_ref[side, i, j, edge].astype(jnp.float32)
                for c in range(2):
                    add(c * nv + i, block * near[c])
        for k in range(rows):
            store(k, edge, total[k])


def rim_kernel(
    wide_in_ref,
    halo_ref,
    turn_ref,
    neighbour_ref,
    dissipation_ref,
    step_ref,
    error_ref,
    square_in_ref,
    wide_ref,
    faces_ref,
    square_ref,
):
    planes = error_ref.shape[1]
    square_ref[...] = square_in_ref[...]

    def store(k, p, change):
        value = wide_ref[k, p + WIDTH] - step_ref[p] * change
        wide_ref[k, p + WIDTH] = value
        if p < WIDTH:
            faces_ref[1, k, p] = value
        else:
            faces_ref[0, k, p - (planes - WIDTH)] = value
        error = error_ref[k, p] + change
        square_ref[...] += error * error

    pitch_terms(halo_ref, turn_ref, neighbour_ref, dissipation_ref, error_ref, store)


def last_kernel(
    wide_ref,
    halo_ref,
    turn_ref,
    neighbour_ref,
    dissipation_ref,
    step_ref,
    error_ref,
    square_in_ref,
    rim_square_ref,
    core_square_ref,
    rim_ref,
    share_ref,
    square_buf,
):
    planes = error_ref.shape[1]
    lanes = share_ref.shape[2]
    square_buf[...] = square_in_ref[...]

    def store(k, p, change):
        at = p if p < WIDTH else p - (planes - 2 * WIDTH)
        rim_ref[k, at] = wide_ref[k, p + WIDTH] - step_ref[p] * change
        error = error_ref[k, p] + change
        square_buf[...] += error * error

    pitch_terms(halo_ref, turn_ref, neighbour_ref, dissipation_ref, error_ref, store)
    lane = lax.broadcasted_iota(jnp.int32, (1, lanes), 1)
    first = jnp.sum(rim_square_ref[...] + core_square_ref[...], axis=0, keepdims=True)
    second = jnp.sum(square_buf[...], axis=0, keepdims=True)
    half = lanes // 2
    folded = jnp.where(
        lane < half,
        first + pltpu.roll(first, half, axis=1),
        second + pltpu.roll(second, half, axis=1),
    )
    share_ref[...] = jnp.broadcast_to(folded[None], share_ref.shape)


def close_kernel(cell_count, out_in_ref, rim_ref, share_ref, out_ref, norm_ref, norm_buf, sems):
    planes = out_ref.shape[1]
    lanes = share_ref.shape[2]
    copies = [
        pltpu.make_async_copy(rim_ref.at[:, 0:WIDTH], out_ref.at[:, 0:WIDTH], sems.at[0]),
        pltpu.make_async_copy(
            rim_ref.at[:, WIDTH : 2 * WIDTH], out_ref.at[:, planes - WIDTH : planes], sems.at[1]
        ),
    ]
    for copy in copies:
        copy.start()
    lane = lax.broadcasted_iota(jnp.int32, (1, lanes), 1)
    row = jnp.sum(share_ref[...], axis=0)
    first = jnp.sum(jnp.where(lane < lanes // 2, row, 0.0), axis=1, keepdims=True)
    second = jnp.sum(jnp.where(lane < lanes // 2, 0.0, row), axis=1, keepdims=True)
    norms = jnp.sqrt(jnp.where(lane == 0, first, second) / cell_count)
    norm_ref[...] = norms[0, 0:ITERS]
    for copy in copies:
        copy.wait()


def body(
    guess, right_side, diag_block, neighbour_blocks, dissipation, omega_volume, pseudo_step, phase
):
    parts, nv, planes, span, lanes = guess.shape
    rows = parts * nv
    pitch_count = lax.axis_size("pitch")
    devices = pitch_count * lax.axis_size("span") * lax.axis_size("axial")
    wide = (rows, planes + 2 * WIDTH, span, lanes)
    block = (rows, planes, span, lanes)
    tile = (span, lanes)
    face_shapes = (
        kept((2, rows, WIDTH, span, lanes)),
        kept((rows, planes, WIDTH, lanes)),
        kept((rows, planes, WIDTH, lanes)),
        kept((lane_groups(rows, planes, lanes), span, lanes)),
    )
    groups = GROUPS if planes % GROUPS == 0 else 1
    dma = pltpu.SemaphoreType.DMA

    def exchange_pitch(faces):
        up = [(i, (i + 1) % pitch_count) for i in range(pitch_count)]
        down = [(j, i) for i, j in up]
        if sorted(up) == sorted(down):
            return lax.ppermute(faces, "pitch", up)
        return jnp.stack(
            [lax.ppermute(faces[0], "pitch", up), lax.ppermute(faces[1], "pitch", down)]
        )

    span_count = lax.axis_size("span")
    axial_count = lax.axis_size("axial")

    def span_swap(values, start):
        partner = {}
        for i in range(start, span_count - 1, 2):
            partner.update({i: i + 1, i + 1: i})
        pairs = []
        for i in range(span_count):
            for j in range(axial_count):
                if i in partner:
                    pairs.append((i * axial_count + j, partner[i] * axial_count + j))
                elif axial_count % 2 == 0:
                    pairs.append((i * axial_count + j, i * axial_count + (j ^ 1)))
        return resident(lax.ppermute(values, ("span", "axial"), pairs))

    def axial_swap(values, start):
        pairs = [(i, i + 1) for i in range(start, axial_count - 1, 2)]
        if start == 1 and axial_count % 2 == 0:
            pairs.append((0, axial_count - 1))
        return resident(lax.ppermute(values, "axial", pairs + [(j, i) for i, j in pairs]))

    def exchange_rest(even, odd, axial):
        return (
            span_swap(even, 0),
            span_swap(odd, 1),
            axial_swap(axial, 0),
            axial_swap(axial, 1),
        )

    neighbour_blocks = outside(neighbour_blocks)
    sources = (right_side.reshape(block), dissipation, omega_volume, pseudo_step, diag_block)
    guess = outside(guess.reshape(block))
    (faces,) = call(faces_kernel, "pitch_faces", face_shapes[:1], [ANY], [dma((2,))])(guess)
    state, even, odd, axial, right, dissipation, omega, step, diag = call(
        open_kernel,
        "open",
        (kept(wide),)
        + face_shapes[1:]
        + tuple(kept(c.shape, c.dtype) for c in sources),
        [ANY] * 6,
        [dma((6,))],
    )(guess, *[outside(c) for c in sources])

    axial_buf = [pltpu.VMEM(face_shapes[3].shape, jnp.float32)]
    span_buf = [pltpu.VMEM((rows, span + 2 * PAD, lanes), jnp.float32)]
    pair = kept((2,) + neighbour_blocks.shape[1:], neighbour_blocks.dtype)
    sweep = (kept(wide), kept(block), kept(tile))
    for iteration in range(ITERS):
        halo = resident(exchange_pitch(faces))
        span_even, span_odd, axial_even, axial_odd = exchange_rest(even, odd, axial)
        if iteration == 0:
            error, *shifts, near_blocks, axial_blocks = call(
                near_loading_kernel,
                "first_near",
                (kept(block),) * 4 + (pair, pair),
                [VMEM, ANY] + [VMEM] * 4,
                [dma((1, groups)), dma],
            )(state, neighbour_blocks, diag, right, dissipation, omega)
            error, span_blocks, turn = call(
                first_axial_kernel,
                "first_axial",
                (kept(block), pair, kept((4,) + tile)),
                [VMEM] * 8 + [SMEM, ANY],
                axial_buf + [dma],
                {0: 0},
            )(
                error,
                axial_even,
                axial_odd,
                *shifts,
                axial_blocks,
                dissipation,
                phase,
                neighbour_blocks,
            )
        else:
            error, *shifts = call(near_kernel, "near", (kept(block),) * 4, [VMEM] * 6)(
                state, near_blocks, diag, right, dissipation, omega
            )
            (error,) = call(axial_kernel, "axial", (kept(block),), [VMEM] * 8, axial_buf, {0: 0})(
                error, axial_even, axial_odd, *shifts, axial_blocks, dissipation
            )
        rest = (span_odd, span_even, span_blocks, dissipation, step)
        terms = (halo, turn, near_blocks, dissipation, step)
        if iteration < ITERS - 1:
            state, error, square = call(
                span_rim_kernel, "span_rim", sweep, [VMEM] * 7, span_buf, {0: 0, 1: 1}
            )(state, error, *rest)
            state, faces, rim_square = call(
                rim_kernel,
                "pitch_terms",
                (kept(wide), face_shapes[0], kept(tile)),
                [VMEM] * 8,
                aliases={0: 0},
            )(state, *terms, error, square)
            state, _, core_square, even, odd, axial = call(
                span_core_kernel,
                "span_core",
                sweep + face_shapes[1:],
                [VMEM] * 7,
                span_buf,
                {0: 0, 1: 1},
            )(state, error, *rest)
        else:
            state, error, square, out = call(
                last_span_kernel,
                "span",
                sweep + (jax.ShapeDtypeStruct(block, jnp.float32),),
                [VMEM] * 7,
                span_buf + [dma],
                {0: 0, 1: 1},
                (VMEM,) * 3 + (ANY,),
            )(state, error, *rest)
            rim, share = call(
                last_kernel,
                "last_pitch_terms",
                (kept((rows, 2 * WIDTH, span, lanes)), kept((devices, 1, lanes))),
                [VMEM] * 10,
                [pltpu.VMEM(tile, jnp.float32)],
            )(state, *terms, error, square, rim_square, core_square)
    shares = lax.all_to_all(share, ("pitch", "span", "axial"), 0, 0, tiled=True)
    cell_count = float(rows * planes * span * lanes * devices)
    out, norms = call(
        functools.partial(close_kernel, cell_count),
        "close",
        (
            jax.ShapeDtypeStruct(block, jnp.float32),
            jax.ShapeDtypeStruct((ITERS,), jnp.float32),
        ),
        [ANY, VMEM, VMEM],
        [pltpu.VMEM((1, lanes), jnp.float32), dma((3,))],
        {0: 0},
        (ANY, VMEM),
    )(out, rim, resident(shares))
    return (out.reshape(parts, nv, planes, span, lanes), norms)


def solution(mesh):
    placed = (
        P(None, None, "pitch", "span", "axial"),
        P(None, None, "pitch", "span", "axial"),
        P(None, None, "pitch", "span", "axial"),
        P(None, None, None, "pitch", "span", "axial"),
        P(None, "pitch", "span", "axial"),
        P("pitch", "span", "axial"),
        P("pitch", "span", "axial"),
        P(),
    )
    return jax.shard_map(
        body,
        mesh=mesh,
        in_specs=placed,
        out_specs=(P(None, None, "pitch", "span", "axial"), P()),
        check_vma=False,
    )
```

```python
import functools

import jax
import jax.numpy as jnp
from jax import lax
from jax.experimental import pallas as pl
from jax.experimental.pallas import tpu as pltpu
from jax.sharding import PartitionSpec as P

ITERS = 2
WIDTH = 2
PAD = 8
GROUPS = 4
VMEM = pl.BlockSpec(memory_space=pltpu.VMEM)
SMEM = pl.BlockSpec(memory_space=pltpu.SMEM)
ANY = pl.BlockSpec(memory_space=pl.ANY)
VMEM_LIMIT = 4 * 1024 * 1024


def resident(values):
    return pltpu.with_memory_space_constraint(values, pltpu.VMEM)


def outside(values):
    return pltpu.with_memory_space_constraint(values, pltpu.HBM)


def kept(shape, dtype=jnp.float32):
    return pltpu.VMEM(shape, dtype)


def call(kernel, name, out_shape, in_specs, scratch_shapes=(), aliases=None, out_specs=None):
    return pl.pallas_call(
        kernel,
        out_shape=out_shape,
        in_specs=in_specs,
        out_specs=out_specs or (VMEM,) * len(out_shape),
        scratch_shapes=scratch_shapes,
        input_output_aliases=aliases or {},
        compiler_params=pltpu.CompilerParams(vmem_limit_bytes=VMEM_LIMIT),
        name=name,
    )


def lane_place(k, planes, lanes):
    per_group = (lanes // (2 * WIDTH)) // planes
    return k // per_group, (k % per_group) * planes


def lane_groups(rows, planes, lanes):
    return lane_place(rows - 1, planes, lanes)[0] + 1


def pack_faces(wide_ref, even_ref, odd_ref, axial_ref):
    rows, wide, span, lanes = wide_ref.shape
    planes = wide - 2 * WIDTH
    span_even = lax.axis_index("span") % 2 == 0
    lane = lax.broadcasted_iota(jnp.int32, (span, lanes), 1)
    packed = None
    for k in range(rows):
        group, base = lane_place(k, planes, lanes)
        for p in range(planes):
            cells = wide_ref[k, p + WIDTH]
            low = cells[:WIDTH]
            high = cells[span - WIDTH :]
            even_ref[k, p] = jnp.where(span_even, high, low)
            odd_ref[k, p] = jnp.where(span_even, low, high)
            place = base + p
            moved = pltpu.roll(cells, (2 * WIDTH * place + WIDTH) % lanes, axis=1)
            if place == 0:
                packed = moved
            else:
                packed = jnp.where(lane >= 2 * WIDTH * place, moved, packed)
        if k == rows - 1 or lane_place(k + 1, planes, lanes)[0] != group:
            axial_ref[group] = packed


def alone(axis):
    at = lax.axis_index(axis)
    count = lax.axis_size(axis)
    return jnp.logical_or(at == 0, jnp.logical_and(at == count - 1, count % 2 == 0))


class Loads:
    def __init__(self, pairs, sems, first, size):
        self.pairs = pairs
        self.sems = sems
        self.first = first
        self.size = size

    def copies(self, group):
        planes = pl.ds(self.first + group * self.size, self.size)
        return [
            pltpu.make_async_copy(
                source.at[(slice(None),) * dim + (planes,)],
                target.at[(slice(None),) * dim + (planes,)],
                self.sems.at[at, group],
            )
            for at, (source, target, dim) in enumerate(self.pairs)
        ]

    def start(self):
        for group in range(self.sems.shape[1]):
            for copy in self.copies(group):
                copy.start()

    def ready(self, p):
        @pl.when(jnp.logical_and(p >= self.first, (p - self.first) % self.size == 0))
        def _():
            for copy in self.copies((p - self.first) // self.size):
                copy.wait()

    def wait(self):
        for group in range(self.sems.shape[1]):
            for copy in self.copies(group):
                copy.wait()


def faces_kernel(guess_hbm, faces_ref, sems):
    planes = guess_hbm.shape[1]
    tail = pltpu.make_async_copy(
        guess_hbm.at[:, planes - WIDTH : planes], faces_ref.at[0], sems.at[0]
    )
    head = pltpu.make_async_copy(guess_hbm.at[:, 0:WIDTH], faces_ref.at[1], sems.at[1])
    tail.start()
    head.start()
    tail.wait()
    head.wait()


def open_kernel(
    guess_hbm,
    right_hbm,
    dissipation_hbm,
    omega_hbm,
    step_hbm,
    diag_hbm,
    wide_ref,
    even_ref,
    odd_ref,
    axial_ref,
    right_ref,
    dissipation_ref,
    omega_ref,
    step_ref,
    diag_ref,
    sems,
):
    rows, wide, span, lanes = wide_ref.shape
    planes = wide - 2 * WIDTH
    pairs = (
        (guess_hbm, wide_ref.at[:, WIDTH : WIDTH + planes]),
        (dissipation_hbm, dissipation_ref),
        (omega_hbm, omega_ref),
        (step_hbm, step_ref),
        (right_hbm, right_ref),
        (diag_hbm, diag_ref),
    )
    copies = [pltpu.make_async_copy(*pair, sems.at[at]) for at, pair in enumerate(pairs)]
    for copy in copies:
        copy.start()
    for k in range(rows):
        for p in (0, 1, wide - 2, wide - 1):
            wide_ref[k, p] = jnp.zeros((span, lanes), jnp.float32)
    copies[0].wait()
    pack_faces(wide_ref, even_ref, odd_ref, axial_ref)
    for copy in copies[1:]:
        copy.wait()


def near_loading_kernel(
    wide_ref,
    neighbour_hbm,
    diag_ref,
    right_ref,
    dissipation_ref,
    omega_ref,
    error_ref,
    lower_ref,
    upper_ref,
    spaced_ref,
    neighbour_ref,
    axial_ref,
    near_sems,
    axial_sem,
):
    planes = error_ref.shape[1]
    groups = near_sems.shape[1]
    loads = Loads([(neighbour_hbm.at[0:2], neighbour_ref, 3)], near_sems, 0, planes // groups)
    later = pltpu.make_async_copy(neighbour_hbm.at[4:6], axial_ref, axial_sem)
    loads.start()
    later.start()
    shifts = (lower_ref, upper_ref)

    def own(p, carry):
        total = own_terms(wide_ref, right_ref, dissipation_ref, omega_ref, p)
        add_blocks(total, [(diag_ref, (), WIDTH)], wide_ref, p, shifts[:2], None)
        for k, value in enumerate(total):
            error_ref[k, p] = value
        return carry

    def pitch(p, carry):
        loads.ready(p)
        total = [error_ref[k, p] for k in range(error_ref.shape[0])]
        add_blocks(
            total,
            [(neighbour_ref, (0,), WIDTH - 1), (neighbour_ref, (1,), WIDTH + 1)],
            wide_ref,
            p,
            None,
            spaced_ref,
        )
        for k, value in enumerate(total):
            error_ref[k, p] = value
        return carry

    lax.fori_loop(0, planes, own, 0)
    lax.fori_loop(0, planes, pitch, 0)
    later.wait()


def near_kernel(
    wide_ref,
    neighbour_ref,
    diag_ref,
    right_ref,
    dissipation_ref,
    omega_ref,
    error_ref,
    lower_ref,
    upper_ref,
    spaced_ref,
):
    def plane(p, carry):
        total = own_terms(wide_ref, right_ref, dissipation_ref, omega_ref, p)
        add_blocks(
            total,
            [
                (diag_ref, (), WIDTH),
                (neighbour_ref, (0,), WIDTH - 1),
                (neighbour_ref, (1,), WIDTH + 1),
            ],
            wide_ref,
            p,
            (lower_ref, upper_ref),
            spaced_ref,
        )
        for k, value in enumerate(total):
            error_ref[k, p] = value
        return carry

    lax.fori_loop(0, error_ref.shape[1], plane, 0)


def own_terms(wide_ref, right_ref, dissipation_ref, omega_ref, p):
    rows = wide_ref.shape[0]
    nv = rows // 2
    omega = omega_ref[p]
    spread = dissipation_ref[0, p]
    total = []
    for k in range(rows):
        other = wide_ref[(k + nv) % rows, p + WIDTH]
        turned = -omega * other if k < nv else omega * other
        far = wide_ref[k, p] + wide_ref[k, p + 2 * WIDTH]
        total.append((turned - right_ref[k, p]) + spread * far)
    return total


def add_blocks(total, sources, wide_ref, p, near_refs, spaced_ref):
    _, _, span, lanes = wide_ref.shape
    nv = len(total) // 2
    lane = lax.broadcasted_iota(jnp.int32, (span, lanes), 1)
    for j in range(nv):
        for blocks_ref, lead, at in sources:
            real = wide_ref[j, p + at]
            imag = wide_ref[nv + j, p + at]
            for i in range(nv):
                block = blocks_ref[lead + (i, j, p)].astype(jnp.float32)
                total[i] = total[i] + block * real
                total[nv + i] = total[nv + i] + block * imag
        for k in (j, nv + j):
            cells = wide_ref[k, p + WIDTH]
            if near_refs is not None:
                near_refs[0][k, p] = pltpu.roll(cells, 1, axis=1)
                near_refs[1][k, p] = pltpu.roll(cells, lanes - 1, axis=1)
            if spaced_ref is not None:
                low = jnp.where(lane < WIDTH, 0.0, pltpu.roll(cells, 2, axis=1))
                high = pltpu.roll(cells, lanes - 2, axis=1)
                spaced_ref[k, p] = low + jnp.where(lane >= lanes - WIDTH, 0.0, high)


def first_axial_kernel(
    error_in_ref,
    even_ref,
    odd_ref,
    lower_ref,
    upper_ref,
    spaced_ref,
    neighbour_ref,
    dissipation_ref,
    phase_ref,
    neighbour_hbm,
    error_ref,
    span_ref,
    turn_ref,
    axial_buf,
    sem,
):
    later = pltpu.make_async_copy(neighbour_hbm.at[2:4], span_ref, sem)
    later.start()
    angle = jnp.full(turn_ref.shape[1:], phase_ref[0], jnp.float32)
    cosine = jnp.cos(angle)
    sine_part = jnp.sin(angle)
    pitch_at = lax.axis_index("pitch")
    first = pitch_at == 0
    last = pitch_at == lax.axis_size("pitch") - 1
    turn_ref[0] = jnp.where(first, cosine, 1.0)
    turn_ref[1] = jnp.where(first, -sine_part, 0.0)
    turn_ref[2] = jnp.where(last, cosine, 1.0)
    turn_ref[3] = jnp.where(last, sine_part, 0.0)
    axial_sweep(
        even_ref,
        odd_ref,
        lower_ref,
        upper_ref,
        spaced_ref,
        neighbour_ref,
        dissipation_ref,
        error_ref,
        axial_buf,
    )
    later.wait()


def axial_kernel(error_in_ref, *refs):
    axial_sweep(*refs)


def axial_sweep(
    even_ref,
    odd_ref,
    lower_ref,
    upper_ref,
    spaced_ref,
    neighbour_ref,
    dissipation_ref,
    error_ref,
    axial_buf,
):
    rows, planes, span, lanes = error_ref.shape
    nv = rows // 2
    axial_even = lax.axis_index("axial") % 2 == 0
    axial_alone = alone("axial")
    lane = lax.broadcasted_iota(jnp.int32, (span, lanes), 1)
    edge = jnp.logical_or(lane < WIDTH, lane >= lanes - WIDTH)
    from_below = lane % (2 * WIDTH) >= WIDTH
    for group in range(axial_buf.shape[0]):
        at_even = even_ref[group]
        at_odd = jnp.where(axial_alone, 0.0, odd_ref[group])
        below = pltpu.roll(jnp.where(axial_even, at_odd, at_even), WIDTH, axis=1)
        above = pltpu.roll(jnp.where(axial_even, at_even, at_odd), lanes - WIDTH, axis=1)
        axial_buf[group] = jnp.where(from_below, below, above)

    def plane(p, carry):
        total = [error_ref[k, p] for k in range(rows)]
        spread = dissipation_ref[2, p]
        for j in range(nv):
            lower = []
            upper = []
            for k in (j, nv + j):
                group, base = lane_place(k, planes, lanes)
                packed = axial_buf[group]
                shift = lanes - WIDTH - 2 * WIDTH * base - 2 * WIDTH * p
                below = pltpu.roll(packed, shift - 1, axis=1)
                above = pltpu.roll(packed, shift + 1, axis=1)
                beyond = pltpu.roll(packed, shift, axis=1)
                lower.append(jnp.where(lane < 1, below, lower_ref[k, p]))
                upper.append(jnp.where(lane >= lanes - 1, above, upper_ref[k, p]))
                far = spaced_ref[k, p] + jnp.where(edge, beyond, 0.0)
                total[k] = total[k] + spread * far
            for side, moved in enumerate((lower, upper)):
                for i in range(nv):
                    block = neighbour_ref[side, i, j, p].astype(jnp.float32)
                    total[i] = total[i] + block * moved[0]
                    total[nv + i] = total[nv + i] + block * moved[1]
        for k in range(rows):
            error_ref[k, p] = total[k]
        return carry

    lax.fori_loop(0, planes, plane, 0)


def span_sweep(
    odd_ref,
    even_ref,
    neighbour_ref,
    dissipation_ref,
    step_ref,
    wide_ref,
    error_ref,
    square_ref,
    span_buf,
    count,
    plane_of,
    after=None,
):
    rows, planes, span, _ = error_ref.shape
    nv = rows // 2
    span_even = lax.axis_index("span") % 2 == 0
    span_alone = alone("span")
    square_ref[...] = jnp.zeros_like(square_ref)

    def plane(at, carry):
        p = plane_of(at)
        for k in range(rows):
            at_even = even_ref[k, p]
            at_odd = jnp.where(span_alone, 0.0, odd_ref[k, p])
            span_buf[k, PAD - WIDTH : PAD] = jnp.where(span_even, at_odd, at_even)
            span_buf[k, PAD : PAD + span] = wide_ref[k, p + WIDTH]
            span_buf[k, PAD + span : PAD + span + WIDTH] = jnp.where(span_even, at_even, at_odd)

        def moved(k, by):
            return span_buf[k, PAD + by : PAD + by + span]

        spread = dissipation_ref[1, p]
        total = [
            error_ref[k, p] + spread * (moved(k, -WIDTH) + moved(k, WIDTH)) for k in range(rows)
        ]
        for j in range(nv):
            for side, by in enumerate((-1, 1)):
                real = moved(j, by)
                imag = moved(nv + j, by)
                for i in range(nv):
                    block = neighbour_ref[side, i, j, p].astype(jnp.float32)
                    total[i] = total[i] + block * real
                    total[nv + i] = total[nv + i] + block * imag
        step = step_ref[p]
        square = None
        for k in range(rows):
            error = total[k]
            error_ref[k, p] = error
            wide_ref[k, p + WIDTH] = wide_ref[k, p + WIDTH] - step * error
            square = error * error if square is None else square + error * error
        inner = jnp.logical_and(p >= WIDTH, p < planes - WIDTH)
        square_ref[...] += jnp.where(inner, square, 0.0)
        if after is not None:
            after(at)
        return carry

    lax.fori_loop(0, count, plane, 0)


def last_span_kernel(wide_in_ref, error_in_ref, *refs):
    planes = error_in_ref.shape[1]
    *args, wide_ref, error_ref, square_ref, out_ref, span_buf, sem = refs
    inner = planes - 2 * WIDTH
    copy = pltpu.make_async_copy(
        wide_ref.at[:, 2 * WIDTH : planes], out_ref.at[:, WIDTH : planes - WIDTH], sem
    )

    def plane_of(at):
        rim = at - inner
        return jnp.where(
            rim < 0, at + WIDTH, jnp.where(rim < WIDTH, rim, rim + planes - 2 * WIDTH)
        )

    def after(at):
        @pl.when(at == inner - 1)
        def _():
            copy.start()

    span_sweep(*args, wide_ref, error_ref, square_ref, span_buf, planes, plane_of, after)
    copy.wait()


def span_rim_kernel(wide_in_ref, error_in_ref, *refs):
    planes = error_in_ref.shape[1]
    span_sweep(
        *refs,
        2 * WIDTH,
        lambda at: jnp.where(at < WIDTH, at, at + planes - 2 * WIDTH),
    )


def span_core_kernel(
    wide_in_ref,
    error_in_ref,
    odd_ref,
    even_ref,
    neighbour_ref,
    dissipation_ref,
    step_ref,
    wide_ref,
    error_ref,
    square_ref,
    even_face_ref,
    odd_face_ref,
    axial_face_ref,
    span_buf,
):
    planes = error_ref.shape[1]
    span_sweep(
        odd_ref,
        even_ref,
        neighbour_ref,
        dissipation_ref,
        step_ref,
        wide_ref,
        error_ref,
        square_ref,
        span_buf,
        planes - 2 * WIDTH,
        lambda at: at + WIDTH,
    )
    pack_faces(wide_ref, even_face_ref, odd_face_ref, axial_face_ref)


def pitch_terms(halo_ref, turn_ref, neighbour_ref, dissipation_ref, error_ref, store):
    rows, planes, span, lanes = error_ref.shape
    nv = rows // 2
    for side in range(2):
        cosine = turn_ref[2 * side]
        sine_part = turn_ref[2 * side + 1]
        near_at, far_at = (1, 0) if side == 0 else (0, 1)
        edge, inside = (0, 1) if side == 0 else (planes - 1, planes - 2)

        def turned(j, at):
            real = halo_ref[side, j, at]
            imag = halo_ref[side, nv + j, at]
            return (cosine * real - sine_part * imag, sine_part * real + cosine * imag)

        total = [None] * rows

        def add(k, value):
            total[k] = value if total[k] is None else total[k] + value

        spread_edge = dissipation_ref[0, edge]
        spread_inside = dissipation_ref[0, inside]
        for j in range(nv):
            near = turned(j, near_at)
            far = turned(j, far_at)
            for c in range(2):
                k = c * nv + j
                add(k, spread_edge * far[c])
                store(k, inside, spread_inside * near[c])
            for i in range(nv):
                block = neighbour_ref[side, i, j, edge].astype(jnp.float32)
                for c in range(2):
                    add(c * nv + i, block * near[c])
        for k in range(rows):
            store(k, edge, total[k])


def rim_kernel(
    wide_in_ref,
    halo_ref,
    turn_ref,
    neighbour_ref,
    dissipation_ref,
    step_ref,
    error_ref,
    square_in_ref,
    wide_ref,
    faces_ref,
    square_ref,
):
    planes = error_ref.shape[1]
    square_ref[...] = square_in_ref[...]

    def store(k, p, change):
        value = wide_ref[k, p + WIDTH] - step_ref[p] * change
        wide_ref[k, p + WIDTH] = value
        if p < WIDTH:
            faces_ref[1, k, p] = value
        else:
            faces_ref[0, k, p - (planes - WIDTH)] = value
        error = error_ref[k, p] + change
        square_ref[...] += error * error

    pitch_terms(halo_ref, turn_ref, neighbour_ref, dissipation_ref, error_ref, store)


def last_kernel(
    wide_ref,
    halo_ref,
    turn_ref,
    neighbour_ref,
    dissipation_ref,
    step_ref,
    error_ref,
    square_in_ref,
    rim_square_ref,
    core_square_ref,
    rim_ref,
    share_ref,
    square_buf,
):
    planes = error_ref.shape[1]
    lanes = share_ref.shape[2]
    square_buf[...] = square_in_ref[...]

    def store(k, p, change):
        at = p if p < WIDTH else p - (planes - 2 * WIDTH)
        rim_ref[k, at] = wide_ref[k, p + WIDTH] - step_ref[p] * change
        error = error_ref[k, p] + change
        square_buf[...] += error * error

    pitch_terms(halo_ref, turn_ref, neighbour_ref, dissipation_ref, error_ref, store)
    lane = lax.broadcasted_iota(jnp.int32, (1, lanes), 1)
    first = jnp.sum(rim_square_ref[...] + core_square_ref[...], axis=0, keepdims=True)
    second = jnp.sum(square_buf[...], axis=0, keepdims=True)
    half = lanes // 2
    folded = jnp.where(
        lane < half,
        first + pltpu.roll(first, half, axis=1),
        second + pltpu.roll(second, half, axis=1),
    )
    share_ref[...] = jnp.broadcast_to(folded[None], share_ref.shape)


def close_kernel(cell_count, out_in_ref, rim_ref, share_ref, out_ref, norm_ref, norm_buf, sems):
    planes = out_ref.shape[1]
    lanes = share_ref.shape[2]
    copies = [
        pltpu.make_async_copy(rim_ref.at[:, 0:WIDTH], out_ref.at[:, 0:WIDTH], sems.at[0]),
        pltpu.make_async_copy(
            rim_ref.at[:, WIDTH : 2 * WIDTH], out_ref.at[:, planes - WIDTH : planes], sems.at[1]
        ),
    ]
    for copy in copies:
        copy.start()
    lane = lax.broadcasted_iota(jnp.int32, (1, lanes), 1)
    row = jnp.sum(share_ref[...], axis=0)
    first = jnp.sum(jnp.where(lane < lanes // 2, row, 0.0), axis=1, keepdims=True)
    second = jnp.sum(jnp.where(lane < lanes // 2, 0.0, row), axis=1, keepdims=True)
    norms = jnp.sqrt(jnp.where(lane == 0, first, second) / cell_count)
    for at in range(ITERS):
        norm_buf[at] = norms[0, at]
    copies.append(pltpu.make_async_copy(norm_buf, norm_ref, sems.at[2]))
    copies[2].start()
    for copy in copies:
        copy.wait()


def body(
    guess, right_side, diag_block, neighbour_blocks, dissipation, omega_volume, pseudo_step, phase
):
    parts, nv, planes, span, lanes = guess.shape
    rows = parts * nv
    pitch_count = lax.axis_size("pitch")
    devices = pitch_count * lax.axis_size("span") * lax.axis_size("axial")
    wide = (rows, planes + 2 * WIDTH, span, lanes)
    block = (rows, planes, span, lanes)
    tile = (span, lanes)
    face_shapes = (
        kept((2, rows, WIDTH, span, lanes)),
        kept((rows, planes, WIDTH, lanes)),
        kept((rows, planes, WIDTH, lanes)),
        kept((lane_groups(rows, planes, lanes), span, lanes)),
    )
    groups = GROUPS if planes % GROUPS == 0 else 1
    dma = pltpu.SemaphoreType.DMA

    def exchange_pitch(faces):
        up = [(i, (i + 1) % pitch_count) for i in range(pitch_count)]
        down = [(j, i) for i, j in up]
        if sorted(up) == sorted(down):
            return lax.ppermute(faces, "pitch", up)
        return jnp.stack(
            [lax.ppermute(faces[0], "pitch", up), lax.ppermute(faces[1], "pitch", down)]
        )

    span_count = lax.axis_size("span")
    axial_count = lax.axis_size("axial")

    def span_swap(values, start):
        partner = {}
        for i in range(start, span_count - 1, 2):
            partner.update({i: i + 1, i + 1: i})
        pairs = []
        for i in range(span_count):
            for j in range(axial_count):
                if i in partner:
                    pairs.append((i * axial_count + j, partner[i] * axial_count + j))
                elif axial_count % 2 == 0:
                    pairs.append((i * axial_count + j, i * axial_count + (j ^ 1)))
        return resident(lax.ppermute(values, ("span", "axial"), pairs))

    def axial_swap(values, start):
        pairs = [(i, i + 1) for i in range(start, axial_count - 1, 2)]
        if start == 1 and axial_count % 2 == 0:
            pairs.append((0, axial_count - 1))
        return resident(lax.ppermute(values, "axial", pairs + [(j, i) for i, j in pairs]))

    def exchange_rest(even, odd, axial):
        return (
            span_swap(even, 0),
            span_swap(odd, 1),
            axial_swap(axial, 0),
            axial_swap(axial, 1),
        )

    neighbour_blocks = outside(neighbour_blocks)
    sources = (right_side.reshape(block), dissipation, omega_volume, pseudo_step, diag_block)
    guess = outside(guess.reshape(block))
    (faces,) = call(faces_kernel, "pitch_faces", face_shapes[:1], [ANY], [dma((2,))])(guess)
    state, even, odd, axial, right, dissipation, omega, step, diag = call(
        open_kernel,
        "open",
        (kept(wide),)
        + face_shapes[1:]
        + tuple(kept(c.shape, c.dtype) for c in sources),
        [ANY] * 6,
        [dma((6,))],
    )(guess, *[outside(c) for c in sources])

    axial_buf = [pltpu.VMEM(face_shapes[3].shape, jnp.float32)]
    span_buf = [pltpu.VMEM((rows, span + 2 * PAD, lanes), jnp.float32)]
    pair = kept((2,) + neighbour_blocks.shape[1:], neighbour_blocks.dtype)
    sweep = (kept(wide), kept(block), kept(tile))
    for iteration in range(ITERS):
        halo = resident(exchange_pitch(faces))
        span_even, span_odd, axial_even, axial_odd = exchange_rest(even, odd, axial)
        if iteration == 0:
            error, *shifts, near_blocks, axial_blocks = call(
                near_loading_kernel,
                "first_near",
                (kept(block),) * 4 + (pair, pair),
                [VMEM, ANY] + [VMEM] * 4,
                [dma((1, groups)), dma],
            )(state, neighbour_blocks, diag, right, dissipation, omega)
            error, span_blocks, turn = call(
                first_axial_kernel,
                "first_axial",
                (kept(block), pair, kept((4,) + tile)),
                [VMEM] * 8 + [SMEM, ANY],
                axial_buf + [dma],
                {0: 0},
            )(
                error,
                axial_even,
                axial_odd,
                *shifts,
                axial_blocks,
                dissipation,
                phase,
                neighbour_blocks,
            )
        else:
            error, *shifts = call(near_kernel, "near", (kept(block),) * 4, [VMEM] * 6)(
                state, near_blocks, diag, right, dissipation, omega
            )
            (error,) = call(axial_kernel, "axial", (kept(block),), [VMEM] * 8, axial_buf, {0: 0})(
                error, axial_even, axial_odd, *shifts, axial_blocks, dissipation
            )
        rest = (span_odd, span_even, span_blocks, dissipation, step)
        terms = (halo, turn, near_blocks, dissipation, step)
        if iteration < ITERS - 1:
            state, error, square = call(
                span_rim_kernel, "span_rim", sweep, [VMEM] * 7, span_buf, {0: 0, 1: 1}
            )(state, error, *rest)
            state, faces, rim_square = call(
                rim_kernel,
                "pitch_terms",
                (kept(wide), face_shapes[0], kept(tile)),
                [VMEM] * 8,
                aliases={0: 0},
            )(state, *terms, error, square)
            state, _, core_square, even, odd, axial = call(
                span_core_kernel,
                "span_core",
                sweep + face_shapes[1:],
                [VMEM] * 7,
                span_buf,
                {0: 0, 1: 1},
            )(state, error, *rest)
        else:
            state, error, square, out = call(
                last_span_kernel,
                "span",
                sweep + (jax.ShapeDtypeStruct(block, jnp.float32),),
                [VMEM] * 7,
                span_buf + [dma],
                {0: 0, 1: 1},
                (VMEM,) * 3 + (ANY,),
            )(state, error, *rest)
            rim, share = call(
                last_kernel,
                "last_pitch_terms",
                (kept((rows, 2 * WIDTH, span, lanes)), kept((devices, 1, lanes))),
                [VMEM] * 10,
                [pltpu.VMEM(tile, jnp.float32)],
            )(state, *terms, error, square, rim_square, core_square)
    shares = lax.all_to_all(share, ("pitch", "span", "axial"), 0, 0, tiled=True)
    cell_count = float(rows * planes * span * lanes * devices)
    out, norms = call(
        functools.partial(close_kernel, cell_count),
        "close",
        (
            jax.ShapeDtypeStruct(block, jnp.float32),
            jax.ShapeDtypeStruct((ITERS,), jnp.float32),
        ),
        [ANY, VMEM, VMEM],
        [pltpu.SMEM((ITERS,), jnp.float32), dma((3,))],
        {0: 0},
        (ANY, ANY),
    )(out, rim, resident(shares))
    return (out.reshape(parts, nv, planes, span, lanes), norms)


def solution(mesh):
    placed = (
        P(None, None, "pitch", "span", "axial"),
        P(None, None, "pitch", "span", "axial"),
        P(None, None, "pitch", "span", "axial"),
        P(None, None, None, "pitch", "span", "axial"),
        P(None, "pitch", "span", "axial"),
        P("pitch", "span", "axial"),
        P("pitch", "span", "axial"),
        P(),
    )
    return jax.shard_map(
        body,
        mesh=mesh,
        in_specs=placed,
        out_specs=(P(None, None, "pitch", "span", "axial"), P()),
        check_vma=False,
    )
```

```python
import functools

import jax
import jax.numpy as jnp
from jax import lax
from jax.experimental import pallas as pl
from jax.experimental.pallas import tpu as pltpu
from jax.sharding import PartitionSpec as P

ITERS = 2
WIDTH = 2
PAD = 8
GROUPS = 4
VMEM = pl.BlockSpec(memory_space=pltpu.VMEM)
SMEM = pl.BlockSpec(memory_space=pltpu.SMEM)
ANY = pl.BlockSpec(memory_space=pl.ANY)
VMEM_LIMIT = 4 * 1024 * 1024


def resident(values):
    return pltpu.with_memory_space_constraint(values, pltpu.VMEM)


def outside(values):
    return pltpu.with_memory_space_constraint(values, pltpu.HBM)


def kept(shape, dtype=jnp.float32):
    return pltpu.VMEM(shape, dtype)


def call(kernel, name, out_shape, in_specs, scratch_shapes=(), aliases=None, out_specs=None):
    return pl.pallas_call(
        kernel,
        out_shape=out_shape,
        in_specs=in_specs,
        out_specs=out_specs or (VMEM,) * len(out_shape),
        scratch_shapes=scratch_shapes,
        input_output_aliases=aliases or {},
        compiler_params=pltpu.CompilerParams(vmem_limit_bytes=VMEM_LIMIT),
        name=name,
    )


def lane_place(k, planes, lanes):
    per_group = (lanes // (2 * WIDTH)) // planes
    return k // per_group, (k % per_group) * planes


def lane_groups(rows, planes, lanes):
    return lane_place(rows - 1, planes, lanes)[0] + 1


def pack_faces(wide_ref, even_ref, odd_ref, axial_ref):
    rows, wide, span, lanes = wide_ref.shape
    planes = wide - 2 * WIDTH
    span_even = lax.axis_index("span") % 2 == 0
    lane = lax.broadcasted_iota(jnp.int32, (span, lanes), 1)
    packed = None
    for k in range(rows):
        group, base = lane_place(k, planes, lanes)
        for p in range(planes):
            cells = wide_ref[k, p + WIDTH]
            low = cells[:WIDTH]
            high = cells[span - WIDTH :]
            even_ref[k, p] = jnp.where(span_even, high, low)
            odd_ref[k, p] = jnp.where(span_even, low, high)
            place = base + p
            moved = pltpu.roll(cells, (2 * WIDTH * place + WIDTH) % lanes, axis=1)
            if place == 0:
                packed = moved
            else:
                packed = jnp.where(lane >= 2 * WIDTH * place, moved, packed)
        if k == rows - 1 or lane_place(k + 1, planes, lanes)[0] != group:
            axial_ref[group] = packed


def alone(axis):
    at = lax.axis_index(axis)
    count = lax.axis_size(axis)
    return jnp.logical_or(at == 0, jnp.logical_and(at == count - 1, count % 2 == 0))


class Loads:
    def __init__(self, pairs, sems, first, size):
        self.pairs = pairs
        self.sems = sems
        self.first = first
        self.size = size

    def copies(self, group):
        planes = pl.ds(self.first + group * self.size, self.size)
        return [
            pltpu.make_async_copy(
                source.at[(slice(None),) * dim + (planes,)],
                target.at[(slice(None),) * dim + (planes,)],
                self.sems.at[at, group],
            )
            for at, (source, target, dim) in enumerate(self.pairs)
        ]

    def start(self):
        for group in range(self.sems.shape[1]):
            for copy in self.copies(group):
                copy.start()

    def ready(self, p):
        @pl.when(jnp.logical_and(p >= self.first, (p - self.first) % self.size == 0))
        def _():
            for copy in self.copies((p - self.first) // self.size):
                copy.wait()

    def wait(self):
        for group in range(self.sems.shape[1]):
            for copy in self.copies(group):
                copy.wait()


def faces_kernel(guess_hbm, after_ref, faces_ref, sems):
    planes = guess_hbm.shape[1]
    tail = pltpu.make_async_copy(
        guess_hbm.at[:, planes - WIDTH : planes], faces_ref.at[0], sems.at[0]
    )
    head = pltpu.make_async_copy(guess_hbm.at[:, 0:WIDTH], faces_ref.at[1], sems.at[1])
    tail.start()
    head.start()
    tail.wait()
    head.wait()


def staggered_open_kernel(turn, *refs):
    @pl.when(lax.axis_index("axial") % 2 == turn)
    def _():
        open_kernel(*refs[:6], *refs[-10:])


def open_kernel(
    guess_hbm,
    right_hbm,
    dissipation_hbm,
    omega_hbm,
    step_hbm,
    diag_hbm,
    wide_ref,
    even_ref,
    odd_ref,
    axial_ref,
    right_ref,
    dissipation_ref,
    omega_ref,
    step_ref,
    diag_ref,
    sems,
):
    rows, wide, span, lanes = wide_ref.shape
    planes = wide - 2 * WIDTH
    pairs = (
        (guess_hbm, wide_ref.at[:, WIDTH : WIDTH + planes]),
        (dissipation_hbm, dissipation_ref),
        (omega_hbm, omega_ref),
        (step_hbm, step_ref),
        (right_hbm, right_ref),
        (diag_hbm, diag_ref),
    )
    copies = [pltpu.make_async_copy(*pair, sems.at[at]) for at, pair in enumerate(pairs)]
    for copy in copies:
        copy.start()
    for k in range(rows):
        for p in (0, 1, wide - 2, wide - 1):
            wide_ref[k, p] = jnp.zeros((span, lanes), jnp.float32)
    copies[0].wait()
    pack_faces(wide_ref, even_ref, odd_ref, axial_ref)
    for copy in copies[1:]:
        copy.wait()


def near_loading_kernel(
    wide_ref,
    neighbour_hbm,
    diag_ref,
    right_ref,
    dissipation_ref,
    omega_ref,
    error_ref,
    lower_ref,
    upper_ref,
    spaced_ref,
    neighbour_ref,
    axial_ref,
    near_sems,
    axial_sem,
):
    planes = error_ref.shape[1]
    groups = near_sems.shape[1]
    loads = Loads([(neighbour_hbm.at[0:2], neighbour_ref, 3)], near_sems, 0, planes // groups)
    later = pltpu.make_async_copy(neighbour_hbm.at[4:6], axial_ref, axial_sem)
    loads.start()
    later.start()
    shifts = (lower_ref, upper_ref)

    def own(p, carry):
        total = own_terms(wide_ref, right_ref, dissipation_ref, omega_ref, p)
        add_blocks(total, [(diag_ref, (), WIDTH)], wide_ref, p, shifts[:2], None)
        for k, value in enumerate(total):
            error_ref[k, p] = value
        return carry

    def pitch(p, carry):
        loads.ready(p)
        total = [error_ref[k, p] for k in range(error_ref.shape[0])]
        add_blocks(
            total,
            [(neighbour_ref, (0,), WIDTH - 1), (neighbour_ref, (1,), WIDTH + 1)],
            wide_ref,
            p,
            None,
            spaced_ref,
        )
        for k, value in enumerate(total):
            error_ref[k, p] = value
        return carry

    lax.fori_loop(0, planes, own, 0)
    lax.fori_loop(0, planes, pitch, 0)
    later.wait()


def near_kernel(
    wide_ref,
    neighbour_ref,
    diag_ref,
    right_ref,
    dissipation_ref,
    omega_ref,
    error_ref,
    lower_ref,
    upper_ref,
    spaced_ref,
):
    def plane(p, carry):
        total = own_terms(wide_ref, right_ref, dissipation_ref, omega_ref, p)
        add_blocks(
            total,
            [
                (diag_ref, (), WIDTH),
                (neighbour_ref, (0,), WIDTH - 1),
                (neighbour_ref, (1,), WIDTH + 1),
            ],
            wide_ref,
            p,
            (lower_ref, upper_ref),
            spaced_ref,
        )
        for k, value in enumerate(total):
            error_ref[k, p] = value
        return carry

    lax.fori_loop(0, error_ref.shape[1], plane, 0)


def own_terms(wide_ref, right_ref, dissipation_ref, omega_ref, p):
    rows = wide_ref.shape[0]
    nv = rows // 2
    omega = omega_ref[p]
    spread = dissipation_ref[0, p]
    total = []
    for k in range(rows):
        other = wide_ref[(k + nv) % rows, p + WIDTH]
        turned = -omega * other if k < nv else omega * other
        far = wide_ref[k, p] + wide_ref[k, p + 2 * WIDTH]
        total.append((turned - right_ref[k, p]) + spread * far)
    return total


def add_blocks(total, sources, wide_ref, p, near_refs, spaced_ref):
    _, _, span, lanes = wide_ref.shape
    nv = len(total) // 2
    lane = lax.broadcasted_iota(jnp.int32, (span, lanes), 1)
    for j in range(nv):
        for blocks_ref, lead, at in sources:
            real = wide_ref[j, p + at]
            imag = wide_ref[nv + j, p + at]
            for i in range(nv):
                block = blocks_ref[lead + (i, j, p)].astype(jnp.float32)
                total[i] = total[i] + block * real
                total[nv + i] = total[nv + i] + block * imag
        for k in (j, nv + j):
            cells = wide_ref[k, p + WIDTH]
            if near_refs is not None:
                near_refs[0][k, p] = pltpu.roll(cells, 1, axis=1)
                near_refs[1][k, p] = pltpu.roll(cells, lanes - 1, axis=1)
            if spaced_ref is not None:
                low = jnp.where(lane < WIDTH, 0.0, pltpu.roll(cells, 2, axis=1))
                high = pltpu.roll(cells, lanes - 2, axis=1)
                spaced_ref[k, p] = low + jnp.where(lane >= lanes - WIDTH, 0.0, high)


def first_axial_kernel(
    error_in_ref,
    even_ref,
    odd_ref,
    lower_ref,
    upper_ref,
    spaced_ref,
    neighbour_ref,
    dissipation_ref,
    phase_ref,
    neighbour_hbm,
    error_ref,
    span_ref,
    turn_ref,
    axial_buf,
    sem,
):
    later = pltpu.make_async_copy(neighbour_hbm.at[2:4], span_ref, sem)
    later.start()
    angle = jnp.full(turn_ref.shape[1:], phase_ref[0], jnp.float32)
    cosine = jnp.cos(angle)
    sine_part = jnp.sin(angle)
    pitch_at = lax.axis_index("pitch")
    first = pitch_at == 0
    last = pitch_at == lax.axis_size("pitch") - 1
    turn_ref[0] = jnp.where(first, cosine, 1.0)
    turn_ref[1] = jnp.where(first, -sine_part, 0.0)
    turn_ref[2] = jnp.where(last, cosine, 1.0)
    turn_ref[3] = jnp.where(last, sine_part, 0.0)
    axial_sweep(
        even_ref,
        odd_ref,
        lower_ref,
        upper_ref,
        spaced_ref,
        neighbour_ref,
        dissipation_ref,
        error_ref,
        axial_buf,
    )
    later.wait()


def axial_kernel(error_in_ref, *refs):
    axial_sweep(*refs)


def axial_sweep(
    even_ref,
    odd_ref,
    lower_ref,
    upper_ref,
    spaced_ref,
    neighbour_ref,
    dissipation_ref,
    error_ref,
    axial_buf,
):
    rows, planes, span, lanes = error_ref.shape
    nv = rows // 2
    axial_even = lax.axis_index("axial") % 2 == 0
    axial_alone = alone("axial")
    lane = lax.broadcasted_iota(jnp.int32, (span, lanes), 1)
    edge = jnp.logical_or(lane < WIDTH, lane >= lanes - WIDTH)
    from_below = lane % (2 * WIDTH) >= WIDTH
    for group in range(axial_buf.shape[0]):
        at_even = even_ref[group]
        at_odd = jnp.where(axial_alone, 0.0, odd_ref[group])
        below = pltpu.roll(jnp.where(axial_even, at_odd, at_even), WIDTH, axis=1)
        above = pltpu.roll(jnp.where(axial_even, at_even, at_odd), lanes - WIDTH, axis=1)
        axial_buf[group] = jnp.where(from_below, below, above)

    def plane(p, carry):
        total = [error_ref[k, p] for k in range(rows)]
        spread = dissipation_ref[2, p]
        for j in range(nv):
            lower = []
            upper = []
            for k in (j, nv + j):
                group, base = lane_place(k, planes, lanes)
                packed = axial_buf[group]
                shift = lanes - WIDTH - 2 * WIDTH * base - 2 * WIDTH * p
                below = pltpu.roll(packed, shift - 1, axis=1)
                above = pltpu.roll(packed, shift + 1, axis=1)
                beyond = pltpu.roll(packed, shift, axis=1)
                lower.append(jnp.where(lane < 1, below, lower_ref[k, p]))
                upper.append(jnp.where(lane >= lanes - 1, above, upper_ref[k, p]))
                far = spaced_ref[k, p] + jnp.where(edge, beyond, 0.0)
                total[k] = total[k] + spread * far
            for side, moved in enumerate((lower, upper)):
                for i in range(nv):
                    block = neighbour_ref[side, i, j, p].astype(jnp.float32)
                    total[i] = total[i] + block * moved[0]
                    total[nv + i] = total[nv + i] + block * moved[1]
        for k in range(rows):
            error_ref[k, p] = total[k]
        return carry

    lax.fori_loop(0, planes, plane, 0)


def span_sweep(
    odd_ref,
    even_ref,
    neighbour_ref,
    dissipation_ref,
    step_ref,
    wide_ref,
    error_ref,
    square_ref,
    span_buf,
    count,
    plane_of,
    after=None,
):
    rows, planes, span, _ = error_ref.shape
    nv = rows // 2
    span_even = lax.axis_index("span") % 2 == 0
    span_alone = alone("span")
    square_ref[...] = jnp.zeros_like(square_ref)

    def plane(at, carry):
        p = plane_of(at)
        for k in range(rows):
            at_even = even_ref[k, p]
            at_odd = jnp.where(span_alone, 0.0, odd_ref[k, p])
            span_buf[k, PAD - WIDTH : PAD] = jnp.where(span_even, at_odd, at_even)
            span_buf[k, PAD : PAD + span] = wide_ref[k, p + WIDTH]
            span_buf[k, PAD + span : PAD + span + WIDTH] = jnp.where(span_even, at_even, at_odd)

        def moved(k, by):
            return span_buf[k, PAD + by : PAD + by + span]

        spread = dissipation_ref[1, p]
        total = [
            error_ref[k, p] + spread * (moved(k, -WIDTH) + moved(k, WIDTH)) for k in range(rows)
        ]
        for j in range(nv):
            for side, by in enumerate((-1, 1)):
                real = moved(j, by)
                imag = moved(nv + j, by)
                for i in range(nv):
                    block = neighbour_ref[side, i, j, p].astype(jnp.float32)
                    total[i] = total[i] + block * real
                    total[nv + i] = total[nv + i] + block * imag
        step = step_ref[p]
        square = None
        for k in range(rows):
            error = total[k]
            error_ref[k, p] = error
            wide_ref[k, p + WIDTH] = wide_ref[k, p + WIDTH] - step * error
            square = error * error if square is None else square + error * error
        inner = jnp.logical_and(p >= WIDTH, p < planes - WIDTH)
        square_ref[...] += jnp.where(inner, square, 0.0)
        if after is not None:
            after(at)
        return carry

    lax.fori_loop(0, count, plane, 0)


def last_span_kernel(wide_in_ref, error_in_ref, *refs):
    planes = error_in_ref.shape[1]
    *args, wide_ref, error_ref, square_ref, out_ref, span_buf, sem = refs
    inner = planes - 2 * WIDTH
    copy = pltpu.make_async_copy(
        wide_ref.at[:, 2 * WIDTH : planes], out_ref.at[:, WIDTH : planes - WIDTH], sem
    )

    def plane_of(at):
        rim = at - inner
        return jnp.where(
            rim < 0, at + WIDTH, jnp.where(rim < WIDTH, rim, rim + planes - 2 * WIDTH)
        )

    def after(at):
        @pl.when(at == inner - 1)
        def _():
            copy.start()

    span_sweep(*args, wide_ref, error_ref, square_ref, span_buf, planes, plane_of, after)
    copy.wait()


def span_rim_kernel(wide_in_ref, error_in_ref, *refs):
    planes = error_in_ref.shape[1]
    span_sweep(
        *refs,
        2 * WIDTH,
        lambda at: jnp.where(at < WIDTH, at, at + planes - 2 * WIDTH),
    )


def span_core_kernel(
    wide_in_ref,
    error_in_ref,
    odd_ref,
    even_ref,
    neighbour_ref,
    dissipation_ref,
    step_ref,
    wide_ref,
    error_ref,
    square_ref,
    even_face_ref,
    odd_face_ref,
    axial_face_ref,
    span_buf,
):
    planes = error_ref.shape[1]
    span_sweep(
        odd_ref,
        even_ref,
        neighbour_ref,
        dissipation_ref,
        step_ref,
        wide_ref,
        error_ref,
        square_ref,
        span_buf,
        planes - 2 * WIDTH,
        lambda at: at + WIDTH,
    )
    pack_faces(wide_ref, even_face_ref, odd_face_ref, axial_face_ref)


def pitch_terms(halo_ref, turn_ref, neighbour_ref, dissipation_ref, error_ref, store):
    rows, planes, span, lanes = error_ref.shape
    nv = rows // 2
    for side in range(2):
        cosine = turn_ref[2 * side]
        sine_part = turn_ref[2 * side + 1]
        near_at, far_at = (1, 0) if side == 0 else (0, 1)
        edge, inside = (0, 1) if side == 0 else (planes - 1, planes - 2)

        def turned(j, at):
            real = halo_ref[side, j, at]
            imag = halo_ref[side, nv + j, at]
            return (cosine * real - sine_part * imag, sine_part * real + cosine * imag)

        total = [None] * rows

        def add(k, value):
            total[k] = value if total[k] is None else total[k] + value

        spread_edge = dissipation_ref[0, edge]
        spread_inside = dissipation_ref[0, inside]
        for j in range(nv):
            near = turned(j, near_at)
            far = turned(j, far_at)
            for c in range(2):
                k = c * nv + j
                add(k, spread_edge * far[c])
                store(k, inside, spread_inside * near[c])
            for i in range(nv):
                block = neighbour_ref[side, i, j, edge].astype(jnp.float32)
                for c in range(2):
                    add(c * nv + i, block * near[c])
        for k in range(rows):
            store(k, edge, total[k])


def rim_kernel(
    wide_in_ref,
    halo_ref,
    turn_ref,
    neighbour_ref,
    dissipation_ref,
    step_ref,
    error_ref,
    square_in_ref,
    wide_ref,
    faces_ref,
    square_ref,
):
    planes = error_ref.shape[1]
    square_ref[...] = square_in_ref[...]

    def store(k, p, change):
        value = wide_ref[k, p + WIDTH] - step_ref[p] * change
        wide_ref[k, p + WIDTH] = value
        if p < WIDTH:
            faces_ref[1, k, p] = value
        else:
            faces_ref[0, k, p - (planes - WIDTH)] = value
        error = error_ref[k, p] + change
        square_ref[...] += error * error

    pitch_terms(halo_ref, turn_ref, neighbour_ref, dissipation_ref, error_ref, store)


def last_kernel(
    wide_ref,
    halo_ref,
    turn_ref,
    neighbour_ref,
    dissipation_ref,
    step_ref,
    error_ref,
    square_in_ref,
    rim_square_ref,
    core_square_ref,
    rim_ref,
    share_ref,
    square_buf,
):
    planes = error_ref.shape[1]
    lanes = share_ref.shape[2]
    square_buf[...] = square_in_ref[...]

    def store(k, p, change):
        at = p if p < WIDTH else p - (planes - 2 * WIDTH)
        rim_ref[k, at] = wide_ref[k, p + WIDTH] - step_ref[p] * change
        error = error_ref[k, p] + change
        square_buf[...] += error * error

    pitch_terms(halo_ref, turn_ref, neighbour_ref, dissipation_ref, error_ref, store)
    lane = lax.broadcasted_iota(jnp.int32, (1, lanes), 1)
    first = jnp.sum(rim_square_ref[...] + core_square_ref[...], axis=0, keepdims=True)
    second = jnp.sum(square_buf[...], axis=0, keepdims=True)
    half = lanes // 2
    folded = jnp.where(
        lane < half,
        first + pltpu.roll(first, half, axis=1),
        second + pltpu.roll(second, half, axis=1),
    )
    share_ref[...] = jnp.broadcast_to(folded[None], share_ref.shape)


def close_kernel(cell_count, out_in_ref, rim_ref, share_ref, out_ref, norm_ref, norm_buf, sems):
    planes = out_ref.shape[1]
    lanes = share_ref.shape[2]
    copies = [
        pltpu.make_async_copy(rim_ref.at[:, 0:WIDTH], out_ref.at[:, 0:WIDTH], sems.at[0]),
        pltpu.make_async_copy(
            rim_ref.at[:, WIDTH : 2 * WIDTH], out_ref.at[:, planes - WIDTH : planes], sems.at[1]
        ),
    ]
    for copy in copies:
        copy.start()
    lane = lax.broadcasted_iota(jnp.int32, (1, lanes), 1)
    row = jnp.sum(share_ref[...], axis=0)
    first = jnp.sum(jnp.where(lane < lanes // 2, row, 0.0), axis=1, keepdims=True)
    second = jnp.sum(jnp.where(lane < lanes // 2, 0.0, row), axis=1, keepdims=True)
    norms = jnp.sqrt(jnp.where(lane == 0, first, second) / cell_count)
    for at in range(ITERS):
        norm_buf[at] = norms[0, at]
    copies.append(pltpu.make_async_copy(norm_buf, norm_ref, sems.at[2]))
    copies[2].start()
    for copy in copies:
        copy.wait()


def body(
    guess, right_side, diag_block, neighbour_blocks, dissipation, omega_volume, pseudo_step, phase
):
    parts, nv, planes, span, lanes = guess.shape
    rows = parts * nv
    pitch_count = lax.axis_size("pitch")
    devices = pitch_count * lax.axis_size("span") * lax.axis_size("axial")
    wide = (rows, planes + 2 * WIDTH, span, lanes)
    block = (rows, planes, span, lanes)
    tile = (span, lanes)
    face_shapes = (
        kept((2, rows, WIDTH, span, lanes)),
        kept((rows, planes, WIDTH, lanes)),
        kept((rows, planes, WIDTH, lanes)),
        kept((lane_groups(rows, planes, lanes), span, lanes)),
    )
    groups = GROUPS if planes % GROUPS == 0 else 1
    dma = pltpu.SemaphoreType.DMA

    def exchange_pitch(faces):
        up = [(i, (i + 1) % pitch_count) for i in range(pitch_count)]
        down = [(j, i) for i, j in up]
        if sorted(up) == sorted(down):
            return lax.ppermute(faces, "pitch", up)
        return jnp.stack(
            [lax.ppermute(faces[0], "pitch", up), lax.ppermute(faces[1], "pitch", down)]
        )

    span_count = lax.axis_size("span")
    axial_count = lax.axis_size("axial")

    def span_swap(values, start):
        partner = {}
        for i in range(start, span_count - 1, 2):
            partner.update({i: i + 1, i + 1: i})
        pairs = []
        for i in range(span_count):
            for j in range(axial_count):
                if i in partner:
                    pairs.append((i * axial_count + j, partner[i] * axial_count + j))
                elif axial_count % 2 == 0:
                    pairs.append((i * axial_count + j, i * axial_count + (j ^ 1)))
        return resident(lax.ppermute(values, ("span", "axial"), pairs))

    def axial_swap(values, start):
        pairs = [(i, i + 1) for i in range(start, axial_count - 1, 2)]
        if start == 1 and axial_count % 2 == 0:
            pairs.append((0, axial_count - 1))
        return resident(lax.ppermute(values, "axial", pairs + [(j, i) for i, j in pairs]))

    def exchange_rest(even, odd, axial):
        return (
            span_swap(even, 0),
            span_swap(odd, 1),
            axial_swap(axial, 0),
            axial_swap(axial, 1),
        )

    neighbour_blocks = outside(neighbour_blocks)
    sources = (right_side.reshape(block), dissipation, omega_volume, pseudo_step, diag_block)
    guess = outside(guess.reshape(block))
    opening = (
        (kept(wide),) + face_shapes[1:] + tuple(kept(c.shape, c.dtype) for c in sources)
    )
    given = (guess, *[outside(c) for c in sources])
    opened = call(
        functools.partial(staggered_open_kernel, 0),
        "open_even",
        opening,
        [ANY] * 6,
        [dma((6,))],
    )(*given)
    (faces,) = call(faces_kernel, "pitch_faces", face_shapes[:1], [ANY, VMEM], [dma((2,))])(
        guess, opened[3]
    )
    state, even, odd, axial, right, dissipation, omega, step, diag = call(
        functools.partial(staggered_open_kernel, 1),
        "open_odd",
        opening,
        [ANY] * 6 + [VMEM] * 9,
        [dma((6,))],
        {6 + at: at for at in range(9)},
    )(*given, *opened)

    axial_buf = [pltpu.VMEM(face_shapes[3].shape, jnp.float32)]
    span_buf = [pltpu.VMEM((rows, span + 2 * PAD, lanes), jnp.float32)]
    pair = kept((2,) + neighbour_blocks.shape[1:], neighbour_blocks.dtype)
    sweep = (kept(wide), kept(block), kept(tile))
    for iteration in range(ITERS):
        halo = resident(exchange_pitch(faces))
        span_even, span_odd, axial_even, axial_odd = exchange_rest(even, odd, axial)
        if iteration == 0:
            error, *shifts, near_blocks, axial_blocks = call(
                near_loading_kernel,
                "first_near",
                (kept(block),) * 4 + (pair, pair),
                [VMEM, ANY] + [VMEM] * 4,
                [dma((1, groups)), dma],
            )(state, neighbour_blocks, diag, right, dissipation, omega)
            error, span_blocks, turn = call(
                first_axial_kernel,
                "first_axial",
                (kept(block), pair, kept((4,) + tile)),
                [VMEM] * 8 + [SMEM, ANY],
                axial_buf + [dma],
                {0: 0},
            )(
                error,
                axial_even,
                axial_odd,
                *shifts,
                axial_blocks,
                dissipation,
                phase,
                neighbour_blocks,
            )
        else:
            error, *shifts = call(near_kernel, "near", (kept(block),) * 4, [VMEM] * 6)(
                state, near_blocks, diag, right, dissipation, omega
            )
            (error,) = call(axial_kernel, "axial", (kept(block),), [VMEM] * 8, axial_buf, {0: 0})(
                error, axial_even, axial_odd, *shifts, axial_blocks, dissipation
            )
        rest = (span_odd, span_even, span_blocks, dissipation, step)
        terms = (halo, turn, near_blocks, dissipation, step)
        if iteration < ITERS - 1:
            state, error, square = call(
                span_rim_kernel, "span_rim", sweep, [VMEM] * 7, span_buf, {0: 0, 1: 1}
            )(state, error, *rest)
            state, faces, rim_square = call(
                rim_kernel,
                "pitch_terms",
                (kept(wide), face_shapes[0], kept(tile)),
                [VMEM] * 8,
                aliases={0: 0},
            )(state, *terms, error, square)
            state, _, core_square, even, odd, axial = call(
                span_core_kernel,
                "span_core",
                sweep + face_shapes[1:],
                [VMEM] * 7,
                span_buf,
                {0: 0, 1: 1},
            )(state, error, *rest)
        else:
            state, error, square, out = call(
                last_span_kernel,
                "span",
                sweep + (jax.ShapeDtypeStruct(block, jnp.float32),),
                [VMEM] * 7,
                span_buf + [dma],
                {0: 0, 1: 1},
                (VMEM,) * 3 + (ANY,),
            )(state, error, *rest)
            rim, share = call(
                last_kernel,
                "last_pitch_terms",
                (kept((rows, 2 * WIDTH, span, lanes)), kept((devices, 1, lanes))),
                [VMEM] * 10,
                [pltpu.VMEM(tile, jnp.float32)],
            )(state, *terms, error, square, rim_square, core_square)
    shares = lax.all_to_all(share, ("pitch", "span", "axial"), 0, 0, tiled=True)
    cell_count = float(rows * planes * span * lanes * devices)
    out, norms = call(
        functools.partial(close_kernel, cell_count),
        "close",
        (
            jax.ShapeDtypeStruct(block, jnp.float32),
            jax.ShapeDtypeStruct((ITERS,), jnp.float32),
        ),
        [ANY, VMEM, VMEM],
        [pltpu.SMEM((ITERS,), jnp.float32), dma((3,))],
        {0: 0},
        (ANY, ANY),
    )(out, rim, resident(shares))
    return (out.reshape(parts, nv, planes, span, lanes), norms)


def solution(mesh):
    placed = (
        P(None, None, "pitch", "span", "axial"),
        P(None, None, "pitch", "span", "axial"),
        P(None, None, "pitch", "span", "axial"),
        P(None, None, None, "pitch", "span", "axial"),
        P(None, "pitch", "span", "axial"),
        P("pitch", "span", "axial"),
        P("pitch", "span", "axial"),
        P(),
    )
    return jax.shard_map(
        body,
        mesh=mesh,
        in_specs=placed,
        out_specs=(P(None, None, "pitch", "span", "axial"), P()),
        check_vma=False,
    )
```

```python
import functools

import jax
import jax.numpy as jnp
from jax import lax
from jax.experimental import pallas as pl
from jax.experimental.pallas import tpu as pltpu
from jax.sharding import PartitionSpec as P

ITERS = 2
WIDTH = 2
PAD = 8
GROUPS = 2
VMEM = pl.BlockSpec(memory_space=pltpu.VMEM)
SMEM = pl.BlockSpec(memory_space=pltpu.SMEM)
ANY = pl.BlockSpec(memory_space=pl.ANY)
VMEM_LIMIT = 4 * 1024 * 1024


def resident(values):
    return pltpu.with_memory_space_constraint(values, pltpu.VMEM)


def outside(values):
    return pltpu.with_memory_space_constraint(values, pltpu.HBM)


def kept(shape, dtype=jnp.float32):
    return pltpu.VMEM(shape, dtype)


def call(kernel, name, out_shape, in_specs, scratch_shapes=(), aliases=None, out_specs=None):
    return pl.pallas_call(
        kernel,
        out_shape=out_shape,
        in_specs=in_specs,
        out_specs=out_specs or (VMEM,) * len(out_shape),
        scratch_shapes=scratch_shapes,
        input_output_aliases=aliases or {},
        compiler_params=pltpu.CompilerParams(vmem_limit_bytes=VMEM_LIMIT),
        name=name,
    )


def lane_place(k, planes, lanes):
    per_group = (lanes // (2 * WIDTH)) // planes
    return k // per_group, (k % per_group) * planes


def lane_groups(rows, planes, lanes):
    return lane_place(rows - 1, planes, lanes)[0] + 1


def pack_faces(wide_ref, even_ref, odd_ref, axial_ref):
    rows, wide, span, lanes = wide_ref.shape
    planes = wide - 2 * WIDTH
    span_even = lax.axis_index("span") % 2 == 0
    lane = lax.broadcasted_iota(jnp.int32, (span, lanes), 1)
    packed = None
    for k in range(rows):
        group, base = lane_place(k, planes, lanes)
        for p in range(planes):
            cells = wide_ref[k, p + WIDTH]
            low = cells[:WIDTH]
            high = cells[span - WIDTH :]
            even_ref[k, p] = jnp.where(span_even, high, low)
            odd_ref[k, p] = jnp.where(span_even, low, high)
            place = base + p
            moved = pltpu.roll(cells, (2 * WIDTH * place + WIDTH) % lanes, axis=1)
            if place == 0:
                packed = moved
            else:
                packed = jnp.where(lane >= 2 * WIDTH * place, moved, packed)
        if k == rows - 1 or lane_place(k + 1, planes, lanes)[0] != group:
            axial_ref[group] = packed


def alone(axis):
    at = lax.axis_index(axis)
    count = lax.axis_size(axis)
    return jnp.logical_or(at == 0, jnp.logical_and(at == count - 1, count % 2 == 0))


class Loads:
    def __init__(self, pairs, sems, first, size):
        self.pairs = pairs
        self.sems = sems
        self.first = first
        self.size = size

    def copies(self, group):
        planes = pl.ds(self.first + group * self.size, self.size)
        return [
            pltpu.make_async_copy(
                source.at[(slice(None),) * dim + (planes,)],
                target.at[(slice(None),) * dim + (planes,)],
                self.sems.at[at, group],
            )
            for at, (source, target, dim) in enumerate(self.pairs)
        ]

    def start(self):
        for group in range(self.sems.shape[1]):
            for copy in self.copies(group):
                copy.start()

    def ready(self, p):
        @pl.when(jnp.logical_and(p >= self.first, (p - self.first) % self.size == 0))
        def _():
            for copy in self.copies((p - self.first) // self.size):
                copy.wait()

    def wait(self):
        for group in range(self.sems.shape[1]):
            for copy in self.copies(group):
                copy.wait()


def faces_kernel(guess_hbm, after_ref, faces_ref, sems):
    planes = guess_hbm.shape[1]
    tail = pltpu.make_async_copy(
        guess_hbm.at[:, planes - WIDTH : planes], faces_ref.at[0], sems.at[0]
    )
    head = pltpu.make_async_copy(guess_hbm.at[:, 0:WIDTH], faces_ref.at[1], sems.at[1])
    tail.start()
    head.start()
    tail.wait()
    head.wait()


def staggered_open_kernel(turn, *refs):
    @pl.when(lax.axis_index("axial") % 2 == turn)
    def _():
        open_kernel(*refs[:7], *refs[-11:])


def open_kernel(
    guess_hbm,
    right_hbm,
    dissipation_hbm,
    omega_hbm,
    step_hbm,
    diag_hbm,
    neighbour_hbm,
    wide_ref,
    even_ref,
    odd_ref,
    axial_ref,
    right_ref,
    dissipation_ref,
    omega_ref,
    step_ref,
    diag_ref,
    neighbour_ref,
    sems,
):
    rows, wide, span, lanes = wide_ref.shape
    planes = wide - 2 * WIDTH
    half = planes // 2
    pairs = (
        (guess_hbm, wide_ref.at[:, WIDTH : WIDTH + planes]),
        (dissipation_hbm, dissipation_ref),
        (omega_hbm, omega_ref),
        (step_hbm, step_ref),
        (right_hbm, right_ref),
        (diag_hbm.at[:, :, 0:half], diag_ref.at[:, :, 0:half]),
        (neighbour_hbm.at[0:2, :, :, 0:half], neighbour_ref.at[:, :, :, 0:half]),
    )
    copies = [pltpu.make_async_copy(*pair, sems.at[at]) for at, pair in enumerate(pairs)]
    for copy in copies:
        copy.start()
    for k in range(rows):
        for p in (0, 1, wide - 2, wide - 1):
            wide_ref[k, p] = jnp.zeros((span, lanes), jnp.float32)
    copies[0].wait()
    pack_faces(wide_ref, even_ref, odd_ref, axial_ref)
    for copy in copies[1:]:
        copy.wait()


def near_loading_kernel(
    wide_ref,
    neighbour_in_ref,
    diag_in_ref,
    neighbour_hbm,
    diag_hbm,
    right_ref,
    dissipation_ref,
    omega_ref,
    neighbour_ref,
    diag_ref,
    error_ref,
    lower_ref,
    upper_ref,
    spaced_ref,
    axial_ref,
    near_sems,
    axial_sem,
):
    planes = error_ref.shape[1]
    half = planes // 2
    loads = Loads(
        [(diag_hbm, diag_ref, 2), (neighbour_hbm.at[0:2], neighbour_ref, 3)],
        near_sems,
        half,
        (planes - half) // near_sems.shape[1],
    )
    later = pltpu.make_async_copy(neighbour_hbm.at[4:6], axial_ref, axial_sem)
    loads.start()
    later.start()
    near_sweep(
        wide_ref,
        neighbour_ref,
        diag_ref,
        right_ref,
        dissipation_ref,
        omega_ref,
        error_ref,
        lower_ref,
        upper_ref,
        spaced_ref,
        loads,
    )
    later.wait()


def near_kernel(*refs):
    near_sweep(*refs, None)


def near_sweep(
    wide_ref,
    neighbour_ref,
    diag_ref,
    right_ref,
    dissipation_ref,
    omega_ref,
    error_ref,
    lower_ref,
    upper_ref,
    spaced_ref,
    loads,
):
    def plane(p, carry):
        if loads is not None:
            loads.ready(p)
        total = own_terms(wide_ref, right_ref, dissipation_ref, omega_ref, p)
        add_blocks(
            total,
            [
                (diag_ref, (), WIDTH),
                (neighbour_ref, (0,), WIDTH - 1),
                (neighbour_ref, (1,), WIDTH + 1),
            ],
            wide_ref,
            p,
            (lower_ref, upper_ref),
            spaced_ref,
        )
        for k, value in enumerate(total):
            error_ref[k, p] = value
        return carry

    lax.fori_loop(0, error_ref.shape[1], plane, 0)


def own_terms(wide_ref, right_ref, dissipation_ref, omega_ref, p):
    rows = wide_ref.shape[0]
    nv = rows // 2
    omega = omega_ref[p]
    spread = dissipation_ref[0, p]
    total = []
    for k in range(rows):
        other = wide_ref[(k + nv) % rows, p + WIDTH]
        turned = -omega * other if k < nv else omega * other
        far = wide_ref[k, p] + wide_ref[k, p + 2 * WIDTH]
        total.append((turned - right_ref[k, p]) + spread * far)
    return total


def add_blocks(total, sources, wide_ref, p, near_refs, spaced_ref):
    _, _, span, lanes = wide_ref.shape
    nv = len(total) // 2
    lane = lax.broadcasted_iota(jnp.int32, (span, lanes), 1)
    for j in range(nv):
        for blocks_ref, lead, at in sources:
            real = wide_ref[j, p + at]
            imag = wide_ref[nv + j, p + at]
            for i in range(nv):
                block = blocks_ref[lead + (i, j, p)].astype(jnp.float32)
                total[i] = total[i] + block * real
                total[nv + i] = total[nv + i] + block * imag
        for k in (j, nv + j):
            cells = wide_ref[k, p + WIDTH]
            if near_refs is not None:
                near_refs[0][k, p] = pltpu.roll(cells, 1, axis=1)
                near_refs[1][k, p] = pltpu.roll(cells, lanes - 1, axis=1)
            if spaced_ref is not None:
                low = jnp.where(lane < WIDTH, 0.0, pltpu.roll(cells, 2, axis=1))
                high = pltpu.roll(cells, lanes - 2, axis=1)
                spaced_ref[k, p] = low + jnp.where(lane >= lanes - WIDTH, 0.0, high)


def first_axial_kernel(
    error_in_ref,
    even_ref,
    odd_ref,
    lower_ref,
    upper_ref,
    spaced_ref,
    neighbour_ref,
    dissipation_ref,
    phase_ref,
    neighbour_hbm,
    error_ref,
    span_ref,
    turn_ref,
    axial_buf,
    sem,
):
    later = pltpu.make_async_copy(neighbour_hbm.at[2:4], span_ref, sem)
    later.start()
    angle = jnp.full(turn_ref.shape[1:], phase_ref[0], jnp.float32)
    cosine = jnp.cos(angle)
    sine_part = jnp.sin(angle)
    pitch_at = lax.axis_index("pitch")
    first = pitch_at == 0
    last = pitch_at == lax.axis_size("pitch") - 1
    turn_ref[0] = jnp.where(first, cosine, 1.0)
    turn_ref[1] = jnp.where(first, -sine_part, 0.0)
    turn_ref[2] = jnp.where(last, cosine, 1.0)
    turn_ref[3] = jnp.where(last, sine_part, 0.0)
    axial_sweep(
        even_ref,
        odd_ref,
        lower_ref,
        upper_ref,
        spaced_ref,
        neighbour_ref,
        dissipation_ref,
        error_ref,
        axial_buf,
    )
    later.wait()


def axial_kernel(error_in_ref, *refs):
    axial_sweep(*refs)


def axial_sweep(
    even_ref,
    odd_ref,
    lower_ref,
    upper_ref,
    spaced_ref,
    neighbour_ref,
    dissipation_ref,
    error_ref,
    axial_buf,
):
    rows, planes, span, lanes = error_ref.shape
    nv = rows // 2
    axial_even = lax.axis_index("axial") % 2 == 0
    axial_alone = alone("axial")
    lane = lax.broadcasted_iota(jnp.int32, (span, lanes), 1)
    edge = jnp.logical_or(lane < WIDTH, lane >= lanes - WIDTH)
    from_below = lane % (2 * WIDTH) >= WIDTH
    for group in range(axial_buf.shape[0]):
        at_even = even_ref[group]
        at_odd = jnp.where(axial_alone, 0.0, odd_ref[group])
        below = pltpu.roll(jnp.where(axial_even, at_odd, at_even), WIDTH, axis=1)
        above = pltpu.roll(jnp.where(axial_even, at_even, at_odd), lanes - WIDTH, axis=1)
        axial_buf[group] = jnp.where(from_below, below, above)

    def plane(p, carry):
        total = [error_ref[k, p] for k in range(rows)]
        spread = dissipation_ref[2, p]
        for j in range(nv):
            lower = []
            upper = []
            for k in (j, nv + j):
                group, base = lane_place(k, planes, lanes)
                packed = axial_buf[group]
                shift = lanes - WIDTH - 2 * WIDTH * base - 2 * WIDTH * p
                below = pltpu.roll(packed, shift - 1, axis=1)
                above = pltpu.roll(packed, shift + 1, axis=1)
                beyond = pltpu.roll(packed, shift, axis=1)
                lower.append(jnp.where(lane < 1, below, lower_ref[k, p]))
                upper.append(jnp.where(lane >= lanes - 1, above, upper_ref[k, p]))
                far = spaced_ref[k, p] + jnp.where(edge, beyond, 0.0)
                total[k] = total[k] + spread * far
            for side, moved in enumerate((lower, upper)):
                for i in range(nv):
                    block = neighbour_ref[side, i, j, p].astype(jnp.float32)
                    total[i] = total[i] + block * moved[0]
                    total[nv + i] = total[nv + i] + block * moved[1]
        for k in range(rows):
            error_ref[k, p] = total[k]
        return carry

    lax.fori_loop(0, planes, plane, 0)


def span_sweep(
    odd_ref,
    even_ref,
    neighbour_ref,
    dissipation_ref,
    step_ref,
    wide_ref,
    error_ref,
    square_ref,
    span_buf,
    count,
    plane_of,
    after=None,
):
    rows, planes, span, _ = error_ref.shape
    nv = rows // 2
    span_even = lax.axis_index("span") % 2 == 0
    span_alone = alone("span")
    square_ref[...] = jnp.zeros_like(square_ref)

    def plane(at, carry):
        p = plane_of(at)
        for k in range(rows):
            at_even = even_ref[k, p]
            at_odd = jnp.where(span_alone, 0.0, odd_ref[k, p])
            span_buf[k, PAD - WIDTH : PAD] = jnp.where(span_even, at_odd, at_even)
            span_buf[k, PAD : PAD + span] = wide_ref[k, p + WIDTH]
            span_buf[k, PAD + span : PAD + span + WIDTH] = jnp.where(span_even, at_even, at_odd)

        def moved(k, by):
            return span_buf[k, PAD + by : PAD + by + span]

        spread = dissipation_ref[1, p]
        total = [
            error_ref[k, p] + spread * (moved(k, -WIDTH) + moved(k, WIDTH)) for k in range(rows)
        ]
        for j in range(nv):
            for side, by in enumerate((-1, 1)):
                real = moved(j, by)
                imag = moved(nv + j, by)
                for i in range(nv):
                    block = neighbour_ref[side, i, j, p].astype(jnp.float32)
                    total[i] = total[i] + block * real
                    total[nv + i] = total[nv + i] + block * imag
        step = step_ref[p]
        square = None
        for k in range(rows):
            error = total[k]
            error_ref[k, p] = error
            wide_ref[k, p + WIDTH] = wide_ref[k, p + WIDTH] - step * error
            square = error * error if square is None else square + error * error
        inner = jnp.logical_and(p >= WIDTH, p < planes - WIDTH)
        square_ref[...] += jnp.where(inner, square, 0.0)
        if after is not None:
            after(at)
        return carry

    lax.fori_loop(0, count, plane, 0)


def last_span_kernel(wide_in_ref, error_in_ref, *refs):
    planes = error_in_ref.shape[1]
    *args, wide_ref, error_ref, square_ref, out_ref, span_buf, sem = refs
    inner = planes - 2 * WIDTH
    copy = pltpu.make_async_copy(
        wide_ref.at[:, 2 * WIDTH : planes], out_ref.at[:, WIDTH : planes - WIDTH], sem
    )

    def plane_of(at):
        rim = at - inner
        return jnp.where(
            rim < 0, at + WIDTH, jnp.where(rim < WIDTH, rim, rim + planes - 2 * WIDTH)
        )

    def after(at):
        @pl.when(at == inner - 1)
        def _():
            copy.start()

    span_sweep(*args, wide_ref, error_ref, square_ref, span_buf, planes, plane_of, after)
    copy.wait()


def span_rim_kernel(wide_in_ref, error_in_ref, *refs):
    planes = error_in_ref.shape[1]
    span_sweep(
        *refs,
        2 * WIDTH,
        lambda at: jnp.where(at < WIDTH, at, at + planes - 2 * WIDTH),
    )


def span_core_kernel(
    wide_in_ref,
    error_in_ref,
    odd_ref,
    even_ref,
    neighbour_ref,
    dissipation_ref,
    step_ref,
    wide_ref,
    error_ref,
    square_ref,
    even_face_ref,
    odd_face_ref,
    axial_face_ref,
    span_buf,
):
    planes = error_ref.shape[1]
    span_sweep(
        odd_ref,
        even_ref,
        neighbour_ref,
        dissipation_ref,
        step_ref,
        wide_ref,
        error_ref,
        square_ref,
        span_buf,
        planes - 2 * WIDTH,
        lambda at: at + WIDTH,
    )
    pack_faces(wide_ref, even_face_ref, odd_face_ref, axial_face_ref)


def pitch_terms(halo_ref, turn_ref, neighbour_ref, dissipation_ref, error_ref, store):
    rows, planes, span, lanes = error_ref.shape
    nv = rows // 2
    for side in range(2):
        cosine = turn_ref[2 * side]
        sine_part = turn_ref[2 * side + 1]
        near_at, far_at = (1, 0) if side == 0 else (0, 1)
        edge, inside = (0, 1) if side == 0 else (planes - 1, planes - 2)

        def turned(j, at):
            real = halo_ref[side, j, at]
            imag = halo_ref[side, nv + j, at]
            return (cosine * real - sine_part * imag, sine_part * real + cosine * imag)

        total = [None] * rows

        def add(k, value):
            total[k] = value if total[k] is None else total[k] + value

        spread_edge = dissipation_ref[0, edge]
        spread_inside = dissipation_ref[0, inside]
        for j in range(nv):
            near = turned(j, near_at)
            far = turned(j, far_at)
            for c in range(2):
                k = c * nv + j
                add(k, spread_edge * far[c])
                store(k, inside, spread_inside * near[c])
            for i in range(nv):
                block = neighbour_ref[side, i, j, edge].astype(jnp.float32)
                for c in range(2):
                    add(c * nv + i, block * near[c])
        for k in range(rows):
            store(k, edge, total[k])


def rim_kernel(
    wide_in_ref,
    halo_ref,
    turn_ref,
    neighbour_ref,
    dissipation_ref,
    step_ref,
    error_ref,
    square_in_ref,
    wide_ref,
    faces_ref,
    square_ref,
):
    planes = error_ref.shape[1]
    square_ref[...] = square_in_ref[...]

    def store(k, p, change):
        value = wide_ref[k, p + WIDTH] - step_ref[p] * change
        wide_ref[k, p + WIDTH] = value
        if p < WIDTH:
            faces_ref[1, k, p] = value
        else:
            faces_ref[0, k, p - (planes - WIDTH)] = value
        error = error_ref[k, p] + change
        square_ref[...] += error * error

    pitch_terms(halo_ref, turn_ref, neighbour_ref, dissipation_ref, error_ref, store)


def last_kernel(
    wide_ref,
    halo_ref,
    turn_ref,
    neighbour_ref,
    dissipation_ref,
    step_ref,
    error_ref,
    square_in_ref,
    rim_square_ref,
    core_square_ref,
    rim_ref,
    share_ref,
    square_buf,
):
    planes = error_ref.shape[1]
    lanes = share_ref.shape[2]
    square_buf[...] = square_in_ref[...]

    def store(k, p, change):
        at = p if p < WIDTH else p - (planes - 2 * WIDTH)
        rim_ref[k, at] = wide_ref[k, p + WIDTH] - step_ref[p] * change
        error = error_ref[k, p] + change
        square_buf[...] += error * error

    pitch_terms(halo_ref, turn_ref, neighbour_ref, dissipation_ref, error_ref, store)
    lane = lax.broadcasted_iota(jnp.int32, (1, lanes), 1)
    first = jnp.sum(rim_square_ref[...] + core_square_ref[...], axis=0, keepdims=True)
    second = jnp.sum(square_buf[...], axis=0, keepdims=True)
    half = lanes // 2
    folded = jnp.where(
        lane < half,
        first + pltpu.roll(first, half, axis=1),
        second + pltpu.roll(second, half, axis=1),
    )
    share_ref[...] = jnp.broadcast_to(folded[None], share_ref.shape)


def close_kernel(cell_count, out_in_ref, rim_ref, share_ref, out_ref, norm_ref, norm_buf, sems):
    planes = out_ref.shape[1]
    lanes = share_ref.shape[2]
    copies = [
        pltpu.make_async_copy(rim_ref.at[:, 0:WIDTH], out_ref.at[:, 0:WIDTH], sems.at[0]),
        pltpu.make_async_copy(
            rim_ref.at[:, WIDTH : 2 * WIDTH], out_ref.at[:, planes - WIDTH : planes], sems.at[1]
        ),
    ]
    for copy in copies:
        copy.start()
    lane = lax.broadcasted_iota(jnp.int32, (1, lanes), 1)
    row = jnp.sum(share_ref[...], axis=0)
    first = jnp.sum(jnp.where(lane < lanes // 2, row, 0.0), axis=1, keepdims=True)
    second = jnp.sum(jnp.where(lane < lanes // 2, 0.0, row), axis=1, keepdims=True)
    norms = jnp.sqrt(jnp.where(lane == 0, first, second) / cell_count)
    for at in range(ITERS):
        norm_buf[at] = norms[0, at]
    copies.append(pltpu.make_async_copy(norm_buf, norm_ref, sems.at[2]))
    copies[2].start()
    for copy in copies:
        copy.wait()


def body(
    guess, right_side, diag_block, neighbour_blocks, dissipation, omega_volume, pseudo_step, phase
):
    parts, nv, planes, span, lanes = guess.shape
    rows = parts * nv
    pitch_count = lax.axis_size("pitch")
    devices = pitch_count * lax.axis_size("span") * lax.axis_size("axial")
    wide = (rows, planes + 2 * WIDTH, span, lanes)
    block = (rows, planes, span, lanes)
    tile = (span, lanes)
    face_shapes = (
        kept((2, rows, WIDTH, span, lanes)),
        kept((rows, planes, WIDTH, lanes)),
        kept((rows, planes, WIDTH, lanes)),
        kept((lane_groups(rows, planes, lanes), span, lanes)),
    )
    groups = GROUPS if (planes - planes // 2) % GROUPS == 0 else 1
    dma = pltpu.SemaphoreType.DMA

    def exchange_pitch(faces):
        up = [(i, (i + 1) % pitch_count) for i in range(pitch_count)]
        down = [(j, i) for i, j in up]
        if sorted(up) == sorted(down):
            return lax.ppermute(faces, "pitch", up)
        return jnp.stack(
            [lax.ppermute(faces[0], "pitch", up), lax.ppermute(faces[1], "pitch", down)]
        )

    span_count = lax.axis_size("span")
    axial_count = lax.axis_size("axial")

    def span_swap(values, start):
        partner = {}
        for i in range(start, span_count - 1, 2):
            partner.update({i: i + 1, i + 1: i})
        pairs = []
        for i in range(span_count):
            for j in range(axial_count):
                if i in partner:
                    pairs.append((i * axial_count + j, partner[i] * axial_count + j))
                elif axial_count % 2 == 0:
                    pairs.append((i * axial_count + j, i * axial_count + (j ^ 1)))
        return resident(lax.ppermute(values, ("span", "axial"), pairs))

    def axial_swap(values, start):
        pairs = [(i, i + 1) for i in range(start, axial_count - 1, 2)]
        if start == 1 and axial_count % 2 == 0:
            pairs.append((0, axial_count - 1))
        return resident(lax.ppermute(values, "axial", pairs + [(j, i) for i, j in pairs]))

    def exchange_rest(even, odd, axial):
        return (
            span_swap(even, 0),
            span_swap(odd, 1),
            axial_swap(axial, 0),
            axial_swap(axial, 1),
        )

    neighbour_blocks = outside(neighbour_blocks)
    sources = (right_side.reshape(block), dissipation, omega_volume, pseudo_step, diag_block)
    guess = outside(guess.reshape(block))
    pair = kept((2,) + neighbour_blocks.shape[1:], neighbour_blocks.dtype)
    opening = (
        (kept(wide),)
        + face_shapes[1:]
        + tuple(kept(c.shape, c.dtype) for c in sources)
        + (pair,)
    )
    given = (guess, *[outside(c) for c in sources], neighbour_blocks)
    opened = call(
        functools.partial(staggered_open_kernel, 0),
        "open_even",
        opening,
        [ANY] * 7,
        [dma((7,))],
    )(*given)
    (faces,) = call(faces_kernel, "pitch_faces", face_shapes[:1], [ANY, VMEM], [dma((2,))])(
        guess, opened[3]
    )
    state, even, odd, axial, right, dissipation, omega, step, diag, near_blocks = call(
        functools.partial(staggered_open_kernel, 1),
        "open_odd",
        opening,
        [ANY] * 7 + [VMEM] * 10,
        [dma((7,))],
        {7 + at: at for at in range(10)},
    )(*given, *opened)

    axial_buf = [pltpu.VMEM(face_shapes[3].shape, jnp.float32)]
    span_buf = [pltpu.VMEM((rows, span + 2 * PAD, lanes), jnp.float32)]
    sweep = (kept(wide), kept(block), kept(tile))
    for iteration in range(ITERS):
        halo = resident(exchange_pitch(faces))
        span_even, span_odd, axial_even, axial_odd = exchange_rest(even, odd, axial)
        if iteration == 0:
            near_blocks, diag, error, *shifts, axial_blocks = call(
                near_loading_kernel,
                "first_near",
                (pair, kept(diag.shape, diag.dtype)) + (kept(block),) * 4 + (pair,),
                [VMEM] * 3 + [ANY] * 2 + [VMEM] * 3,
                [dma((2, groups)), dma],
                {1: 0, 2: 1},
            )(
                state,
                near_blocks,
                diag,
                neighbour_blocks,
                outside(diag_block),
                right,
                dissipation,
                omega,
            )
            error, span_blocks, turn = call(
                first_axial_kernel,
                "first_axial",
                (kept(block), pair, kept((4,) + tile)),
                [VMEM] * 8 + [SMEM, ANY],
                axial_buf + [dma],
                {0: 0},
            )(
                error,
                axial_even,
                axial_odd,
                *shifts,
                axial_blocks,
                dissipation,
                phase,
                neighbour_blocks,
            )
        else:
            error, *shifts = call(near_kernel, "near", (kept(block),) * 4, [VMEM] * 6)(
                state, near_blocks, diag, right, dissipation, omega
            )
            (error,) = call(axial_kernel, "axial", (kept(block),), [VMEM] * 8, axial_buf, {0: 0})(
                error, axial_even, axial_odd, *shifts, axial_blocks, dissipation
            )
        rest = (span_odd, span_even, span_blocks, dissipation, step)
        terms = (halo, turn, near_blocks, dissipation, step)
        if iteration < ITERS - 1:
            state, error, square = call(
                span_rim_kernel, "span_rim", sweep, [VMEM] * 7, span_buf, {0: 0, 1: 1}
            )(state, error, *rest)
            state, faces, rim_square = call(
                rim_kernel,
                "pitch_terms",
                (kept(wide), face_shapes[0], kept(tile)),
                [VMEM] * 8,
                aliases={0: 0},
            )(state, *terms, error, square)
            state, _, core_square, even, odd, axial = call(
                span_core_kernel,
                "span_core",
                sweep + face_shapes[1:],
                [VMEM] * 7,
                span_buf,
                {0: 0, 1: 1},
            )(state, error, *rest)
        else:
            state, error, square, out = call(
                last_span_kernel,
                "span",
                sweep + (jax.ShapeDtypeStruct(block, jnp.float32),),
                [VMEM] * 7,
                span_buf + [dma],
                {0: 0, 1: 1},
                (VMEM,) * 3 + (ANY,),
            )(state, error, *rest)
            rim, share = call(
                last_kernel,
                "last_pitch_terms",
                (kept((rows, 2 * WIDTH, span, lanes)), kept((devices, 1, lanes))),
                [VMEM] * 10,
                [pltpu.VMEM(tile, jnp.float32)],
            )(state, *terms, error, square, rim_square, core_square)
    shares = lax.all_to_all(share, ("pitch", "span", "axial"), 0, 0, tiled=True)
    cell_count = float(rows * planes * span * lanes * devices)
    out, norms = call(
        functools.partial(close_kernel, cell_count),
        "close",
        (
            jax.ShapeDtypeStruct(block, jnp.float32),
            jax.ShapeDtypeStruct((ITERS,), jnp.float32),
        ),
        [ANY, VMEM, VMEM],
        [pltpu.SMEM((ITERS,), jnp.float32), dma((3,))],
        {0: 0},
        (ANY, ANY),
    )(out, rim, resident(shares))
    return (out.reshape(parts, nv, planes, span, lanes), norms)


def solution(mesh):
    placed = (
        P(None, None, "pitch", "span", "axial"),
        P(None, None, "pitch", "span", "axial"),
        P(None, None, "pitch", "span", "axial"),
        P(None, None, None, "pitch", "span", "axial"),
        P(None, "pitch", "span", "axial"),
        P("pitch", "span", "axial"),
        P("pitch", "span", "axial"),
        P(),
    )
    return jax.shard_map(
        body,
        mesh=mesh,
        in_specs=placed,
        out_specs=(P(None, None, "pitch", "span", "axial"), P()),
        check_vma=False,
    )
```
